32 devices in a mesh: slab: 2 (over y), dom: 4 (over z), band: 2 (over x), sub: 2 (over core).
Axes of the slice: x: 2, y: 2, z: 4, core: 2. Of those that a mesh axis runs over, the one named last changes fastest.
Arguments:
- panel: float32 [256, 12, 32, 128], P(('slab', 'band', 'sub'), 'dom'), parts along dimension 0, may hold values from -6 to 6
- potential: float32 [24, 32, 128], P(('slab', 'dom')), parts along dimension 0, may hold values from 0 to 1
- point_offsets: int32 [384, 3, 128], P(('slab', 'dom')), parts along dimension 0, may hold values from -1 to 12287, as said below
- point_coefs: float32 [384, 3, 8, 128], P(('slab', 'dom')), parts along dimension 0, may hold values from -0.2 to 0.2
- correlation: float32 [384, 8, 8], P(('slab', 'dom')), parts along dimension 0, may hold values from -6 to 6
Outputs:
- filtered: float32 [256, 12, 32, 128], P(('slab', 'band', 'sub'), 'dom'), parts along dimension 0
- gram: float32 [256, 128], P(('slab', 'band', 'sub')), parts along dimension 0
The draws below stay inside these ranges and needn't reach their ends.
There are 2 independent parts, one for each index of `slab`. The reference program is written for one: setup_inputs(seed, part) draws one part's arguments, and reference() takes and returns one part's arrays. A program takes and returns all parts, laid end to end along the dimension named above; each array names one. Nothing has to cross between parts.
Inputs may be any that keep to these rules, and one draw needn't show every extreme that they name: `point_offsets`: entry [h * 48 + j, r, k] is the k-th point, as a flat index within grid block h, of the projector of atom j of home block (h + r - 1) mod 4; -1 marks a padded entry, and the live entries of one atom in one block come first.
All inputs are finite; a program needn't handle non-finite values.
Results may differ from the reference program's by a relative error of at most 0.0003.
Values sent between devices are 32-bit elements; how exact they have to be, the bound alone decides.
No kernel may reach another device: no remote copies, remote signals or barrier semaphores. Data moves between devices by JAX's collectives and lax.ppermute only.
A program may use at most 64 MiB of HBM per device.

```python
import math
import jax
import jax.numpy as jnp
from jax import lax

ORBS = 128
PROJ = 8
DEGREE = 12
SPREAD = 128
CX = 3
NY = 32
NZ = 128
ATOM_DEV = 48
NX = 12
ATOMS = 192
N_DOM = 4


def draw_point_offsets(key, part):
    key = jax.random.fold_in(key, 11)
    key_points, key_own, key_side = jax.random.split(key, 3)
    block_points = CX * NY * NZ
    raw_points = jax.random.randint(key_points, (ATOMS, 3, SPREAD), 0, block_points)
    own_count = jax.random.randint(key_own, (ATOMS, 1, 1), SPREAD // 2, SPREAD + 1)
    side_count = jax.random.randint(key_side, (ATOMS, 2, 1), 0, SPREAD // 2 + 1)
    counts = jnp.concatenate([side_count[:, :1], own_count, side_count[:, 1:]], axis=1)
    position = jnp.arange(SPREAD, dtype=jnp.int32)[None, None, :]
    offsets = jnp.where(position < counts, raw_points, -1)
    offsets = offsets.at[::ATOM_DEV, 1, 0].set(block_points - 1)
    return offsets.astype(jnp.int32)


def shard_levels(stream_key, dims, pieces, low, largest):
    factor_of = 1.0
    for axis_at, parts in pieces:
        draws = jax.random.uniform(jax.random.fold_in(jax.random.fold_in(stream_key, 6), axis_at), (parts,), jnp.float32, low / len(pieces), largest / len(pieces))
        factor_of = factor_of * jnp.repeat(jnp.exp(draws), dims[axis_at] // parts).reshape((-1,) + (1,) * (len(dims) - 1 - axis_at))
    return factor_of


def centred(rng, shape, deviation, most, cuts=(), kind=jnp.bfloat16):
    result = jax.random.normal(rng, shape, jnp.float32) * deviation
    if len(cuts) > 0:
        result = shard_levels(rng, shape, cuts, -0.22, 0.18) * result
    return jnp.clip(result, min=-most, max=most).astype(kind)


def setup_inputs(seed: int = 0, part: int = 0) -> dict:
    splits = jax.random.split(jax.random.key(seed), 6)
    own_keys = jax.random.split(jax.random.fold_in(splits[5], part), 6)
    panel = centred(own_keys[0], (ORBS, NX, NY, NZ), 1.0, 6.0, ((0, 4), (1, 4)), jnp.float32)
    potential = jnp.clip(1.0 * jax.random.uniform(own_keys[1], (NX, NY, NZ), jnp.float32) ** shard_levels(own_keys[1], (NX, NY, NZ), ((0, 4),), -0.2, 0.2), 0.0, 1.0)
    point_offsets = draw_point_offsets(jax.random.fold_in(jax.random.fold_in(splits[5], part), 71), part)
    point_coefs = centred(own_keys[3], (ATOMS, 3, PROJ, SPREAD), 0.03, 0.2, ((0, 4),), jnp.float32)
    correlation = centred(own_keys[4], (ATOMS, PROJ, PROJ), 1.0, 6.0, ((0, 4),), jnp.float32)
    return {"panel": panel, "potential": potential, "point_offsets": point_offsets, "point_coefs": point_coefs, "correlation": correlation}


center_level = 3.6
half_width = 3.4

def operator(extended, local_potential):
    centre_part = extended[:, 1:-1]
    along_x = extended[:, 2:] + extended[:, :-2]
    along_y = jnp.roll(centre_part, 1, axis=2) + jnp.roll(centre_part, -1, axis=2)
    zero_plane = jnp.zeros_like(centre_part[..., :1])
    along_z = jnp.concatenate([centre_part[..., 1:], zero_plane], axis=3) + jnp.concatenate([zero_plane, centre_part[..., :-1]], axis=3)
    hamiltonian = (local_potential + 3.0) * centre_part - 0.5 * (along_x + along_y + along_z)
    return (hamiltonian - center_level * centre_part) / half_width

def wrapped(field, local_potential):
    extended = jnp.concatenate([field[:, -1:], field, field[:, :1]], axis=1)
    return operator(extended, local_potential)

def reference(panel, potential, point_offsets, point_coefs, correlation):
    before = panel
    current = wrapped(panel, potential)
    for step_index in range(DEGREE - 1):
        before, current = (current, 2.0 * wrapped(current, potential) - before)
    block_points = CX * NY * NZ
    grid_rows = current.reshape(ORBS, N_DOM, block_points)
    offsets = point_offsets.reshape(N_DOM, ATOM_DEV, 3, SPREAD)
    coefs = point_coefs.reshape(N_DOM, ATOM_DEV, 3, PROJ, SPREAD)

    def per_block(block):
        values = lax.dynamic_index_in_dim(grid_rows, block, 1, keepdims=False)
        block_offsets = lax.dynamic_index_in_dim(offsets, block, 0, keepdims=False)
        block_coefs = lax.dynamic_index_in_dim(coefs, block, 0, keepdims=False)
        live_mask = block_offsets >= 0
        safe_offsets = jnp.maximum(block_offsets, 0)
        picked = jnp.where(live_mask[None], values[:, safe_offsets], 0.0)
        return jnp.einsum('oark,arpk->roap', picked, block_coefs, precision=lax.Precision.HIGHEST)
    partial_value = lax.map(per_block, jnp.arange(N_DOM, dtype=jnp.int32))
    own_part = partial_value[:, 1]
    from_right = jnp.roll(partial_value[:, 0], -1, axis=0)
    from_left = jnp.roll(partial_value[:, 2], 1, axis=0)
    projections = own_part + from_right + from_left
    correlations = correlation.reshape(N_DOM, ATOM_DEV, PROJ, PROJ)
    weighted = jnp.einsum('dapq,doaq->doap', correlations, projections, precision=lax.Precision.HIGHEST)
    inv_points = 1.0 / (NX * NY * NZ)
    atom_scale = 1.0 / math.sqrt(ATOMS)
    flat_panel = current.reshape(ORBS, -1)
    grid_part = jnp.einsum('or,pr->op', flat_panel, flat_panel * inv_points, precision=lax.Precision.HIGHEST)
    atom_part = jnp.einsum('doap,dqap->oq', projections, weighted * atom_scale, precision=lax.Precision.HIGHEST)
    return (current, grid_part + atom_part)
```

```python
import functools
import math

import jax
import jax.numpy as jnp
from jax import lax
from jax.experimental import pallas as pl
from jax.experimental.pallas import tpu as pltpu
from jax.sharding import PartitionSpec as P

DEGREE = 12

CENTER_LEVEL = 3.6
HALF_WIDTH = 3.4
SHIFT = 3.0

MAX_CHUNKS = 2
MIB = 1024 * 1024

VMEM = pl.BlockSpec(memory_space=pltpu.VMEM)
SMEM = pl.BlockSpec(memory_space=pltpu.SMEM)
NT = (((1,), (1,)), ((), ()))
TN = (((0,), (0,)), ((), ()))


def params(mib):
    return pltpu.CompilerParams(vmem_limit_bytes=mib * MIB)


def split_bf16(x):
    high = x.astype(jnp.bfloat16)
    return high, (x - high.astype(jnp.float32)).astype(jnp.bfloat16)


def swap_over(x, axes, size, by):
    return lax.ppermute(x, axes, [(i, i ^ by) for i in range(size)])


def filter_kernel(n_dom, me_ref, *refs):
    potentials = refs[:n_dom]
    ins = refs[n_dom : 2 * n_dom]
    outs = refs[2 * n_dom : 3 * n_dom]
    even, odd, diagonal = refs[3 * n_dom :]
    me = me_ref[0]
    planes = ins[0].shape[1]
    total = n_dom * planes
    step_scale = 1.0 / HALF_WIDTH
    for m in range(n_dom):
        first = (me ^ m) * planes
        for i in range(planes):
            even[first + i] = ins[m][:, i]
            diagonal[first + i] = (potentials[m][i] + (SHIFT - CENTER_LEVEL)) * (2.0 * step_scale)
    rows, lanes = even.shape[2], even.shape[3]
    lane = lax.broadcasted_iota(jnp.int32, (1, rows, lanes), 2)
    scale_low = jnp.where(lane == 0, 0.0, step_scale)
    scale_high = jnp.where(lane == lanes - 1, 0.0, step_scale)

    def twice_operator(source, x):
        below = jnp.where(x == 0, total - 1, x - 1)
        above = jnp.where(x == total - 1, 0, x + 1)
        centre = source[x]
        near = source[below] + source[above]
        near += pltpu.roll(centre, 1, 1) + pltpu.roll(centre, rows - 1, 1)
        result = diagonal[x][None] * centre - step_scale * near
        result -= scale_low * pltpu.roll(centre, 1, 2)
        return result - scale_high * pltpu.roll(centre, lanes - 1, 2)

    def first_plane(x, _):
        odd[x] = 0.5 * twice_operator(even, x)
        return 0

    def next_plane(source, target, x, _):
        target[x] = twice_operator(source, x) - target[x]
        return 0

    onto_even = functools.partial(next_plane, odd, even)
    onto_odd = functools.partial(next_plane, even, odd)
    lax.fori_loop(0, total, first_plane, 0)
    lax.fori_loop(0, total, onto_even, 0)

    def two_steps(_, carry):
        lax.fori_loop(0, total, onto_odd, 0)
        lax.fori_loop(0, total, onto_even, 0)
        return carry

    lax.fori_loop(0, DEGREE // 2 - 1, two_steps, 0)
    for m in range(n_dom):
        first = (me ^ m) * planes
        for i in range(planes):
            outs[m][:, i] = even[first + i]


def filter_orbitals(me, potentials, blocks):
    n_dom = len(blocks)
    orbitals, planes, rows, lanes = blocks[0].shape
    field = pltpu.VMEM((n_dom * planes, orbitals, rows, lanes), jnp.float32)
    cells = n_dom * blocks[0].size
    return pl.pallas_call(
        functools.partial(filter_kernel, n_dom),
        out_shape=[jax.ShapeDtypeStruct(blocks[0].shape, jnp.float32)] * n_dom,
        in_specs=[SMEM] + [VMEM] * (2 * n_dom),
        out_specs=[VMEM] * n_dom,
        scratch_shapes=[field, field, pltpu.VMEM((n_dom * planes, rows, lanes), jnp.float32)],
        compiler_params=params(16),
        cost_estimate=pl.CostEstimate(
            flops=12 * DEGREE * cells, bytes_accessed=8 * cells, transcendentals=0
        ),
        name="chebyshev",
    )(me, *potentials, *blocks)


def assemble_kernel(me_ref, *refs):
    *pieces, out = refs
    per = pieces[0].shape[0]
    for m, piece in enumerate(pieces):
        out[pl.ds((me_ref[0] ^ m) * per, per)] = piece[...]


def assemble(me, pieces):
    per = pieces[0].shape[0]
    return pl.pallas_call(
        assemble_kernel,
        out_shape=jax.ShapeDtypeStruct((per * len(pieces),) + pieces[0].shape[1:], jnp.float32),
        in_specs=[SMEM] + [VMEM] * len(pieces),
        out_specs=VMEM,
        compiler_params=params(8),
        name="assemble",
    )(me, *pieces)


def regroup_kernel(cells, group_ref, *refs):
    *pieces, high_out, low_out = refs
    orbitals = pieces[0].shape[0] // cells
    pairs = cells // 2

    for j, piece in enumerate(pieces):
        target = group_ref[0] ^ j

        def one_row(row, _, piece=piece, target=target):
            for half in range(2):
                picked = piece[pl.ds(row + half * pairs, orbitals, stride=cells), :]
                high, low = split_bf16(picked)
                lanes = picked.shape[1]
                high_out[target, row, :, half * lanes : (half + 1) * lanes] = high
                low_out[target, row, :, half * lanes : (half + 1) * lanes] = low
            return 0

        lax.fori_loop(0, pairs, one_row, 0, unroll=4)


def regroup(group, pieces):
    orbitals = pieces[0].shape[0]
    lanes = pieces[0].shape[3]
    cells = pieces[0].size // (orbitals * lanes)
    shape = jax.ShapeDtypeStruct((len(pieces), cells // 2, orbitals, 2 * lanes), jnp.bfloat16)
    return pl.pallas_call(
        functools.partial(regroup_kernel, cells),
        out_shape=[shape, shape],
        in_specs=[SMEM] + [VMEM] * len(pieces),
        out_specs=[VMEM, VMEM],
        compiler_params=params(16),
        name="regroup",
    )(group, *[piece.reshape(orbitals * cells, lanes) for piece in pieces])


def projector_kernel(groups, group_ref, offsets_ref, coefs_ref, high_out, low_out):
    pairs = high_out.shape[0]
    per_group = offsets_ref.shape[0] // groups
    channels, spread = coefs_ref.shape[2], coefs_ref.shape[3]
    step = pl.program_id(0)
    shell = step // (per_group // 2)
    first_atom = group_ref[0] * per_group + 2 * (step % (per_group // 2))
    lanes = high_out.shape[2] // 2
    row_index = lax.broadcasted_iota(jnp.int32, (2 * pairs, channels, spread), 0)
    lane_index = lax.broadcasted_iota(jnp.int32, (lanes, spread), 0)
    dense = []
    for i in range(2):
        offsets = offsets_ref[first_atom + i, pl.ds(shell, 1), :]
        coefs = coefs_ref[first_atom + i, shell]
        at_row = row_index == (offsets // lanes)[None]
        at_row &= (offsets >= 0)[None]
        high, low = split_bf16(coefs)
        left = [
            jnp.where(at_row, part.astype(jnp.float32)[None], 0.0)
            .reshape(2 * pairs * channels, spread)
            .astype(jnp.bfloat16)
            for part in (high, low)
        ]
        at_lane = jnp.where(lane_index == (offsets & (lanes - 1)), 1.0, 0.0).astype(jnp.bfloat16)
        values = lax.dot_general(
            jnp.concatenate(left, axis=1),
            jnp.concatenate([at_lane, at_lane], axis=1),
            NT,
            preferred_element_type=jnp.float32,
        )
        dense.append(values.reshape(2 * pairs, channels, lanes))
    both = jnp.concatenate(dense, axis=1)
    high, low = split_bf16(both)
    for half in range(2):
        high_out[:, :, half * lanes : (half + 1) * lanes] = high[half * pairs : (half + 1) * pairs]
        low_out[:, :, half * lanes : (half + 1) * lanes] = low[half * pairs : (half + 1) * pairs]


def build_projectors(groups, group, offsets, coefs, cells, lanes):
    atoms, shells, channels, spread = coefs.shape
    per_group = atoms // groups
    rows = per_group * shells * channels
    shape = jax.ShapeDtypeStruct((cells // 2, rows, 2 * lanes), jnp.bfloat16)
    spec = pl.BlockSpec((cells // 2, 2 * channels, 2 * lanes), lambda i: (0, i, 0))
    return pl.pallas_call(
        functools.partial(projector_kernel, groups),
        grid=(shells * per_group // 2,),
        out_shape=[shape, shape],
        in_specs=[SMEM, VMEM, VMEM],
        out_specs=[spec, spec],
        compiler_params=params(16),
        cost_estimate=pl.CostEstimate(
            flops=4 * rows * cells * lanes * spread,
            bytes_accessed=8 * rows * cells * lanes,
            transcendentals=0,
        ),
        name="projectors",
    )(group, offsets, coefs)


def product_kernel(n_chunks, *refs):
    w_high, w_low = refs[:2]
    f_high, f_low = refs[2 : 2 + n_chunks], refs[2 + n_chunks : 2 + 2 * n_chunks]
    grid_out, proj_out = refs[2 + 2 * n_chunks :]
    orbitals = grid_out.shape[0]
    groups = f_high[0].shape[0]

    @pl.when(pl.program_id(0) == 0)
    def _():
        grid_out[...] = jnp.zeros_like(grid_out)
        proj_out[...] = jnp.zeros_like(proj_out)

    total = 0.0
    for h in range(w_high.shape[0]):
        fields = [
            jnp.concatenate([part[g, h] for g in range(groups) for part in parts], axis=0)
            for parts in (f_high, f_low)
        ]
        right = jnp.concatenate(fields, axis=0)
        left_high = jnp.concatenate([fields[0], w_high[h]], axis=0)
        left_low = jnp.concatenate([fields[1], w_low[h]], axis=0)
        wide = lax.dot_general(left_high, right, NT, preferred_element_type=jnp.float32)
        low = lax.dot_general(left_low, fields[0], NT, preferred_element_type=jnp.float32)
        total += wide[:, :orbitals] + wide[:, orbitals:] + low
    grid_out[...] += total[:orbitals]
    proj_out[...] += total[orbitals:]


def products(projectors, highs, lows):
    pairs, rows, depth = projectors[0].shape
    groups, _, per, _ = highs[0].shape
    n_chunks = len(highs)
    orbitals = groups * per * n_chunks
    block = 6
    w_spec = pl.BlockSpec((block, rows, depth), lambda i: (i, 0, 0))
    f_spec = pl.BlockSpec((groups, block, per, depth), lambda i: (0, i, 0, 0))
    whole = lambda i: (0, 0)
    return pl.pallas_call(
        functools.partial(product_kernel, n_chunks),
        grid=(pairs // block,),
        out_shape=[
            jax.ShapeDtypeStruct((orbitals, orbitals), jnp.float32),
            jax.ShapeDtypeStruct((rows, orbitals), jnp.float32),
        ],
        in_specs=[w_spec] * 2 + [f_spec] * (2 * n_chunks),
        out_specs=[
            pl.BlockSpec((orbitals, orbitals), whole),
            pl.BlockSpec((rows, orbitals), whole),
        ],
        compiler_params=params(24),
        name="products",
    )(*projectors, *highs, *lows)


def gram_kernel(
    scale_point, scale_atom, proj_ref, right_ref, left_ref, corr_ref, grid_ref, out
):
    rows = right_ref.shape[0]
    projections = proj_ref[rows : 2 * rows, :] + right_ref[...] + left_ref[...]
    highest = lax.Precision.HIGHEST
    weighted = jnp.dot(
        corr_ref[...], projections, precision=highest, preferred_element_type=jnp.float32
    )
    atom_part = lax.dot_general(
        projections, weighted, TN, precision=highest, preferred_element_type=jnp.float32
    )
    out[...] = grid_ref[...] * scale_point + atom_part * scale_atom


def whole_columns(panel, potential, me):
    n_dom = lax.axis_size("dom")
    orbitals = panel.shape[0]
    n_chunks = math.gcd(MAX_CHUNKS, orbitals // n_dom)
    per_chunk = orbitals // n_chunks
    per_block = per_chunk // n_dom
    potentials = [potential] + [swap_over(potential, "dom", n_dom, m) for m in range(1, n_dom)]
    arrived = []
    for c in range(n_chunks):
        blocks = []
        for m in range(n_dom):
            first = c * per_chunk + (me ^ m) * per_block
            block = lax.dynamic_slice_in_dim(panel, first, per_block, 0)
            blocks.append(swap_over(block, "dom", n_dom, m) if m else block)
        arrived.append(blocks)
    for blocks in arrived:
        done = filter_orbitals(me.reshape(1), potentials, blocks)
        yield assemble(
            me.reshape(1), [swap_over(b, "dom", n_dom, m) if m else b for m, b in enumerate(done)]
        )


def plane_by_plane(panel, potential):
    n_dom = lax.axis_size("dom")
    diagonal = (potential + (SHIFT - CENTER_LEVEL)) * (2.0 / HALF_WIDTH)

    def twice_operator(field):
        low = lax.ppermute(field[:, -1:], "dom", [(i, (i + 1) % n_dom) for i in range(n_dom)])
        high = lax.ppermute(field[:, :1], "dom", [(i, (i - 1) % n_dom) for i in range(n_dom)])
        extended = jnp.concatenate([low, field, high], axis=1)
        near = extended[:, 2:] + extended[:, :-2]
        near += jnp.roll(field, 1, axis=2) + jnp.roll(field, -1, axis=2)
        padded = jnp.pad(field, ((0, 0), (0, 0), (0, 0), (1, 1)))
        near += padded[..., 2:] + padded[..., :-2]
        return diagonal * field - near / HALF_WIDTH

    def one_step(_, carry):
        before, current = carry
        return current, twice_operator(current) - before

    start = (panel, 0.5 * twice_operator(panel))
    return lax.fori_loop(0, DEGREE - 1, one_step, start)[1]


def on_device(panel, potential, point_offsets, point_coefs, correlation):
    orbitals, planes, rows, lanes = panel.shape
    n_dom, n_band, n_sub = (lax.axis_size(axis) for axis in ("dom", "band", "sub"))
    groups = n_band * n_sub
    me = lax.axis_index("dom")
    group = lax.axis_index(("band", "sub"))
    group_ref = group.reshape(1)

    cells = planes * rows
    projectors = build_projectors(groups, group_ref, point_offsets, point_coefs, cells, lanes)
    channels = correlation.shape[1]
    own_atoms = point_offsets.shape[0] // groups
    own_corr = lax.dynamic_slice_in_dim(correlation, group * own_atoms, own_atoms, 0)
    same_atom = jnp.eye(own_atoms, dtype=jnp.float32)
    corr_matrix = (same_atom[:, None, :, None] * own_corr[:, :, None, :]).reshape(
        own_atoms * channels, own_atoms * channels
    )

    if orbitals % n_dom == 0:
        chunks = whole_columns(panel, potential, me)
    else:
        chunks = [plane_by_plane(panel, potential)]
    filtered, highs, lows = [], [], []
    for own in chunks:
        filtered.append(own)
        pieces = []
        for m in range(n_band):
            over_band = swap_over(own, "band", n_band, m) if m else own
            pieces += [over_band] + [swap_over(over_band, "sub", n_sub, k) for k in range(1, n_sub)]
        high, low = regroup(group_ref, pieces)
        highs.append(high)
        lows.append(low)

    grid_part, proj = products(projectors, highs, lows)
    rows_atom = own_atoms * channels
    from_right = lax.ppermute(
        proj[:rows_atom], "dom", [(i, (i - 1) % n_dom) for i in range(n_dom)]
    )
    from_left = lax.ppermute(
        proj[2 * rows_atom :], "dom", [(i, (i + 1) % n_dom) for i in range(n_dom)]
    )
    scale_point = 1.0 / (cells * lanes * n_dom * groups)
    scale_atom = 1.0 / math.sqrt(point_offsets.shape[0] * n_dom)
    share = pl.pallas_call(
        functools.partial(gram_kernel, scale_point, scale_atom),
        out_shape=jax.ShapeDtypeStruct(grid_part.shape, jnp.float32),
        in_specs=[VMEM] * 5,
        out_specs=VMEM,
        compiler_params=params(8),
        name="gram_share",
    )(proj, from_right, from_left, corr_matrix, grid_part)

    gram_rows = 0.0
    for m in range(groups):
        part = lax.dynamic_slice_in_dim(share, (group ^ m) * orbitals, orbitals, 0)
        gram_rows += swap_over(part, ("band", "sub"), groups, m) if m else part
    if n_dom <= 8:
        gram_rows = sum(
            [gram_rows] + [swap_over(gram_rows, "dom", n_dom, m) for m in range(1, n_dom)]
        )
    else:
        gram_rows = lax.psum(gram_rows, "dom")
    return (jnp.concatenate(filtered, axis=0), gram_rows)


def solution(mesh):
    placed = (
        P(("slab", "band", "sub"), "dom", None, None),
        P(("slab", "dom"), None, None),
        P(("slab", "dom"), None, None),
        P(("slab", "dom"), None, None, None),
        P(("slab", "dom"), None, None),
    )
    return jax.shard_map(
        on_device,
        mesh=mesh,
        in_specs=placed,
        out_specs=(P(("slab", "band", "sub"), "dom", None, None), P(("slab", "band", "sub"), None)),
        check_vma=False,
    )
```

```python
import functools
import math

import jax
import jax.numpy as jnp
from jax import lax
from jax.experimental import pallas as pl
from jax.experimental.pallas import tpu as pltpu
from jax.sharding import PartitionSpec as P

DEGREE = 12

CENTER_LEVEL = 3.6
HALF_WIDTH = 3.4
SHIFT = 3.0

TOGETHER = 4
SUBLANES = 8
MIB = 1024 * 1024

VMEM = pl.BlockSpec(memory_space=pltpu.VMEM)
SMEM = pl.BlockSpec(memory_space=pltpu.SMEM)
NT = (((1,), (1,)), ((), ()))
TN = (((0,), (0,)), ((), ()))


def params(mib):
    return pltpu.CompilerParams(vmem_limit_bytes=mib * MIB)


def split_bf16(x):
    high = x.astype(jnp.bfloat16)
    return high, (x - high.astype(jnp.float32)).astype(jnp.bfloat16)


def shifted(x, by):
    size = lax.axis_size("dom")
    return lax.ppermute(x, "dom", [(i, (i - by) % size) for i in range(size)])


def swapped(x, axes, size, by):
    return lax.ppermute(x, axes, [(i, i ^ by) for i in range(size)])


def filter_kernel(n_dom, planes, rows, first, *refs):
    refs = list(refs)
    given = None if first else refs.pop(0)
    ins, outs = refs[:n_dom], refs[n_dom : 2 * n_dom]
    refs = refs[2 * n_dom :]
    diagonal = refs.pop(0) if first else given
    even, odd = refs
    half_planes = n_dom * planes // 2
    cells = planes * rows
    lanes = even.shape[3]
    scale = 1.0 / HALF_WIDTH

    for x in range(half_planes):
        for half in range(2):
            m, i = divmod(half * half_planes + x, planes)
            part = slice(half * TOGETHER, (half + 1) * TOGETHER)
            for y in range(rows):
                even[x, y, part] = ins[m][pl.ds(i * rows + y, TOGETHER, stride=cells), :]
                if first:
                    at = TOGETHER * cells + i * rows + y
                    level = ins[m][at : at + 1, :] + (SHIFT - CENTER_LEVEL)
                    diagonal[x, y, part] = jnp.broadcast_to(
                        level * (2.0 * scale), (TOGETHER, lanes)
                    )

    block = SUBLANES
    lane = lax.broadcasted_iota(jnp.int32, (block, SUBLANES, lanes), 2)
    at_start, at_end = lane == 0, lane == lanes - 1

    def twice_operator(source, x, y):
        here = slice(y, y + block)
        centre = source[x, here]
        if x == 0:
            near = pltpu.roll(source[half_planes - 1, here], TOGETHER, 1) + source[x + 1, here]
        elif x == half_planes - 1:
            near = pltpu.roll(source[0, here], TOGETHER, 1) + source[x - 1, here]
        else:
            near = source[x - 1, here] + source[x + 1, here]
        before = (y - 1) % rows
        after = (y + block) % rows
        near += jnp.concatenate([source[x, before : before + 1], centre[:-1]], axis=0)
        near += jnp.concatenate([centre[1:], source[x, after : after + 1]], axis=0)
        low = pltpu.roll(centre, 1, 2)
        high = pltpu.roll(centre, lanes - 1, 2)
        near += jnp.where(at_start, high, jnp.where(at_end, low, low + high))
        return diagonal[x, here] * centre - scale * near

    places = [(x, y) for x in range(half_planes) for y in range(0, rows, block)]

    def next_field(source, target):
        for x, y in places:
            target[x, y : y + block] = twice_operator(source, x, y) - target[x, y : y + block]

    for x, y in places:
        odd[x, y : y + block] = 0.5 * twice_operator(even, x, y)
    next_field(odd, even)

    def two_steps(_, carry):
        next_field(even, odd)
        next_field(odd, even)
        return carry

    lax.fori_loop(0, DEGREE // 2 - 1, two_steps, 0)
    for m in range(n_dom):
        for i in range(planes):
            half, x = divmod(m * planes + i, half_planes)
            for y in range(rows):
                at = (i * rows + y) * TOGETHER
                outs[m][at : at + TOGETHER, :] = even[
                    x, y, half * TOGETHER : (half + 1) * TOGETHER
                ]


def filter_orbitals(diagonal, blocks, planes, rows):
    n_dom = len(blocks)
    first = diagonal is None
    cells = planes * rows
    lanes = blocks[0].shape[1]
    field = (n_dom * planes // 2, rows, SUBLANES, lanes)
    out = jax.ShapeDtypeStruct((cells * TOGETHER, lanes), jnp.float32)
    extra = [jax.ShapeDtypeStruct(field, jnp.float32)] if first else []
    given = [] if first else [diagonal]
    size = n_dom * cells * TOGETHER * lanes
    return pl.pallas_call(
        functools.partial(filter_kernel, n_dom, planes, rows, first),
        out_shape=[out] * n_dom + extra,
        in_specs=[VMEM] * (n_dom + len(given)),
        out_specs=[VMEM] * (n_dom + len(extra)),
        scratch_shapes=[pltpu.VMEM(field, jnp.float32)] * 2,
        compiler_params=params(12),
        cost_estimate=pl.CostEstimate(
            flops=12 * DEGREE * size, bytes_accessed=8 * size, transcendentals=0
        ),
        name="chebyshev",
    )(*given, *blocks)


def assemble_kernel(me_ref, *refs):
    *pieces, orbital_first, cell_first = refs
    n_dom = len(pieces)
    cells = cell_first.shape[0]
    me = me_ref[0]
    for m, piece in enumerate(pieces):
        start = lax.rem(me + m, n_dom) * TOGETHER
        for t in range(TOGETHER):
            orbital_first[start + t] = piece[pl.ds(t, cells, stride=TOGETHER), :]
    for cell in range(cells):
        here = slice(cell * TOGETHER, (cell + 1) * TOGETHER)
        tile = jnp.concatenate([piece[here, :] for piece in pieces], axis=0)
        cell_first[cell] = pltpu.roll(tile, me * TOGETHER, 0)


def assemble(me, pieces):
    n_dom = len(pieces)
    rows, lanes = pieces[0].shape
    cells, orbitals = rows // TOGETHER, n_dom * TOGETHER
    return pl.pallas_call(
        assemble_kernel,
        out_shape=[
            jax.ShapeDtypeStruct((orbitals, cells, lanes), jnp.float32),
            jax.ShapeDtypeStruct((cells, orbitals, lanes), jnp.float32),
        ],
        in_specs=[SMEM] + [VMEM] * n_dom,
        out_specs=[VMEM] * 2,
        compiler_params=params(8),
        name="assemble",
    )(me.reshape(1), *pieces)


def projector_kernel(groups, group_ref, offsets_ref, coefs_ref, high_out, low_out):
    per_group = offsets_ref.shape[0] // groups
    _, shells, channels, spread = coefs_ref.shape
    lanes = spread
    cells = high_out.shape[1] // lanes
    pairs = per_group // 2
    row_index = lax.broadcasted_iota(jnp.int32, (cells, channels, spread), 0)
    lane_index = lax.broadcasted_iota(jnp.int32, (lanes, spread), 0)

    def two_atoms(step, carry):
        shell = step // pairs
        first_atom = group_ref[0] * per_group + 2 * (step % pairs)
        dense = []
        for i in range(2):
            offsets = offsets_ref[first_atom + i, pl.ds(shell, 1), :]
            coefs = coefs_ref[first_atom + i, shell]
            at_row = row_index == (offsets // lanes)[None]
            at_row &= (offsets >= 0)[None]
            left = [
                jnp.where(at_row, part.astype(jnp.float32)[None], 0.0)
                .reshape(cells * channels, spread)
                .astype(jnp.bfloat16)
                for part in split_bf16(coefs)
            ]
            at_lane = jnp.where(lane_index == (offsets & (lanes - 1)), 1.0, 0.0)
            at_lane = at_lane.astype(jnp.bfloat16)
            values = lax.dot_general(
                jnp.concatenate(left, axis=1),
                jnp.concatenate([at_lane, at_lane], axis=1),
                NT,
                preferred_element_type=jnp.float32,
            )
            dense.append(values.reshape(cells, channels, lanes))
        high, low = split_bf16(jnp.concatenate(dense, axis=1))
        rows = pl.ds(pl.multiple_of(step * 2 * channels, 2 * channels), 2 * channels)
        for cell in range(cells):
            high_out[rows, cell * lanes : (cell + 1) * lanes] = high[cell]
            low_out[rows, cell * lanes : (cell + 1) * lanes] = low[cell]
        return carry

    lax.fori_loop(0, shells * pairs, two_atoms, 0)


def build_projectors(groups, group, offsets, coefs, cells, lanes):
    atoms, shells, channels, spread = coefs.shape
    rows = atoms // groups * shells * channels
    shape = jax.ShapeDtypeStruct((rows, cells * lanes), jnp.bfloat16)
    return pl.pallas_call(
        functools.partial(projector_kernel, groups),
        out_shape=[shape, shape],
        in_specs=[SMEM, VMEM, VMEM],
        out_specs=[VMEM, VMEM],
        compiler_params=params(20),
        cost_estimate=pl.CostEstimate(
            flops=4 * rows * cells * lanes * spread,
            bytes_accessed=8 * rows * cells * lanes,
            transcendentals=0,
        ),
        name="projectors",
    )(group, offsets, coefs)


def product_kernel(n_chunks, w_high, w_low, *refs):
    *fields, grid_out, proj_out = refs
    orbitals = grid_out.shape[0]
    cells, _, lanes = fields[0].shape
    n_groups = len(fields) // n_chunks
    block = 12
    grid_out[...] = jnp.zeros_like(grid_out)
    proj_out[...] = jnp.zeros_like(proj_out)

    def one_block(step, carry):
        highs, lows = [], []
        for g in range(n_groups):
            for c in range(n_chunks):
                field = fields[c * n_groups + g][pl.ds(step * block, block)]
                high, low = split_bf16(field)
                highs.append(jnp.concatenate([high[k] for k in range(block)], axis=1))
                lows.append(jnp.concatenate([low[k] for k in range(block)], axis=1))
        high, low = jnp.concatenate(highs, axis=0), jnp.concatenate(lows, axis=0)
        depth = block * lanes
        part = pl.ds(pl.multiple_of(step * depth, depth), depth)
        left_high = jnp.concatenate([high, w_high[:, part]], axis=0)
        left_low = jnp.concatenate([low, w_low[:, part]], axis=0)
        right = jnp.concatenate([high, low], axis=0)
        wide = lax.dot_general(left_high, right, NT, preferred_element_type=jnp.float32)
        narrow = lax.dot_general(left_low, high, NT, preferred_element_type=jnp.float32)
        total = wide[:, :orbitals] + wide[:, orbitals:] + narrow
        grid_out[...] += total[:orbitals]
        proj_out[...] += total[orbitals:]
        return carry

    lax.fori_loop(0, cells // block, one_block, 0)


def products(projectors, fields):
    rows = projectors[0].shape[0]
    n_chunks, n_groups = len(fields), len(fields[0])
    orbitals = n_chunks * n_groups * fields[0][0].shape[1]
    return pl.pallas_call(
        functools.partial(product_kernel, n_chunks),
        out_shape=[
            jax.ShapeDtypeStruct((orbitals, orbitals), jnp.float32),
            jax.ShapeDtypeStruct((rows, orbitals), jnp.float32),
        ],
        in_specs=[VMEM] * (2 + n_chunks * n_groups),
        out_specs=[VMEM] * 2,
        compiler_params=params(32),
        name="products",
    )(*projectors, *[field for chunk in fields for field in chunk])


def gram_kernel(
    scales, groups, group_ref, proj_ref, right_ref, left_ref, corr_ref, grid_ref, kept, sent
):
    rows = right_ref.shape[0]
    orbitals = grid_ref.shape[0]
    projections = proj_ref[rows : 2 * rows, :] + right_ref[...] + left_ref[...]
    highest = lax.Precision.HIGHEST
    weighted = jnp.dot(
        corr_ref[...], projections, precision=highest, preferred_element_type=jnp.float32
    )
    atom_part = lax.dot_general(
        projections, weighted, TN, precision=highest, preferred_element_type=jnp.float32
    )
    share = grid_ref[...] * scales[0] + atom_part * scales[1]
    column = lax.broadcasted_iota(jnp.int32, share.shape, 1)
    width = orbitals // groups
    bit = 1
    while bit < groups:
        span = width * bit
        turned = jnp.where(
            (column & span) == 0,
            pltpu.roll(share, orbitals - span, 1),
            pltpu.roll(share, span, 1),
        )
        share = jnp.where((group_ref[0] & bit) != 0, turned, share)
        bit *= 2
    kept[...] = share[: orbitals // 2]
    sent[...] = share[orbitals // 2 :]


def gram_share(scales, groups, group, proj, right, left, corr, grid_part):
    half = jax.ShapeDtypeStruct((grid_part.shape[0] // 2, grid_part.shape[1]), jnp.float32)
    return pl.pallas_call(
        functools.partial(gram_kernel, scales, groups),
        out_shape=[half, half],
        in_specs=[SMEM] + [VMEM] * 5,
        out_specs=[VMEM] * 2,
        compiler_params=params(8),
        name="gram_share",
    )(group, proj, right, left, corr, grid_part)


def whole_columns(panel, potential, me, projectors):
    n_dom = lax.axis_size("dom")
    orbitals, planes, rows, lanes = panel.shape
    cells = planes * rows
    flat = panel.reshape(orbitals * cells, lanes)
    levels = potential.reshape(cells, lanes)
    size = TOGETHER * cells
    n_chunks = orbitals // (n_dom * TOGETHER)
    arrived = []
    for c in range(n_chunks):
        blocks = []
        for m in range(n_dom):
            first = (c * n_dom + lax.rem(me - m + n_dom, n_dom)) * size
            block = lax.dynamic_slice_in_dim(flat, first, size, 0)
            if c == 0:
                block = jnp.concatenate([block, levels], axis=0)
            blocks.append(shifted(block, m) if m else block)
        arrived.append(blocks)
    arrived[0], projectors = lax.optimization_barrier((arrived[0], projectors))
    diagonal = None
    filtered, fields = [], []
    for blocks in arrived:
        done = filter_orbitals(diagonal, blocks, planes, rows)
        if diagonal is None:
            diagonal = done[n_dom]
        pieces = [shifted(done[(n_dom - m) % n_dom], m) if m else done[0] for m in range(n_dom)]
        orbital_first, cell_first = assemble(me, pieces)
        filtered.append(orbital_first)
        fields.append(cell_first)
    filtered = jnp.concatenate(filtered, axis=0).reshape(panel.shape)
    return filtered, fields, projectors


def plane_by_plane(panel, potential):
    n_dom = lax.axis_size("dom")
    orbitals, planes, rows, lanes = panel.shape
    diagonal = (potential + (SHIFT - CENTER_LEVEL)) * (2.0 / HALF_WIDTH)

    def twice_operator(field):
        low, high = shifted(field[:, -1:], -1), shifted(field[:, :1], 1)
        extended = jnp.concatenate([low, field, high], axis=1)
        near = extended[:, 2:] + extended[:, :-2]
        near += jnp.roll(field, 1, axis=2) + jnp.roll(field, -1, axis=2)
        padded = jnp.pad(field, ((0, 0), (0, 0), (0, 0), (1, 1)))
        near += padded[..., 2:] + padded[..., :-2]
        return diagonal * field - near / HALF_WIDTH

    def one_step(_, carry):
        before, current = carry
        return current, twice_operator(current) - before

    start = (panel, 0.5 * twice_operator(panel))
    filtered = lax.fori_loop(0, DEGREE - 1, one_step, start)[1]
    return filtered, [filtered.reshape(orbitals, planes * rows, lanes).swapaxes(0, 1)]


def on_device(panel, potential, point_offsets, point_coefs, correlation):
    orbitals, planes, rows, lanes = panel.shape
    n_dom, n_band, n_sub = (lax.axis_size(axis) for axis in ("dom", "band", "sub"))
    groups = n_band * n_sub
    me = lax.axis_index("dom")
    group = lax.axis_index(("band", "sub"))
    group_ref = group.reshape(1)

    cells = planes * rows
    projectors = build_projectors(groups, group_ref, point_offsets, point_coefs, cells, lanes)
    channels = correlation.shape[1]
    own_atoms = point_offsets.shape[0] // groups
    own_corr = lax.dynamic_slice_in_dim(correlation, group * own_atoms, own_atoms, 0)
    same_atom = jnp.eye(own_atoms, dtype=jnp.float32)
    corr_matrix = (same_atom[:, None, :, None] * own_corr[:, :, None, :]).reshape(
        own_atoms * channels, own_atoms * channels
    )

    if orbitals % (n_dom * TOGETHER) == 0 and (n_dom * planes) % 2 == 0:
        filtered, own_fields, projectors = whole_columns(panel, potential, me, projectors)
    else:
        filtered, own_fields = plane_by_plane(panel, potential)
    fields = []
    for own in own_fields:
        chunk = []
        for m in range(n_band):
            over_band = swapped(own, "band", n_band, m) if m else own
            chunk += [over_band] + [swapped(over_band, "sub", n_sub, k) for k in range(1, n_sub)]
        fields.append(chunk)

    grid_part, proj = products(projectors, fields)
    rows_atom = own_atoms * channels
    from_right = shifted(proj[:rows_atom], 1)
    from_left = shifted(proj[2 * rows_atom :], -1)
    scale_point = 1.0 / (cells * lanes * n_dom * groups)
    scale_atom = 1.0 / math.sqrt(point_offsets.shape[0] * n_dom)
    kept, sent = gram_share(
        (scale_point, scale_atom), groups, group_ref, proj, from_right, from_left, corr_matrix,
        grid_part,
    )
    by = groups // 2
    while by:
        kept += swapped(sent, ("band", "sub"), groups, by)
        by //= 2
        if by:
            kept, sent = kept[: by * orbitals], kept[by * orbitals :]
    by = 1
    while by < n_dom:
        kept += swapped(kept, "dom", n_dom, by)
        by *= 2
    return filtered, kept


def solution(mesh):
    placed = (
        P(("slab", "band", "sub"), "dom", None, None),
        P(("slab", "dom"), None, None),
        P(("slab", "dom"), None, None),
        P(("slab", "dom"), None, None, None),
        P(("slab", "dom"), None, None),
    )
    return jax.shard_map(
        on_device,
        mesh=mesh,
        in_specs=placed,
        out_specs=(P(("slab", "band", "sub"), "dom", None, None), P(("slab", "band", "sub"), None)),
        check_vma=False,
    )
```

```python
import functools
import math

import jax
import jax.numpy as jnp
from jax import lax
from jax.experimental import pallas as pl
from jax.experimental.pallas import tpu as pltpu
from jax.sharding import PartitionSpec as P

DEGREE = 12

CENTER_LEVEL = 3.6
HALF_WIDTH = 3.4
SHIFT = 3.0

TOGETHER = 4
SUBLANES = 8
MIB = 1024 * 1024

VMEM = pl.BlockSpec(memory_space=pltpu.VMEM)
SMEM = pl.BlockSpec(memory_space=pltpu.SMEM)
NT = (((1,), (1,)), ((), ()))
TN = (((0,), (0,)), ((), ()))


def params(mib):
    return pltpu.CompilerParams(vmem_limit_bytes=mib * MIB)


def split_bf16(x):
    high = x.astype(jnp.bfloat16)
    return high, (x - high.astype(jnp.float32)).astype(jnp.bfloat16)


def shifted(x, by):
    size = lax.axis_size("dom")
    return lax.ppermute(x, "dom", [(i, (i - by) % size) for i in range(size)])


def transposed(x):
    return lax.all_to_all(x, "dom", split_axis=0, concat_axis=0, tiled=True)


def swapped(x, axes, size, by):
    return lax.ppermute(x, axes, [(i, i ^ by) for i in range(size)])


def filter_kernel(n_dom, planes, rows, first, *refs):
    refs = list(refs)
    given = None if first else refs.pop(0)
    ins, outs = refs[:2]
    refs = refs[2:]
    diagonal = refs.pop(0) if first else given
    even, odd = refs
    half_planes = n_dom * planes // 2
    cells = planes * rows
    lanes = even.shape[3]
    scale = 1.0 / HALF_WIDTH

    for x in range(half_planes):
        for half in range(2):
            m, i = divmod(half * half_planes + x, planes)
            part = slice(half * TOGETHER, (half + 1) * TOGETHER)
            for y in range(rows):
                even[x, y, part] = ins[m, pl.ds(i * rows + y, TOGETHER, stride=cells), :]
                if first:
                    at = TOGETHER * cells + i * rows + y
                    level = ins[m, at : at + 1, :] + (SHIFT - CENTER_LEVEL)
                    diagonal[x, y, part] = jnp.broadcast_to(
                        level * (2.0 * scale), (TOGETHER, lanes)
                    )

    block = SUBLANES
    lane = lax.broadcasted_iota(jnp.int32, (block, SUBLANES, lanes), 2)
    at_start, at_end = lane == 0, lane == lanes - 1

    def twice_operator(source, x, y):
        here = slice(y, y + block)
        centre = source[x, here]
        if x == 0:
            near = pltpu.roll(source[half_planes - 1, here], TOGETHER, 1) + source[x + 1, here]
        elif x == half_planes - 1:
            near = pltpu.roll(source[0, here], TOGETHER, 1) + source[x - 1, here]
        else:
            near = source[x - 1, here] + source[x + 1, here]
        before = (y - 1) % rows
        after = (y + block) % rows
        near += jnp.concatenate([source[x, before : before + 1], centre[:-1]], axis=0)
        near += jnp.concatenate([centre[1:], source[x, after : after + 1]], axis=0)
        low = pltpu.roll(centre, 1, 2)
        high = pltpu.roll(centre, lanes - 1, 2)
        near += jnp.where(at_start, high, jnp.where(at_end, low, low + high))
        return diagonal[x, here] * centre - scale * near

    places = [(x, y) for x in range(half_planes) for y in range(0, rows, block)]

    def next_field(source, target):
        for x, y in places:
            target[x, y : y + block] = twice_operator(source, x, y) - target[x, y : y + block]

    for x, y in places:
        odd[x, y : y + block] = 0.5 * twice_operator(even, x, y)
    next_field(odd, even)

    def two_steps(_, carry):
        next_field(even, odd)
        next_field(odd, even)
        return carry

    lax.fori_loop(0, DEGREE // 2 - 1, two_steps, 0)
    for m in range(n_dom):
        for i in range(planes):
            half, x = divmod(m * planes + i, half_planes)
            for y in range(rows):
                at = (i * rows + y) * TOGETHER
                outs[m, at : at + TOGETHER, :] = even[
                    x, y, half * TOGETHER : (half + 1) * TOGETHER
                ]


def filter_orbitals(diagonal, blocks, planes, rows):
    n_dom, _, lanes = blocks.shape
    first = diagonal is None
    cells = planes * rows
    field = (n_dom * planes // 2, rows, SUBLANES, lanes)
    out = jax.ShapeDtypeStruct((n_dom, cells * TOGETHER, lanes), jnp.float32)
    extra = [jax.ShapeDtypeStruct(field, jnp.float32)] if first else []
    given = [] if first else [diagonal]
    size = n_dom * cells * TOGETHER * lanes
    return pl.pallas_call(
        functools.partial(filter_kernel, n_dom, planes, rows, first),
        out_shape=[out] + extra,
        in_specs=[VMEM] * (1 + len(given)),
        out_specs=[VMEM] * (1 + len(extra)),
        scratch_shapes=[pltpu.VMEM(field, jnp.float32)] * 2,
        compiler_params=params(8),
        cost_estimate=pl.CostEstimate(
            flops=12 * DEGREE * size, bytes_accessed=8 * size, transcendentals=0
        ),
        name="chebyshev",
    )(*given, blocks)


def assemble_kernel(pieces, orbital_first, cell_first):
    n_dom = pieces.shape[0]
    cells = cell_first.shape[0]
    for m in range(n_dom):
        for t in range(TOGETHER):
            orbital_first[m * TOGETHER + t] = pieces[m, pl.ds(t, cells, stride=TOGETHER), :]
    for cell in range(cells):
        here = slice(cell * TOGETHER, (cell + 1) * TOGETHER)
        cell_first[cell] = jnp.concatenate([pieces[m, here, :] for m in range(n_dom)], axis=0)


def assemble(pieces):
    n_dom, rows, lanes = pieces.shape
    cells, orbitals = rows // TOGETHER, n_dom * TOGETHER
    return pl.pallas_call(
        assemble_kernel,
        out_shape=[
            jax.ShapeDtypeStruct((orbitals, cells, lanes), jnp.float32),
            jax.ShapeDtypeStruct((cells, orbitals, lanes), jnp.float32),
        ],
        in_specs=[VMEM],
        out_specs=[VMEM] * 2,
        compiler_params=params(8),
        name="assemble",
    )(pieces)


def projector_kernel(groups, group_ref, offsets_ref, coefs_ref, high_out, low_out):
    per_group = offsets_ref.shape[0] // groups
    _, shells, channels, spread = coefs_ref.shape
    lanes = spread
    cells = high_out.shape[1] // lanes
    pairs = per_group // 2
    row_index = lax.broadcasted_iota(jnp.int32, (cells, channels, spread), 0)
    lane_index = lax.broadcasted_iota(jnp.int32, (lanes, spread), 0)

    def two_atoms(step, carry):
        shell = step // pairs
        first_atom = group_ref[0] * per_group + 2 * (step % pairs)
        dense = []
        for i in range(2):
            offsets = offsets_ref[first_atom + i, pl.ds(shell, 1), :]
            coefs = coefs_ref[first_atom + i, shell]
            at_row = row_index == (offsets // lanes)[None]
            at_row &= (offsets >= 0)[None]
            left = [
                jnp.where(at_row, part.astype(jnp.float32)[None], 0.0)
                .reshape(cells * channels, spread)
                .astype(jnp.bfloat16)
                for part in split_bf16(coefs)
            ]
            at_lane = jnp.where(lane_index == (offsets & (lanes - 1)), 1.0, 0.0)
            at_lane = at_lane.astype(jnp.bfloat16)
            values = lax.dot_general(
                jnp.concatenate(left, axis=1),
                jnp.concatenate([at_lane, at_lane], axis=1),
                NT,
                preferred_element_type=jnp.float32,
            )
            dense.append(values.reshape(cells, channels, lanes))
        high, low = split_bf16(jnp.concatenate(dense, axis=1))
        rows = pl.ds(pl.multiple_of(step * 2 * channels, 2 * channels), 2 * channels)
        for cell in range(cells):
            high_out[rows, cell * lanes : (cell + 1) * lanes] = high[cell]
            low_out[rows, cell * lanes : (cell + 1) * lanes] = low[cell]
        return carry

    lax.fori_loop(0, shells * pairs, two_atoms, 0)


def build_projectors(groups, group, offsets, coefs, cells, lanes):
    atoms, shells, channels, spread = coefs.shape
    rows = atoms // groups * shells * channels
    shape = jax.ShapeDtypeStruct((rows, cells * lanes), jnp.bfloat16)
    return pl.pallas_call(
        functools.partial(projector_kernel, groups),
        out_shape=[shape, shape],
        in_specs=[SMEM, VMEM, VMEM],
        out_specs=[VMEM, VMEM],
        compiler_params=params(12),
        cost_estimate=pl.CostEstimate(
            flops=4 * rows * cells * lanes * spread,
            bytes_accessed=8 * rows * cells * lanes,
            transcendentals=0,
        ),
        name="projectors",
    )(group, offsets, coefs)


def product_kernel(n_chunks, groups, group_ref, w_high, w_low, *refs):
    *fields, grid_out, proj_out = refs
    orbitals = grid_out.shape[0]
    cells, _, lanes = fields[0].shape
    n_groups = len(fields) // n_chunks
    block = 12

    def parts(start):
        highs, lows = [], []
        for g in range(n_groups):
            for c in range(n_chunks):
                high, low = split_bf16(fields[c * n_groups + g][pl.ds(start, block)])
                highs.append(jnp.concatenate([high[k] for k in range(block)], axis=1))
                lows.append(jnp.concatenate([low[k] for k in range(block)], axis=1))
        return jnp.concatenate(highs, axis=0), jnp.concatenate(lows, axis=0)

    def product(left_high, left_low, high, low):
        right = jnp.concatenate([high, low], axis=0)
        wide = lax.dot_general(left_high, right, NT, preferred_element_type=jnp.float32)
        narrow = lax.dot_general(left_low, high, NT, preferred_element_type=jnp.float32)
        return wide[:, :orbitals] + wide[:, orbitals:] + narrow

    def grid_block(step, carry):
        high, low = parts(group_ref[0] * (cells // groups) + step * block)
        grid_out[...] += product(high, low, high, low)
        return carry

    def proj_block(step, carry):
        high, low = parts(step * block)
        depth = block * lanes
        here = pl.ds(pl.multiple_of(step * depth, depth), depth)
        proj_out[...] += product(w_high[:, here], w_low[:, here], high, low)
        return carry

    grid_out[...] = jnp.zeros_like(grid_out)
    proj_out[...] = jnp.zeros_like(proj_out)
    lax.fori_loop(0, cells // (groups * block), grid_block, 0)
    lax.fori_loop(0, cells // block, proj_block, 0)


def products(groups, group, projectors, fields):
    rows = projectors[0].shape[0]
    n_chunks, n_groups = len(fields), len(fields[0])
    orbitals = n_chunks * n_groups * fields[0][0].shape[1]
    return pl.pallas_call(
        functools.partial(product_kernel, n_chunks, groups),
        out_shape=[
            jax.ShapeDtypeStruct((orbitals, orbitals), jnp.float32),
            jax.ShapeDtypeStruct((rows, orbitals), jnp.float32),
        ],
        in_specs=[SMEM] + [VMEM] * (2 + n_chunks * n_groups),
        out_specs=[VMEM] * 2,
        compiler_params=params(12),
        name="products",
    )(group, *projectors, *[field for chunk in fields for field in chunk])


def gram_kernel(
    scales, groups, group_ref, proj_ref, right_ref, left_ref, corr_ref, grid_ref, kept, sent
):
    rows = right_ref.shape[0]
    orbitals = grid_ref.shape[0]
    projections = proj_ref[rows : 2 * rows, :] + right_ref[...] + left_ref[...]
    highest = lax.Precision.HIGHEST
    weighted = jnp.dot(
        corr_ref[...], projections, precision=highest, preferred_element_type=jnp.float32
    )
    atom_part = lax.dot_general(
        projections, weighted, TN, precision=highest, preferred_element_type=jnp.float32
    )
    share = grid_ref[...] * scales[0] + atom_part * scales[1]
    column = lax.broadcasted_iota(jnp.int32, share.shape, 1)
    width = orbitals // groups
    bit = 1
    while bit < groups:
        span = width * bit
        turned = jnp.where(
            (column & span) == 0,
            pltpu.roll(share, orbitals - span, 1),
            pltpu.roll(share, span, 1),
        )
        share = jnp.where((group_ref[0] & bit) != 0, turned, share)
        bit *= 2
    kept[...] = share[: orbitals // 2]
    sent[...] = share[orbitals // 2 :]


def gram_share(scales, groups, group, proj, right, left, corr, grid_part):
    half = jax.ShapeDtypeStruct((grid_part.shape[0] // 2, grid_part.shape[1]), jnp.float32)
    return pl.pallas_call(
        functools.partial(gram_kernel, scales, groups),
        out_shape=[half, half],
        in_specs=[SMEM] + [VMEM] * 5,
        out_specs=[VMEM] * 2,
        compiler_params=params(8),
        name="gram_share",
    )(group, proj, right, left, corr, grid_part)


def whole_columns(panel, potential, projectors):
    n_dom = lax.axis_size("dom")
    orbitals, planes, rows, lanes = panel.shape
    cells = planes * rows
    n_chunks = orbitals // (n_dom * TOGETHER)
    by_chunk = panel.reshape(n_chunks, n_dom, TOGETHER * cells, lanes)
    levels = jnp.broadcast_to(potential.reshape(1, cells, lanes), (n_dom, cells, lanes))
    arrived = []
    for c in range(n_chunks):
        blocks = by_chunk[c]
        if c == 0:
            blocks = jnp.concatenate([blocks, levels], axis=1)
        arrived.append(transposed(blocks))
    arrived[0], projectors = lax.optimization_barrier((arrived[0], projectors))
    diagonal = None
    filtered, fields = [], []
    for blocks in arrived:
        done = filter_orbitals(diagonal, blocks, planes, rows)
        if diagonal is None:
            diagonal = done[1]
        orbital_first, cell_first = assemble(transposed(done[0]))
        filtered.append(orbital_first)
        fields.append(cell_first)
    filtered = jnp.concatenate(filtered, axis=0).reshape(panel.shape)
    return filtered, fields, projectors


def plane_by_plane(panel, potential):
    n_dom = lax.axis_size("dom")
    orbitals, planes, rows, lanes = panel.shape
    diagonal = (potential + (SHIFT - CENTER_LEVEL)) * (2.0 / HALF_WIDTH)

    def twice_operator(field):
        low, high = shifted(field[:, -1:], -1), shifted(field[:, :1], 1)
        extended = jnp.concatenate([low, field, high], axis=1)
        near = extended[:, 2:] + extended[:, :-2]
        near += jnp.roll(field, 1, axis=2) + jnp.roll(field, -1, axis=2)
        padded = jnp.pad(field, ((0, 0), (0, 0), (0, 0), (1, 1)))
        near += padded[..., 2:] + padded[..., :-2]
        return diagonal * field - near / HALF_WIDTH

    def one_step(_, carry):
        before, current = carry
        return current, twice_operator(current) - before

    start = (panel, 0.5 * twice_operator(panel))
    filtered = lax.fori_loop(0, DEGREE - 1, one_step, start)[1]
    return filtered, [filtered.reshape(orbitals, planes * rows, lanes).swapaxes(0, 1)]


def on_device(panel, potential, point_offsets, point_coefs, correlation):
    orbitals, planes, rows, lanes = panel.shape
    n_dom, n_band, n_sub = (lax.axis_size(axis) for axis in ("dom", "band", "sub"))
    groups = n_band * n_sub
    group = lax.axis_index(("band", "sub"))
    group_ref = group.reshape(1)

    cells = planes * rows
    projectors = build_projectors(groups, group_ref, point_offsets, point_coefs, cells, lanes)
    channels = correlation.shape[1]
    own_atoms = point_offsets.shape[0] // groups
    own_corr = lax.dynamic_slice_in_dim(correlation, group * own_atoms, own_atoms, 0)
    same_atom = jnp.eye(own_atoms, dtype=jnp.float32)
    corr_matrix = (same_atom[:, None, :, None] * own_corr[:, :, None, :]).reshape(
        own_atoms * channels, own_atoms * channels
    )

    if orbitals % (n_dom * TOGETHER) == 0 and (n_dom * planes) % 2 == 0:
        filtered, own_fields, projectors = whole_columns(panel, potential, projectors)
    else:
        filtered, own_fields = plane_by_plane(panel, potential)
    fields = []
    for own in own_fields:
        chunk = []
        for m in range(n_band):
            over_band = swapped(own, "band", n_band, m) if m else own
            chunk += [over_band] + [swapped(over_band, "sub", n_sub, k) for k in range(1, n_sub)]
        fields.append(chunk)

    grid_part, proj = products(groups, group_ref, projectors, fields)
    rows_atom = own_atoms * channels
    from_right = shifted(proj[:rows_atom], 1)
    from_left = shifted(proj[2 * rows_atom :], -1)
    scale_point = 1.0 / (cells * lanes * n_dom)
    scale_atom = 1.0 / math.sqrt(point_offsets.shape[0] * n_dom)
    kept, sent = gram_share(
        (scale_point, scale_atom), groups, group_ref, proj, from_right, from_left, corr_matrix,
        grid_part,
    )
    by = groups // 2
    while by:
        kept += swapped(sent, ("band", "sub"), groups, by)
        by //= 2
        if by:
            kept, sent = kept[: by * orbitals], kept[by * orbitals :]
    by = 1
    while by < n_dom:
        kept += swapped(kept, "dom", n_dom, by)
        by *= 2
    return filtered, kept


def solution(mesh):
    placed = (
        P(("slab", "band", "sub"), "dom", None, None),
        P(("slab", "dom"), None, None),
        P(("slab", "dom"), None, None),
        P(("slab", "dom"), None, None, None),
        P(("slab", "dom"), None, None),
    )
    return jax.shard_map(
        on_device,
        mesh=mesh,
        in_specs=placed,
        out_specs=(P(("slab", "band", "sub"), "dom", None, None), P(("slab", "band", "sub"), None)),
        check_vma=False,
    )
```

```python
import functools
import math

import jax
import jax.numpy as jnp
from jax import lax
from jax.experimental import pallas as pl
from jax.experimental.pallas import tpu as pltpu
from jax.sharding import PartitionSpec as P

DEGREE = 12

CENTER_LEVEL = 3.6
HALF_WIDTH = 3.4
SHIFT = 3.0

TOGETHER = 4
SUBLANES = 8
MIB = 1024 * 1024

VMEM = pl.BlockSpec(memory_space=pltpu.VMEM)
SMEM = pl.BlockSpec(memory_space=pltpu.SMEM)
NT = (((1,), (1,)), ((), ()))
TN = (((0,), (0,)), ((), ()))


def params(mib):
    return pltpu.CompilerParams(vmem_limit_bytes=mib * MIB)


def split_bf16(x):
    high = x.astype(jnp.bfloat16)
    return high, (x - high.astype(jnp.float32)).astype(jnp.bfloat16)


def shifted(x, by):
    size = lax.axis_size("dom")
    return lax.ppermute(x, "dom", [(i, (i - by) % size) for i in range(size)])


def swapped(x, axes, size, by):
    return lax.ppermute(x, axes, [(i, i ^ by) for i in range(size)])


def filter_kernel(n_dom, planes, rows, starts, first, me_ref, *refs):
    refs = list(refs)
    given = None if first else refs.pop(0)
    ins, outs = refs[:n_dom], refs[n_dom : 2 * n_dom]
    refs = refs[2 * n_dom :]
    diagonal = refs.pop(0) if first else given
    even, odd = refs
    half_planes = n_dom * planes // 2
    cells = planes * rows
    lanes = even.shape[3]
    scale = 1.0 / HALF_WIDTH
    mirrored = (me_ref[0] & 1) != 0
    plane_at = [jnp.where(mirrored, planes - 1 - i, i) for i in range(planes)]

    for x in range(half_planes):
        for half in range(2):
            m, i = divmod(half * half_planes + x, planes)
            part = slice(half * TOGETHER, (half + 1) * TOGETHER)
            base = starts[m] + plane_at[i] * rows
            for y in range(rows):
                even[x, y, part] = ins[m][pl.ds(base + y, TOGETHER, stride=cells), :]
                if first:
                    level = ins[m][pl.ds(base + (TOGETHER * cells + y), 1), :]
                    diagonal[x, y, part] = jnp.broadcast_to(
                        (level + (SHIFT - CENTER_LEVEL)) * (2.0 * scale), (TOGETHER, lanes)
                    )

    block = SUBLANES
    lane = lax.broadcasted_iota(jnp.int32, (block, SUBLANES, lanes), 2)
    at_start, at_end = lane == 0, lane == lanes - 1

    def twice_operator(source, x, y):
        here = slice(y, y + block)
        centre = source[x, here]
        if x == 0:
            near = pltpu.roll(source[half_planes - 1, here], TOGETHER, 1) + source[x + 1, here]
        elif x == half_planes - 1:
            near = pltpu.roll(source[0, here], TOGETHER, 1) + source[x - 1, here]
        else:
            near = source[x - 1, here] + source[x + 1, here]
        before = (y - 1) % rows
        after = (y + block) % rows
        near += jnp.concatenate([source[x, before : before + 1], centre[:-1]], axis=0)
        near += jnp.concatenate([centre[1:], source[x, after : after + 1]], axis=0)
        low = pltpu.roll(centre, 1, 2)
        high = pltpu.roll(centre, lanes - 1, 2)
        near += jnp.where(at_start, high, jnp.where(at_end, low, low + high))
        return diagonal[x, here] * centre - scale * near

    places = [(x, y) for x in range(half_planes) for y in range(0, rows, block)]

    def next_field(source, target):
        for x, y in places:
            target[x, y : y + block] = twice_operator(source, x, y) - target[x, y : y + block]

    for x, y in places:
        odd[x, y : y + block] = 0.5 * twice_operator(even, x, y)
    next_field(odd, even)

    def two_steps(_, carry):
        next_field(even, odd)
        next_field(odd, even)
        return carry

    lax.fori_loop(0, DEGREE // 2 - 1, two_steps, 0)
    for m in range(n_dom):
        for i in range(planes):
            half, x = divmod(m * planes + i, half_planes)
            part = slice(half * TOGETHER, (half + 1) * TOGETHER)
            for y in range(rows):
                here = slice(y * TOGETHER, (y + 1) * TOGETHER)
                outs[m][plane_at[i], here, :] = even[x, y, part]


def filter_orbitals(me, diagonal, blocks, starts, planes, rows):
    n_dom = len(blocks)
    first = diagonal is None
    lanes = blocks[0].shape[1]
    field = (n_dom * planes // 2, rows, SUBLANES, lanes)
    out = jax.ShapeDtypeStruct((planes, rows * TOGETHER, lanes), jnp.float32)
    extra = [jax.ShapeDtypeStruct(field, jnp.float32)] if first else []
    given = [] if first else [diagonal]
    size = n_dom * planes * rows * TOGETHER * lanes
    return pl.pallas_call(
        functools.partial(filter_kernel, n_dom, planes, rows, starts, first),
        out_shape=[out] * n_dom + extra,
        in_specs=[SMEM] + [VMEM] * (n_dom + len(given)),
        out_specs=[VMEM] * (n_dom + len(extra)),
        scratch_shapes=[pltpu.VMEM(field, jnp.float32)] * 2,
        compiler_params=params(8),
        cost_estimate=pl.CostEstimate(
            flops=12 * DEGREE * size, bytes_accessed=8 * size, transcendentals=0
        ),
        name="chebyshev",
    )(me, *given, *blocks)


def assemble_kernel(n_dom, n_band, me_ref, band_ref, *refs):
    pieces, orbital_first, parts = refs[:n_dom], refs[n_dom], refs[n_dom + 1 :]
    cells = orbital_first.shape[1]
    share = cells // n_band
    me = me_ref[0]
    for m, piece in enumerate(pieces):
        start = (me ^ m) * TOGETHER
        for t in range(TOGETHER):
            orbital_first[start + t] = piece[pl.ds(t, cells, stride=TOGETHER), :]
    per_load = SUBLANES // TOGETHER
    together = SUBLANES // TOGETHER
    for p, part in enumerate(parts):
        base = pl.multiple_of((band_ref[0] ^ p) * (share * TOGETHER), SUBLANES)
        for first in range(0, share, per_load):
            loaded = [
                piece[pl.ds(base + first * TOGETHER, SUBLANES), :] for piece in pieces
            ]
            for k in range(per_load):
                here = slice(k * TOGETHER, (k + 1) * TOGETHER)
                for q in range(n_dom // together):
                    tile = jnp.concatenate(
                        [loaded[q * together + i][here] for i in range(together)], axis=0
                    )
                    tile = jnp.where((me & 1) != 0, pltpu.roll(tile, TOGETHER, 0), tile)
                    row = pl.multiple_of((q ^ (me // together)) * SUBLANES, SUBLANES)
                    part[first + k, pl.ds(row, SUBLANES), :] = tile


def assemble(me, band, n_band, pieces):
    n_dom = len(pieces)
    planes, rows, lanes = pieces[0].shape
    cells, orbitals = planes * rows // TOGETHER, n_dom * TOGETHER
    part = jax.ShapeDtypeStruct((cells // n_band, orbitals, lanes), jnp.float32)
    return pl.pallas_call(
        functools.partial(assemble_kernel, n_dom, n_band),
        out_shape=[jax.ShapeDtypeStruct((orbitals, cells, lanes), jnp.float32)] + [part] * n_band,
        in_specs=[SMEM] * 2 + [VMEM] * n_dom,
        out_specs=[VMEM] * (1 + n_band),
        compiler_params=params(8),
        name="assemble",
    )(me, band, *[piece.reshape(planes * rows, lanes) for piece in pieces])


def projector_kernel(n_band, n_sub, band_ref, sub_ref, offsets_ref, coefs_ref, high_out, low_out):
    atoms, shells, channels, spread = coefs_ref.shape
    own = atoms // (n_band * n_sub)
    lanes = spread
    cells = high_out.shape[1] // lanes
    pairs = own // 2
    row_index = lax.broadcasted_iota(jnp.int32, (cells, channels, spread), 0)
    row_index += band_ref[0] * cells
    lane_index = lax.broadcasted_iota(jnp.int32, (lanes, spread), 0)

    def two_atoms(step, carry):
        shell = step // (n_band * pairs)
        band = band_ref[0] ^ ((step // pairs) % n_band)
        first_atom = (sub_ref[0] * n_band + band) * own + 2 * (step % pairs)
        dense = []
        for i in range(2):
            offsets = offsets_ref[first_atom + i, pl.ds(shell, 1), :]
            coefs = coefs_ref[first_atom + i, shell]
            at_row = row_index == (offsets // lanes)[None]
            at_row &= (offsets >= 0)[None]
            left = [
                jnp.where(at_row, part.astype(jnp.float32)[None], 0.0)
                .reshape(cells * channels, spread)
                .astype(jnp.bfloat16)
                for part in split_bf16(coefs)
            ]
            at_lane = jnp.where(lane_index == (offsets & (lanes - 1)), 1.0, 0.0)
            at_lane = at_lane.astype(jnp.bfloat16)
            values = lax.dot_general(
                jnp.concatenate(left, axis=1),
                jnp.concatenate([at_lane, at_lane], axis=1),
                NT,
                preferred_element_type=jnp.float32,
            )
            dense.append(values.reshape(cells, channels, lanes))
        high, low = split_bf16(jnp.concatenate(dense, axis=1))
        rows = pl.ds(pl.multiple_of(step * 2 * channels, 2 * channels), 2 * channels)
        for cell in range(cells):
            high_out[rows, cell * lanes : (cell + 1) * lanes] = high[cell]
            low_out[rows, cell * lanes : (cell + 1) * lanes] = low[cell]
        return carry

    lax.fori_loop(0, shells * n_band * pairs, two_atoms, 0)


def build_projectors(n_band, n_sub, band, sub, offsets, coefs, cells, lanes):
    atoms, shells, channels, spread = coefs.shape
    rows = atoms // n_sub * shells * channels
    shape = jax.ShapeDtypeStruct((rows, cells * lanes), jnp.bfloat16)
    return pl.pallas_call(
        functools.partial(projector_kernel, n_band, n_sub),
        out_shape=[shape, shape],
        in_specs=[SMEM, SMEM, VMEM, VMEM],
        out_specs=[VMEM, VMEM],
        compiler_params=params(8),
        cost_estimate=pl.CostEstimate(
            flops=4 * rows * cells * lanes * spread,
            bytes_accessed=8 * rows * cells * lanes,
            transcendentals=0,
        ),
        name="projectors",
    )(band, sub, offsets, coefs)


def product_kernel(n_chunks, n_sub, sub_ref, w_high, w_low, *refs):
    *fields, grid_out, proj_out = refs
    orbitals = grid_out.shape[0]
    cells, _, lanes = fields[0].shape
    n_groups = len(fields) // n_chunks
    block = 12

    def parts(start):
        highs, lows = [], []
        for g in range(n_groups):
            for c in range(n_chunks):
                high, low = split_bf16(fields[c * n_groups + g][pl.ds(start, block)])
                highs.append(jnp.concatenate([high[k] for k in range(block)], axis=1))
                lows.append(jnp.concatenate([low[k] for k in range(block)], axis=1))
        return jnp.concatenate(highs, axis=0), jnp.concatenate(lows, axis=0)

    def product(left_high, left_low, high, low):
        right = jnp.concatenate([high, low], axis=0)
        wide = lax.dot_general(left_high, right, NT, preferred_element_type=jnp.float32)
        narrow = lax.dot_general(left_low, high, NT, preferred_element_type=jnp.float32)
        return wide[:, :orbitals] + wide[:, orbitals:] + narrow

    def grid_block(step, carry):
        high, low = parts(sub_ref[0] * (cells // n_sub) + step * block)
        grid_out[...] += product(high, low, high, low)
        return carry

    def proj_block(step, carry):
        high, low = parts(step * block)
        depth = block * lanes
        here = pl.ds(pl.multiple_of(step * depth, depth), depth)
        proj_out[...] += product(w_high[:, here], w_low[:, here], high, low)
        return carry

    grid_out[...] = jnp.zeros_like(grid_out)
    proj_out[...] = jnp.zeros_like(proj_out)
    lax.fori_loop(0, cells // (n_sub * block), grid_block, 0)
    lax.fori_loop(0, cells // block, proj_block, 0)


def products(n_sub, sub, projectors, fields):
    rows = projectors[0].shape[0]
    n_chunks, n_groups = len(fields), len(fields[0])
    orbitals = n_chunks * n_groups * fields[0][0].shape[1]
    return pl.pallas_call(
        functools.partial(product_kernel, n_chunks, n_sub),
        out_shape=[
            jax.ShapeDtypeStruct((orbitals, orbitals), jnp.float32),
            jax.ShapeDtypeStruct((rows, orbitals), jnp.float32),
        ],
        in_specs=[SMEM] + [VMEM] * (2 + n_chunks * n_groups),
        out_specs=[VMEM] * 2,
        compiler_params=params(12),
        name="products",
    )(sub, *projectors, *[field for chunk in fields for field in chunk])


def reordered(x, width, by):
    span = width * by
    column = lax.broadcasted_iota(jnp.int32, x.shape, 1)
    up, down = pltpu.roll(x, span, 1), pltpu.roll(x, x.shape[1] - span, 1)
    return jnp.where((column & span) == 0, down, up)


def gram_kernel(scales, groups, seen, own_row, group_ref, corr_ref, grid_ref, proj_ref, *refs):
    *sums, kept, sent = refs
    orbitals = grid_ref.shape[0]
    width = orbitals // groups
    bits = [1 << k for k in range(groups.bit_length() - 1)]
    projections = proj_ref[own_row : own_row + corr_ref.shape[0], :]
    for part, by in zip(sums, seen):
        columns = part[...]
        for bit in bits:
            if by & bit:
                columns = reordered(columns, width, bit)
        projections += columns
    highest = lax.Precision.HIGHEST
    weighted = jnp.dot(
        corr_ref[...], projections, precision=highest, preferred_element_type=jnp.float32
    )
    atom_part = lax.dot_general(
        projections, weighted, TN, precision=highest, preferred_element_type=jnp.float32
    )
    share = grid_ref[...] * scales[0] + atom_part * scales[1]
    for bit in bits:
        share = jnp.where((group_ref[0] & bit) != 0, reordered(share, width, bit), share)
    kept[...] = share[: orbitals // 2]
    sent[...] = share[orbitals // 2 :]


def gram_share(scales, groups, seen, own_row, group, corr, grid_part, proj, sums):
    half = jax.ShapeDtypeStruct((grid_part.shape[0] // 2, grid_part.shape[1]), jnp.float32)
    return pl.pallas_call(
        functools.partial(gram_kernel, scales, groups, seen, own_row),
        out_shape=[half, half],
        in_specs=[SMEM] + [VMEM] * (3 + len(sums)),
        out_specs=[VMEM] * 2,
        compiler_params=params(8),
        name="gram_share",
    )(group, corr, grid_part, proj, *sums)


def whole_columns(panel, potential, me, band):
    n_dom, n_band = lax.axis_size("dom"), lax.axis_size("band")
    orbitals, planes, rows, lanes = panel.shape
    cells = planes * rows
    flat = panel.reshape(orbitals * cells, lanes)
    levels = potential.reshape(cells, lanes)
    size = TOGETHER * cells
    n_chunks = orbitals // (n_dom * TOGETHER)
    own = []
    for m in range(n_dom):
        blocks = [
            lax.dynamic_slice_in_dim(flat, (c * n_dom + (me ^ m)) * size, size, 0)
            for c in range(n_chunks)
        ]
        blocks[0] = jnp.concatenate([blocks[0], levels], axis=0)
        own.append(blocks)
    near = swapped(jnp.concatenate(own[1], axis=0), "dom", n_dom, 1)
    arrived = [
        [own[0][c], near] + [swapped(own[m][c], "dom", n_dom, m) for m in range(2, n_dom)]
        for c in range(1)
    ]
    for c in range(1, n_chunks):
        far = [own[m][c] for m in range(2, n_dom)]
        near, far = lax.optimization_barrier((near, far))
        arrived.append(
            [own[0][c], near]
            + [swapped(b, "dom", n_dom, m) for m, b in enumerate(far, start=2)]
        )
    diagonal = None
    done = []
    for c, blocks in enumerate(arrived):
        starts = [0] * n_dom
        starts[1] = c * size + (cells if c else 0)
        filtered = filter_orbitals(me.reshape(1), diagonal, blocks, starts, planes, rows)
        if diagonal is None:
            diagonal = filtered[n_dom]
        done.append(filtered[:n_dom])
    return [
        [swapped(b, "dom", n_dom, m) if m else b for m, b in enumerate(blocks)] for blocks in done
    ]


def plane_by_plane(panel, potential):
    n_dom = lax.axis_size("dom")
    diagonal = (potential + (SHIFT - CENTER_LEVEL)) * (2.0 / HALF_WIDTH)

    def twice_operator(field):
        low, high = shifted(field[:, -1:], -1), shifted(field[:, :1], 1)
        extended = jnp.concatenate([low, field, high], axis=1)
        near = extended[:, 2:] + extended[:, :-2]
        near += jnp.roll(field, 1, axis=2) + jnp.roll(field, -1, axis=2)
        padded = jnp.pad(field, ((0, 0), (0, 0), (0, 0), (1, 1)))
        near += padded[..., 2:] + padded[..., :-2]
        return diagonal * field - near / HALF_WIDTH

    def one_step(_, carry):
        before, current = carry
        return current, twice_operator(current) - before

    start = (panel, 0.5 * twice_operator(panel))
    return lax.fori_loop(0, DEGREE - 1, one_step, start)[1]


def on_device(panel, potential, point_offsets, point_coefs, correlation):
    orbitals, planes, rows, lanes = panel.shape
    n_dom, n_band, n_sub = (lax.axis_size(axis) for axis in ("dom", "band", "sub"))
    groups = n_band * n_sub
    me, band, sub = (lax.axis_index(axis) for axis in ("dom", "band", "sub"))
    group = band * n_sub + sub

    cells = planes * rows
    share = cells // n_band
    channels = correlation.shape[1]
    own_atoms = point_offsets.shape[0] // groups
    own_corr = lax.dynamic_slice_in_dim(
        correlation, (sub * n_band + band) * own_atoms, own_atoms, 0
    )
    same_atom = jnp.eye(own_atoms, dtype=jnp.float32)
    corr_matrix = (same_atom[:, None, :, None] * own_corr[:, :, None, :]).reshape(
        own_atoms * channels, own_atoms * channels
    )

    def build(offsets):
        return build_projectors(
            n_band, n_sub, band.reshape(1), sub.reshape(1), offsets, point_coefs, share, lanes
        )

    filtered, parts = [], []
    if n_dom in (2, 4) and orbitals % (n_dom * TOGETHER) == 0 and planes * n_dom % 2 == 0:
        chunks = whole_columns(panel, potential, me, band)
        chunks[-1][0], point_offsets = lax.optimization_barrier((chunks[-1][0], point_offsets))
        projectors = build(point_offsets)
        chunks[0], projectors = lax.optimization_barrier((chunks[0], projectors))
        for pieces in chunks:
            orbital_first, *by_band = assemble(me.reshape(1), band.reshape(1), n_band, pieces)
            filtered.append(orbital_first)
            parts.append(by_band)
    else:
        projectors = build(point_offsets)
        filtered = [plane_by_plane(panel, potential)]
        cell_first = filtered[0].reshape(orbitals, cells, lanes).swapaxes(0, 1)
        parts = [
            [
                lax.dynamic_slice_in_dim(cell_first, (band ^ m) * share, share, 0)
                for m in range(n_band)
            ]
        ]
    filtered = jnp.concatenate(filtered, axis=0).reshape(panel.shape)
    fields = []
    for by_band in parts:
        chunk = []
        for m in range(n_band):
            here = swapped(by_band[m], "band", n_band, m) if m else by_band[0]
            chunk += [here] + [swapped(here, "sub", n_sub, k) for k in range(1, n_sub)]
        fields.append(chunk)

    grid_part, proj = products(n_sub, sub.reshape(1), projectors, fields)
    rows_atom = own_atoms * channels
    sums, seen = [], []
    for shell, by in ((1, 0), (0, 1), (2, -1)):
        for m in range(n_band):
            if by == 0 and m == 0:
                continue
            first = (shell * n_band + m) * rows_atom
            pairs = [
                (d * n_band + b, (d - by) % n_dom * n_band + (b ^ m))
                for d in range(n_dom)
                for b in range(n_band)
            ]
            seen.append(m * n_sub)
            sums.append(lax.ppermute(proj[first : first + rows_atom], ("dom", "band"), pairs))
    scale_point = 1.0 / (cells * lanes * n_dom)
    scale_atom = 1.0 / math.sqrt(point_offsets.shape[0] * n_dom)
    kept, sent = gram_share(
        (scale_point, scale_atom), groups, seen, n_band * rows_atom, group.reshape(1),
        corr_matrix, grid_part, proj, sums,
    )
    by = groups // 2
    while by:
        kept += swapped(sent, ("band", "sub"), groups, by)
        by //= 2
        if by:
            kept, sent = kept[: by * orbitals], kept[by * orbitals :]
    by = 1
    while by < n_dom:
        kept += swapped(kept, "dom", n_dom, by)
        by *= 2
    return filtered, kept


def solution(mesh):
    placed = (
        P(("slab", "band", "sub"), "dom", None, None),
        P(("slab", "dom"), None, None),
        P(("slab", "dom"), None, None),
        P(("slab", "dom"), None, None, None),
        P(("slab", "dom"), None, None),
    )
    return jax.shard_map(
        on_device,
        mesh=mesh,
        in_specs=placed,
        out_specs=(P(("slab", "band", "sub"), "dom", None, None), P(("slab", "band", "sub"), None)),
        check_vma=False,
    )
```

```python
import functools
import math

import jax
import jax.numpy as jnp
from jax import lax
from jax.experimental import pallas as pl
from jax.experimental.pallas import tpu as pltpu
from jax.sharding import PartitionSpec as P

DEGREE = 12

CENTER_LEVEL = 3.6
HALF_WIDTH = 3.4
SHIFT = 3.0

TOGETHER = 4
SUBLANES = 8
ME, BAND, SUB, GROUP = range(4)
MIB = 1024 * 1024

VMEM = pl.BlockSpec(memory_space=pltpu.VMEM)
SMEM = pl.BlockSpec(memory_space=pltpu.SMEM)
NT = (((1,), (1,)), ((), ()))
TN = (((0,), (0,)), ((), ()))


def params(mib):
    return pltpu.CompilerParams(vmem_limit_bytes=mib * MIB)


def split_bf16(x):
    high = x.astype(jnp.bfloat16)
    return high, (x - high.astype(jnp.float32)).astype(jnp.bfloat16)


def shifted(x, by):
    size = lax.axis_size("dom")
    return lax.ppermute(x, "dom", [(i, (i - by) % size) for i in range(size)])


def swapped(x, axes, size, by):
    return lax.ppermute(x, axes, [(i, i ^ by) for i in range(size)])


def filter_kernel(n_dom, planes, rows, starts, first, place, *refs):
    refs = list(refs)
    given = None if first else refs.pop(0)
    ins, outs = refs[:n_dom], refs[n_dom : 2 * n_dom]
    refs = refs[2 * n_dom :]
    diagonal = refs.pop(0) if first else given
    even, odd = refs
    half_planes = n_dom * planes // 2
    cells = planes * rows
    lanes = even.shape[3]
    scale = 1.0 / HALF_WIDTH
    mirrored = (place[ME] & 1) != 0
    plane_at = [jnp.where(mirrored, planes - 1 - i, i) for i in range(planes)]

    for x in range(half_planes):
        for half in range(2):
            m, i = divmod(half * half_planes + x, planes)
            part = slice(half * TOGETHER, (half + 1) * TOGETHER)
            base = starts[m] + plane_at[i] * rows
            for y in range(rows):
                even[x, y, part] = ins[m][pl.ds(base + y, TOGETHER, stride=cells), :]
                if first:
                    level = ins[m][pl.ds(base + (TOGETHER * cells + y), 1), :]
                    diagonal[x, y, part] = jnp.broadcast_to(
                        (level + (SHIFT - CENTER_LEVEL)) * (2.0 * scale), (TOGETHER, lanes)
                    )

    block = SUBLANES
    lane = lax.broadcasted_iota(jnp.int32, (block, SUBLANES, lanes), 2)
    at_start, at_end = lane == 0, lane == lanes - 1

    def twice_operator(source, x, y):
        here = slice(y, y + block)
        centre = source[x, here]
        if x == 0:
            near = pltpu.roll(source[half_planes - 1, here], TOGETHER, 1) + source[x + 1, here]
        elif x == half_planes - 1:
            near = pltpu.roll(source[0, here], TOGETHER, 1) + source[x - 1, here]
        else:
            near = source[x - 1, here] + source[x + 1, here]
        before = (y - 1) % rows
        after = (y + block) % rows
        near += jnp.concatenate([source[x, before : before + 1], centre[:-1]], axis=0)
        near += jnp.concatenate([centre[1:], source[x, after : after + 1]], axis=0)
        low = pltpu.roll(centre, 1, 2)
        high = pltpu.roll(centre, lanes - 1, 2)
        near += jnp.where(at_start, high, jnp.where(at_end, low, low + high))
        return diagonal[x, here] * centre - scale * near

    places = [(x, y) for x in range(half_planes) for y in range(0, rows, block)]

    def next_field(source, target):
        for x, y in places:
            target[x, y : y + block] = twice_operator(source, x, y) - target[x, y : y + block]

    for x, y in places:
        odd[x, y : y + block] = 0.5 * twice_operator(even, x, y)
    next_field(odd, even)

    def two_steps(_, carry):
        next_field(even, odd)
        next_field(odd, even)
        return carry

    lax.fori_loop(0, DEGREE // 2 - 1, two_steps, 0)
    for m in range(n_dom):
        for i in range(planes):
            half, x = divmod(m * planes + i, half_planes)
            part = slice(half * TOGETHER, (half + 1) * TOGETHER)
            for y in range(rows):
                here = slice(y * TOGETHER, (y + 1) * TOGETHER)
                outs[m][plane_at[i], here, :] = even[x, y, part]


def filter_orbitals(place, diagonal, blocks, starts, planes, rows):
    n_dom = len(blocks)
    first = diagonal is None
    lanes = blocks[0].shape[1]
    field = (n_dom * planes // 2, rows, SUBLANES, lanes)
    out = jax.ShapeDtypeStruct((planes, rows * TOGETHER, lanes), jnp.float32)
    extra = [jax.ShapeDtypeStruct(field, jnp.float32)] if first else []
    given = [] if first else [diagonal]
    size = n_dom * planes * rows * TOGETHER * lanes
    return pl.pallas_call(
        functools.partial(filter_kernel, n_dom, planes, rows, starts, first),
        out_shape=[out] * n_dom + extra,
        in_specs=[SMEM] + [VMEM] * (n_dom + len(given)),
        out_specs=[VMEM] * (n_dom + len(extra)),
        scratch_shapes=[pltpu.VMEM(field, jnp.float32)] * 2,
        compiler_params=params(8),
        cost_estimate=pl.CostEstimate(
            flops=12 * DEGREE * size, bytes_accessed=8 * size, transcendentals=0
        ),
        name="chebyshev",
    )(place, *given, *blocks)


def assemble_kernel(n_dom, n_band, place, *refs):
    pieces, orbital_first, parts = refs[:n_dom], refs[n_dom], refs[n_dom + 1 :]
    cells = orbital_first.shape[1]
    share = cells // n_band
    me = place[ME]
    for m, piece in enumerate(pieces):
        start = (me ^ m) * TOGETHER
        for t in range(TOGETHER):
            orbital_first[start + t] = piece[pl.ds(t, cells, stride=TOGETHER), :]
    per_load = SUBLANES // TOGETHER
    together = SUBLANES // TOGETHER
    for p, part in enumerate(parts):
        base = pl.multiple_of((place[BAND] ^ p) * (share * TOGETHER), SUBLANES)
        for first in range(0, share, per_load):
            loaded = [
                piece[pl.ds(base + first * TOGETHER, SUBLANES), :] for piece in pieces
            ]
            for k in range(per_load):
                here = slice(k * TOGETHER, (k + 1) * TOGETHER)
                for q in range(n_dom // together):
                    tile = jnp.concatenate(
                        [loaded[q * together + i][here] for i in range(together)], axis=0
                    )
                    tile = jnp.where((me & 1) != 0, pltpu.roll(tile, TOGETHER, 0), tile)
                    row = pl.multiple_of((q ^ (me // together)) * SUBLANES, SUBLANES)
                    part[first + k, pl.ds(row, SUBLANES), :] = tile


def assemble(place, n_band, pieces):
    n_dom = len(pieces)
    planes, rows, lanes = pieces[0].shape
    cells, orbitals = planes * rows // TOGETHER, n_dom * TOGETHER
    part = jax.ShapeDtypeStruct((cells // n_band, orbitals, lanes), jnp.float32)
    return pl.pallas_call(
        functools.partial(assemble_kernel, n_dom, n_band),
        out_shape=[jax.ShapeDtypeStruct((orbitals, cells, lanes), jnp.float32)] + [part] * n_band,
        in_specs=[SMEM] + [VMEM] * n_dom,
        out_specs=[VMEM] * (1 + n_band),
        compiler_params=params(8),
        name="assemble",
    )(place, *[piece.reshape(planes * rows, lanes) for piece in pieces])


def projector_kernel(n_band, n_sub, place, offsets_ref, coefs_ref, high_out, low_out):
    atoms, shells, channels, spread = coefs_ref.shape
    own = atoms // (n_band * n_sub)
    lanes = spread
    cells = high_out.shape[1] // lanes
    pairs = own // 2
    row_index = lax.broadcasted_iota(jnp.int32, (cells, channels, spread), 0)
    row_index += place[BAND] * cells
    lane_index = lax.broadcasted_iota(jnp.int32, (lanes, spread), 0)

    def two_atoms(step, carry):
        shell = step // (n_band * pairs)
        band = place[BAND] ^ ((step // pairs) % n_band)
        first_atom = (place[SUB] * n_band + band) * own + 2 * (step % pairs)
        dense = []
        for i in range(2):
            offsets = offsets_ref[shell, pl.ds(first_atom + i, 1), :]
            coefs = coefs_ref[first_atom + i, shell]
            at_row = row_index == (offsets // lanes)[None]
            at_row &= (offsets >= 0)[None]
            left = [
                jnp.where(at_row, part.astype(jnp.float32)[None], 0.0)
                .reshape(cells * channels, spread)
                .astype(jnp.bfloat16)
                for part in split_bf16(coefs)
            ]
            at_lane = jnp.where(lane_index == (offsets & (lanes - 1)), 1.0, 0.0)
            at_lane = at_lane.astype(jnp.bfloat16)
            values = lax.dot_general(
                jnp.concatenate(left, axis=1),
                jnp.concatenate([at_lane, at_lane], axis=1),
                NT,
                preferred_element_type=jnp.float32,
            )
            dense.append(values.reshape(cells, channels, lanes))
        high, low = split_bf16(jnp.concatenate(dense, axis=1))
        rows = pl.ds(pl.multiple_of(step * 2 * channels, 2 * channels), 2 * channels)
        for cell in range(cells):
            high_out[rows, cell * lanes : (cell + 1) * lanes] = high[cell]
            low_out[rows, cell * lanes : (cell + 1) * lanes] = low[cell]
        return carry

    lax.fori_loop(0, shells * n_band * pairs, two_atoms, 0)


def build_projectors(n_band, n_sub, place, offsets, coefs, cells, lanes):
    atoms, shells, channels, spread = coefs.shape
    rows = atoms // n_sub * shells * channels
    shape = jax.ShapeDtypeStruct((rows, cells * lanes), jnp.bfloat16)
    return pl.pallas_call(
        functools.partial(projector_kernel, n_band, n_sub),
        out_shape=[shape, shape],
        in_specs=[SMEM, VMEM, VMEM],
        out_specs=[VMEM, VMEM],
        compiler_params=params(8),
        cost_estimate=pl.CostEstimate(
            flops=4 * rows * cells * lanes * spread,
            bytes_accessed=8 * rows * cells * lanes,
            transcendentals=0,
        ),
        name="projectors",
    )(place, offsets.swapaxes(0, 1), coefs)


def product_kernel(n_chunks, n_sub, n_blocks, place, w_high, w_low, *refs):
    refs, proj_out = refs[:-1], refs[-1]
    fields, grid_out, outs = refs[: -n_blocks - 1], refs[-n_blocks - 1], refs[-n_blocks:]
    orbitals = grid_out.shape[0]
    cells, _, lanes = fields[0].shape
    n_groups = len(fields) // n_chunks
    block = 12

    def parts(start):
        highs, lows = [], []
        for g in range(n_groups):
            for c in range(n_chunks):
                high, low = split_bf16(fields[c * n_groups + g][pl.ds(start, block)])
                highs.append(jnp.concatenate([high[k] for k in range(block)], axis=1))
                lows.append(jnp.concatenate([low[k] for k in range(block)], axis=1))
        return jnp.concatenate(highs, axis=0), jnp.concatenate(lows, axis=0)

    def product(left_high, left_low, high, low):
        right = jnp.concatenate([high, low], axis=0)
        wide = lax.dot_general(left_high, right, NT, preferred_element_type=jnp.float32)
        narrow = lax.dot_general(left_low, high, NT, preferred_element_type=jnp.float32)
        return wide[:, :orbitals] + wide[:, orbitals:] + narrow

    def grid_block(step, carry):
        high, low = parts(place[SUB] * (cells // n_sub) + step * block)
        grid_out[...] += product(high, low, high, low)
        return carry

    def proj_block(step, carry):
        high, low = parts(step * block)
        depth = block * lanes
        here = pl.ds(pl.multiple_of(step * depth, depth), depth)
        proj_out[...] += product(w_high[:, here], w_low[:, here], high, low)
        return carry

    grid_out[...] = jnp.zeros_like(grid_out)
    proj_out[...] = jnp.zeros_like(proj_out)
    lax.fori_loop(0, cells // (n_sub * block), grid_block, 0)
    lax.fori_loop(0, cells // block, proj_block, 0)
    rows = outs[0].shape[0]
    for k, out in enumerate(outs):
        out[...] = proj_out[k * rows : (k + 1) * rows, :]


def products(n_sub, n_blocks, place, projectors, fields):
    rows = projectors[0].shape[0]
    n_chunks, n_groups = len(fields), len(fields[0])
    orbitals = n_chunks * n_groups * fields[0][0].shape[1]
    block = jax.ShapeDtypeStruct((rows // n_blocks, orbitals), jnp.float32)
    return pl.pallas_call(
        functools.partial(product_kernel, n_chunks, n_sub, n_blocks),
        out_shape=[jax.ShapeDtypeStruct((orbitals, orbitals), jnp.float32)] + [block] * n_blocks,
        in_specs=[SMEM] + [VMEM] * (2 + n_chunks * n_groups),
        out_specs=[VMEM] * (1 + n_blocks),
        scratch_shapes=[pltpu.VMEM((rows, orbitals), jnp.float32)],
        compiler_params=params(8),
        name="products",
    )(place, *projectors, *[field for chunk in fields for field in chunk])


def reordered(x, width, by):
    span = width * by
    column = lax.broadcasted_iota(jnp.int32, x.shape, 1)
    up, down = pltpu.roll(x, span, 1), pltpu.roll(x, x.shape[1] - span, 1)
    return jnp.where((column & span) == 0, down, up)


def gram_kernel(scales, groups, seen, place, corr_ref, grid_ref, proj_ref, *refs):
    sums, outs = refs[: len(seen)], refs[len(seen) :]
    orbitals = grid_ref.shape[0]
    width = orbitals // groups
    bits = [1 << k for k in range(groups.bit_length() - 1)]
    projections = proj_ref[...]
    for part, by in zip(sums, seen):
        columns = part[...]
        for bit in bits:
            if by & bit:
                columns = reordered(columns, width, bit)
        projections += columns
    highest = lax.Precision.HIGHEST
    weighted = jnp.dot(
        corr_ref[...], projections, precision=highest, preferred_element_type=jnp.float32
    )
    atom_part = lax.dot_general(
        projections, weighted, TN, precision=highest, preferred_element_type=jnp.float32
    )
    share = grid_ref[...] * scales[0] + atom_part * scales[1]
    for bit in bits:
        share = jnp.where((place[GROUP] & bit) != 0, reordered(share, width, bit), share)
    for k, out in enumerate(outs):
        out[...] = share[k * width : (k + 1) * width]


def gram_share(scales, groups, seen, place, corr, grid_part, proj, sums):
    rows = jax.ShapeDtypeStruct((grid_part.shape[0] // groups, grid_part.shape[1]), jnp.float32)
    return pl.pallas_call(
        functools.partial(gram_kernel, scales, groups, seen),
        out_shape=[rows] * groups,
        in_specs=[SMEM] + [VMEM] * (3 + len(sums)),
        out_specs=[VMEM] * groups,
        compiler_params=params(8),
        name="gram_share",
    )(place, corr, grid_part, proj, *sums)


def added(terms):
    while len(terms) > 1:
        terms = [a + b for a, b in zip(terms[::2], terms[1::2])]
    return terms[0]


def whole_columns(panel, potential, place, me):
    n_dom = lax.axis_size("dom")
    orbitals, planes, rows, lanes = panel.shape
    cells = planes * rows
    flat = panel.reshape(orbitals * cells, lanes)
    levels = potential.reshape(cells, lanes)
    size = TOGETHER * cells
    n_chunks = orbitals // (n_dom * TOGETHER)
    own = []
    for m in range(n_dom):
        blocks = [
            lax.dynamic_slice_in_dim(flat, (c * n_dom + (me ^ m)) * size, size, 0)
            for c in range(n_chunks)
        ]
        blocks[0] = jnp.concatenate([blocks[0], levels], axis=0)
        own.append(blocks)
    near = swapped(jnp.concatenate(own[1], axis=0), "dom", n_dom, 1)
    arrived = [
        [own[0][c], near] + [swapped(own[m][c], "dom", n_dom, m) for m in range(2, n_dom)]
        for c in range(1)
    ]
    for c in range(1, n_chunks):
        far = [own[m][c] for m in range(2, n_dom)]
        near, far = lax.optimization_barrier((near, far))
        arrived.append(
            [own[0][c], near]
            + [swapped(b, "dom", n_dom, m) for m, b in enumerate(far, start=2)]
        )
    diagonal = None
    done = []
    for c, blocks in enumerate(arrived):
        starts = [0] * n_dom
        starts[1] = c * size + (cells if c else 0)
        filtered = filter_orbitals(place, diagonal, blocks, starts, planes, rows)
        if diagonal is None:
            diagonal = filtered[n_dom]
        done.append(filtered[:n_dom])
    return [
        [swapped(b, "dom", n_dom, m) if m else b for m, b in enumerate(blocks)] for blocks in done
    ]


def plane_by_plane(panel, potential):
    n_dom = lax.axis_size("dom")
    diagonal = (potential + (SHIFT - CENTER_LEVEL)) * (2.0 / HALF_WIDTH)

    def twice_operator(field):
        low, high = shifted(field[:, -1:], -1), shifted(field[:, :1], 1)
        extended = jnp.concatenate([low, field, high], axis=1)
        near = extended[:, 2:] + extended[:, :-2]
        near += jnp.roll(field, 1, axis=2) + jnp.roll(field, -1, axis=2)
        padded = jnp.pad(field, ((0, 0), (0, 0), (0, 0), (1, 1)))
        near += padded[..., 2:] + padded[..., :-2]
        return diagonal * field - near / HALF_WIDTH

    def one_step(_, carry):
        before, current = carry
        return current, twice_operator(current) - before

    start = (panel, 0.5 * twice_operator(panel))
    return lax.fori_loop(0, DEGREE - 1, one_step, start)[1]


def on_device(panel, potential, point_offsets, point_coefs, correlation):
    orbitals, planes, rows, lanes = panel.shape
    n_dom, n_band, n_sub = (lax.axis_size(axis) for axis in ("dom", "band", "sub"))
    groups = n_band * n_sub
    me, band, sub = (lax.axis_index(axis) for axis in ("dom", "band", "sub"))
    place = jnp.stack([me, band, sub, band * n_sub + sub]).astype(jnp.int32)

    cells = planes * rows
    share = cells // n_band
    channels = correlation.shape[1]
    own_atoms = point_offsets.shape[0] // groups
    own_corr = lax.dynamic_slice_in_dim(
        correlation, (sub * n_band + band) * own_atoms, own_atoms, 0
    )
    same_atom = jnp.eye(own_atoms, dtype=jnp.float32)
    corr_matrix = (same_atom[:, None, :, None] * own_corr[:, :, None, :]).reshape(
        own_atoms * channels, own_atoms * channels
    )

    place, corr_matrix = lax.optimization_barrier((place, corr_matrix))

    def build(offsets):
        return build_projectors(n_band, n_sub, place, offsets, point_coefs, share, lanes)

    filtered, parts = [], []
    if n_dom in (2, 4) and orbitals % (n_dom * TOGETHER) == 0 and planes * n_dom % 2 == 0:
        chunks = whole_columns(panel, potential, place, me)
        chunks[-1][0], point_offsets = lax.optimization_barrier((chunks[-1][0], point_offsets))
        projectors = build(point_offsets)
        chunks[0], projectors = lax.optimization_barrier((chunks[0], projectors))
        for pieces in chunks:
            orbital_first, *by_band = assemble(place, n_band, pieces)
            filtered.append(orbital_first)
            parts.append(by_band)
    else:
        projectors = build(point_offsets)
        filtered = [plane_by_plane(panel, potential)]
        cell_first = filtered[0].reshape(orbitals, cells, lanes).swapaxes(0, 1)
        parts = [
            [
                lax.dynamic_slice_in_dim(cell_first, (band ^ m) * share, share, 0)
                for m in range(n_band)
            ]
        ]
    filtered = jnp.concatenate(filtered, axis=0).reshape(panel.shape)
    fields = []
    for by_band in parts:
        chunk = []
        for m in range(n_band):
            here = swapped(by_band[m], "band", n_band, m) if m else by_band[0]
            chunk += [here] + [swapped(here, "sub", n_sub, k) for k in range(1, n_sub)]
        fields.append(chunk)

    grid_part, *proj = products(n_sub, 3 * n_band, place, projectors, fields)
    sums, seen = [], []
    for shell, by in ((1, 0), (0, 1), (2, -1)):
        for m in range(n_band):
            if by == 0 and m == 0:
                continue
            pairs = [
                (d * n_band + b, (d - by) % n_dom * n_band + (b ^ m))
                for d in range(n_dom)
                for b in range(n_band)
            ]
            seen.append(m * n_sub)
            sums.append(lax.ppermute(proj[shell * n_band + m], ("dom", "band"), pairs))
    scale_point = 1.0 / (cells * lanes * n_dom)
    scale_atom = 1.0 / math.sqrt(own_atoms * groups * n_dom)
    shares = gram_share(
        (scale_point, scale_atom), groups, seen, place, corr_matrix, grid_part, proj[n_band], sums
    )
    gram_rows = added(
        [swapped(x, ("band", "sub"), groups, m) if m else x for m, x in enumerate(shares)]
    )
    if n_dom <= 4:
        gram_rows = added(
            [swapped(gram_rows, "dom", n_dom, m) if m else gram_rows for m in range(n_dom)]
        )
    else:
        by = 1
        while by < n_dom:
            gram_rows += swapped(gram_rows, "dom", n_dom, by)
            by *= 2
    return filtered, gram_rows


def solution(mesh):
    placed = (
        P(("slab", "band", "sub"), "dom", None, None),
        P(("slab", "dom"), None, None),
        P(("slab", "dom"), None, None),
        P(("slab", "dom"), None, None, None),
        P(("slab", "dom"), None, None),
    )
    return jax.shard_map(
        on_device,
        mesh=mesh,
        in_specs=placed,
        out_specs=(P(("slab", "band", "sub"), "dom", None, None), P(("slab", "band", "sub"), None)),
        check_vma=False,
    )
```

```python
import functools
import math

import jax
import jax.numpy as jnp
from jax import lax
from jax.experimental import pallas as pl
from jax.experimental.pallas import tpu as pltpu
from jax.sharding import PartitionSpec as P

DEGREE = 12

CENTER_LEVEL = 3.6
HALF_WIDTH = 3.4
SHIFT = 3.0

TOGETHER = 4
SUBLANES = 8
ME, BAND, SUB, GROUP = range(4)
MIB = 1024 * 1024

VMEM = pl.BlockSpec(memory_space=pltpu.VMEM)
SMEM = pl.BlockSpec(memory_space=pltpu.SMEM)
NT = (((1,), (1,)), ((), ()))
TN = (((0,), (0,)), ((), ()))


def params(mib):
    return pltpu.CompilerParams(vmem_limit_bytes=mib * MIB)


def split_bf16(x):
    high = x.astype(jnp.bfloat16)
    return high, (x - high.astype(jnp.float32)).astype(jnp.bfloat16)


def shifted(x, by):
    size = lax.axis_size("dom")
    return lax.ppermute(x, "dom", [(i, (i - by) % size) for i in range(size)])


def swapped(x, axes, size, by):
    return lax.ppermute(x, axes, [(i, i ^ by) for i in range(size)])


def filter_kernel(n_dom, planes, rows, starts, first, place, *refs):
    refs = list(refs)
    given = None if first else refs.pop(0)
    ins, outs = refs[:n_dom], refs[n_dom : 2 * n_dom]
    refs = refs[2 * n_dom :]
    diagonal = refs.pop(0) if first else given
    even, odd = refs
    half_planes = n_dom * planes // 2
    cells = planes * rows
    lanes = even.shape[3]
    scale = 1.0 / HALF_WIDTH
    mirrored = (place[ME] & 1) != 0
    plane_at = [jnp.where(mirrored, planes - 1 - i, i) for i in range(planes)]

    for x in range(half_planes):
        for half in range(2):
            m, i = divmod(half * half_planes + x, planes)
            part = slice(half * TOGETHER, (half + 1) * TOGETHER)
            base = starts[m] + plane_at[i] * rows
            for y in range(rows):
                even[x, y, part] = ins[m][pl.ds(base + y, TOGETHER, stride=cells), :]
                if first:
                    level = ins[m][pl.ds(base + (TOGETHER * cells + y), 1), :]
                    diagonal[x, y, part] = jnp.broadcast_to(
                        (level + (SHIFT - CENTER_LEVEL)) * (2.0 * scale), (TOGETHER, lanes)
                    )

    block = SUBLANES
    lane = lax.broadcasted_iota(jnp.int32, (block, SUBLANES, lanes), 2)
    at_start, at_end = lane == 0, lane == lanes - 1

    def twice_operator(source, x, y):
        here = slice(y, y + block)
        centre = source[x, here]
        if x == 0:
            near = pltpu.roll(source[half_planes - 1, here], TOGETHER, 1) + source[x + 1, here]
        elif x == half_planes - 1:
            near = pltpu.roll(source[0, here], TOGETHER, 1) + source[x - 1, here]
        else:
            near = source[x - 1, here] + source[x + 1, here]
        before = (y - 1) % rows
        after = (y + block) % rows
        near += jnp.concatenate([source[x, before : before + 1], centre[:-1]], axis=0)
        near += jnp.concatenate([centre[1:], source[x, after : after + 1]], axis=0)
        low = pltpu.roll(centre, 1, 2)
        high = pltpu.roll(centre, lanes - 1, 2)
        near += jnp.where(at_start, high, jnp.where(at_end, low, low + high))
        return diagonal[x, here] * centre - scale * near

    places = [(x, y) for x in range(half_planes) for y in range(0, rows, block)]

    def next_field(source, target):
        for x, y in places:
            target[x, y : y + block] = twice_operator(source, x, y) - target[x, y : y + block]

    for x, y in places:
        odd[x, y : y + block] = 0.5 * twice_operator(even, x, y)
    next_field(odd, even)

    def two_steps(_, carry):
        next_field(even, odd)
        next_field(odd, even)
        return carry

    lax.fori_loop(0, DEGREE // 2 - 1, two_steps, 0)
    for m in range(n_dom):
        for i in range(planes):
            half, x = divmod(m * planes + i, half_planes)
            part = slice(half * TOGETHER, (half + 1) * TOGETHER)
            for y in range(rows):
                here = slice(y * TOGETHER, (y + 1) * TOGETHER)
                outs[m][plane_at[i], here, :] = even[x, y, part]


def filter_orbitals(place, diagonal, blocks, starts, planes, rows):
    n_dom = len(blocks)
    first = diagonal is None
    lanes = blocks[0].shape[1]
    field = (n_dom * planes // 2, rows, SUBLANES, lanes)
    out = jax.ShapeDtypeStruct((planes, rows * TOGETHER, lanes), jnp.float32)
    extra = [jax.ShapeDtypeStruct(field, jnp.float32)] if first else []
    given = [] if first else [diagonal]
    size = n_dom * planes * rows * TOGETHER * lanes
    return pl.pallas_call(
        functools.partial(filter_kernel, n_dom, planes, rows, starts, first),
        out_shape=[out] * n_dom + extra,
        in_specs=[SMEM] + [VMEM] * (n_dom + len(given)),
        out_specs=[VMEM] * (n_dom + len(extra)),
        scratch_shapes=[pltpu.VMEM(field, jnp.float32)] * 2,
        compiler_params=params(8),
        cost_estimate=pl.CostEstimate(
            flops=12 * DEGREE * size, bytes_accessed=8 * size, transcendentals=0
        ),
        name="chebyshev",
    )(place, *given, *blocks)


def cell_first_kernel(n_band, place, *refs):
    pieces, parts = refs[:-n_band], refs[-n_band:]
    share = parts[0].shape[0]
    me = place[ME]
    together = SUBLANES // TOGETHER
    tiles = len(pieces) // together
    for p, part in enumerate(parts):
        base = pl.multiple_of((place[BAND] ^ p) * (share * TOGETHER), SUBLANES)
        for first in range(0, share, together):
            loaded = [piece[pl.ds(base + first * TOGETHER, SUBLANES), :] for piece in pieces]
            for k in range(together):
                here = slice(k * TOGETHER, (k + 1) * TOGETHER)
                for q in range(tiles):
                    tile = jnp.concatenate(
                        [loaded[q * together + i][here] for i in range(together)], axis=0
                    )
                    tile = jnp.where((me & 1) != 0, pltpu.roll(tile, TOGETHER, 0), tile)
                    if tiles == 1:
                        part[first + k] = tile
                    else:
                        row = pl.multiple_of((q ^ (me // together)) * SUBLANES, SUBLANES)
                        part[first + k, pl.ds(row, SUBLANES), :] = tile


def cell_first(place, n_band, pieces):
    rows, lanes = pieces[0].shape
    orbitals = len(pieces) * TOGETHER
    part = jax.ShapeDtypeStruct((rows // (TOGETHER * n_band), orbitals, lanes), jnp.float32)
    return pl.pallas_call(
        functools.partial(cell_first_kernel, n_band),
        out_shape=[part] * n_band,
        in_specs=[SMEM] + [VMEM] * len(pieces),
        out_specs=[VMEM] * n_band,
        compiler_params=params(8),
        name="cell_first",
    )(place, *pieces)


def orbital_first_kernel(n_dom, place, *refs):
    *pieces, out = refs
    cells = out.shape[1]
    for k, piece in enumerate(pieces):
        chunk, m = divmod(k, n_dom)
        start = (chunk * n_dom + (place[ME] ^ m)) * TOGETHER
        for t in range(TOGETHER):
            out[start + t] = piece[pl.ds(t, cells, stride=TOGETHER), :]


def orbital_first(place, n_dom, pieces):
    rows, lanes = pieces[0].shape
    shape = (len(pieces) * TOGETHER, rows // TOGETHER, lanes)
    return pl.pallas_call(
        functools.partial(orbital_first_kernel, n_dom),
        out_shape=jax.ShapeDtypeStruct(shape, jnp.float32),
        in_specs=[SMEM] + [VMEM] * len(pieces),
        out_specs=VMEM,
        compiler_params=params(8),
        name="orbital_first",
    )(place, *pieces)


def projector_kernel(n_band, n_sub, place, offsets_ref, coefs_ref, high_out, low_out):
    atoms, shells, channels, spread = coefs_ref.shape
    own = atoms // (n_band * n_sub)
    lanes = spread
    cells = high_out.shape[1] // lanes
    pairs = own // 2
    row_index = lax.broadcasted_iota(jnp.int32, (cells, channels, spread), 0)
    row_index += place[BAND] * cells
    lane_index = lax.broadcasted_iota(jnp.int32, (lanes, spread), 0)

    def two_atoms(step, carry):
        shell = lax.rem(2 * (step // (n_band * pairs)), shells)
        band = place[BAND] ^ ((step // pairs) % n_band)
        first_atom = (place[SUB] * n_band + band) * own + 2 * (step % pairs)
        dense = []
        for i in range(2):
            offsets = offsets_ref[shell, pl.ds(first_atom + i, 1), :]
            coefs = coefs_ref[first_atom + i, shell]
            at_row = row_index == (offsets // lanes)[None]
            at_row &= (offsets >= 0)[None]
            left = [
                jnp.where(at_row, part.astype(jnp.float32)[None], 0.0)
                .reshape(cells * channels, spread)
                .astype(jnp.bfloat16)
                for part in split_bf16(coefs)
            ]
            at_lane = jnp.where(lane_index == (offsets & (lanes - 1)), 1.0, 0.0)
            at_lane = at_lane.astype(jnp.bfloat16)
            values = lax.dot_general(
                jnp.concatenate(left, axis=1),
                jnp.concatenate([at_lane, at_lane], axis=1),
                NT,
                preferred_element_type=jnp.float32,
            )
            dense.append(values.reshape(cells, channels, lanes))
        high, low = split_bf16(jnp.concatenate(dense, axis=1))
        rows = pl.ds(pl.multiple_of(step * 2 * channels, 2 * channels), 2 * channels)
        for cell in range(cells):
            high_out[rows, cell * lanes : (cell + 1) * lanes] = high[cell]
            low_out[rows, cell * lanes : (cell + 1) * lanes] = low[cell]
        return carry

    lax.fori_loop(0, shells * n_band * pairs, two_atoms, 0)


def build_projectors(n_band, n_sub, place, offsets, coefs, cells, lanes):
    atoms, shells, channels, spread = coefs.shape
    rows = atoms // n_sub * shells * channels
    shape = jax.ShapeDtypeStruct((rows, cells * lanes), jnp.bfloat16)
    return pl.pallas_call(
        functools.partial(projector_kernel, n_band, n_sub),
        out_shape=[shape, shape],
        in_specs=[SMEM, VMEM, VMEM],
        out_specs=[VMEM, VMEM],
        compiler_params=params(8),
        cost_estimate=pl.CostEstimate(
            flops=4 * rows * cells * lanes * spread,
            bytes_accessed=8 * rows * cells * lanes,
            transcendentals=0,
        ),
        name="projectors",
    )(place, offsets.swapaxes(0, 1), coefs)


def product_kernel(spots, n_sub, first_row, n_blocks, with_grid, place, w_high, w_low, *refs):
    refs, proj_out = refs[:-1], refs[-1]
    n_outs = n_blocks + (1 if with_grid else 0)
    arrays, outs = refs[:-n_outs], list(refs[-n_outs:])
    rows, orbitals = proj_out.shape
    cells, _, lanes = arrays[0].shape
    block = 12

    def parts(start):
        highs, lows = [], []
        for at, first, width in spots:
            high, low = split_bf16(arrays[at][pl.ds(start, block), first : first + width])
            highs.append(jnp.concatenate([high[k] for k in range(block)], axis=1))
            lows.append(jnp.concatenate([low[k] for k in range(block)], axis=1))
        return jnp.concatenate(highs, axis=0), jnp.concatenate(lows, axis=0)

    def product(left_high, left_low, high, low):
        right = jnp.concatenate([high, low], axis=0)
        wide = lax.dot_general(left_high, right, NT, preferred_element_type=jnp.float32)
        narrow = lax.dot_general(left_low, high, NT, preferred_element_type=jnp.float32)
        return wide[:, :orbitals] + wide[:, orbitals:] + narrow

    if with_grid:
        grid_out = outs.pop(0)
        grid_out[...] = jnp.zeros_like(grid_out)

        def grid_block(step, carry):
            high, low = parts(place[SUB] * (cells // n_sub) + step * block)
            grid_out[...] += product(high, low, high, low)
            return carry

        lax.fori_loop(0, cells // (n_sub * block), grid_block, 0)

    def proj_block(step, carry):
        high, low = parts(step * block)
        depth = block * lanes
        here = pl.ds(pl.multiple_of(step * depth, depth), depth)
        some = slice(first_row, first_row + rows)
        proj_out[...] += product(w_high[some, here], w_low[some, here], high, low)
        return carry

    proj_out[...] = jnp.zeros_like(proj_out)
    lax.fori_loop(0, cells // block, proj_block, 0)
    for k, out in enumerate(outs):
        out[...] = proj_out[k * (rows // n_blocks) : (k + 1) * (rows // n_blocks), :]


def products(n_sub, first_row, rows, n_blocks, with_grid, place, projectors, arrays, spots):
    orbitals = sum(width for _, _, width in spots)
    grid = [jax.ShapeDtypeStruct((orbitals, orbitals), jnp.float32)] if with_grid else []
    block = jax.ShapeDtypeStruct((rows // n_blocks, orbitals), jnp.float32)
    flops = 12 * rows * orbitals * projectors[0].shape[1]
    return pl.pallas_call(
        functools.partial(product_kernel, spots, n_sub, first_row, n_blocks, with_grid),
        out_shape=grid + [block] * n_blocks,
        in_specs=[SMEM] + [VMEM] * (2 + len(arrays)),
        out_specs=[VMEM] * (len(grid) + n_blocks),
        scratch_shapes=[pltpu.VMEM((rows, orbitals), jnp.float32)],
        compiler_params=params(8),
        cost_estimate=pl.CostEstimate(
            flops=flops, bytes_accessed=4 * rows * projectors[0].shape[1], transcendentals=0
        ),
        name="products",
    )(place, *projectors, *arrays)


def reordered(x, width, by):
    span = width * by
    column = lax.broadcasted_iota(jnp.int32, x.shape, 1)
    up, down = pltpu.roll(x, span, 1), pltpu.roll(x, x.shape[1] - span, 1)
    return jnp.where((column & span) == 0, down, up)


def gram_kernel(scales, groups, seen, place, corr_ref, grid_ref, proj_ref, *refs):
    sums, outs = refs[: len(seen)], refs[len(seen) :]
    orbitals = grid_ref.shape[0]
    width = orbitals // groups
    bits = [1 << k for k in range(groups.bit_length() - 1)]
    projections = proj_ref[...]
    for part, by in zip(sums, seen):
        columns = part[...]
        for bit in bits:
            if by & bit:
                columns = reordered(columns, width, bit)
        projections += columns
    highest = lax.Precision.HIGHEST
    weighted = jnp.dot(
        corr_ref[...], projections, precision=highest, preferred_element_type=jnp.float32
    )
    atom_part = lax.dot_general(
        projections, weighted, TN, precision=highest, preferred_element_type=jnp.float32
    )
    share = grid_ref[...] * scales[0] + atom_part * scales[1]
    for bit in bits:
        share = jnp.where((place[GROUP] & bit) != 0, reordered(share, width, bit), share)
    for k, out in enumerate(outs):
        out[...] = share[k * width : (k + 1) * width]


def gram_share(scales, groups, seen, place, corr, grid_part, proj, sums):
    rows = jax.ShapeDtypeStruct((grid_part.shape[0] // groups, grid_part.shape[1]), jnp.float32)
    return pl.pallas_call(
        functools.partial(gram_kernel, scales, groups, seen),
        out_shape=[rows] * groups,
        in_specs=[SMEM] + [VMEM] * (3 + len(sums)),
        out_specs=[VMEM] * groups,
        compiler_params=params(8),
        name="gram_share",
    )(place, corr, grid_part, proj, *sums)


def added(terms):
    while len(terms) > 1:
        terms = [a + b for a, b in zip(terms[::2], terms[1::2])]
    return terms[0]


def whole_columns(panel, potential, place, me):
    n_dom = lax.axis_size("dom")
    orbitals, planes, rows, lanes = panel.shape
    cells = planes * rows
    flat = panel.reshape(orbitals * cells, lanes)
    levels = potential.reshape(cells, lanes)
    size = TOGETHER * cells
    n_chunks = orbitals // (n_dom * TOGETHER)

    def block(c, m):
        return lax.dynamic_slice_in_dim(flat, (c * n_dom + (me ^ m)) * size, size, 0)

    def sent(x, m):
        return swapped(x, "dom", n_dom, m)

    far = [jnp.concatenate([block(0, m), levels], axis=0) for m in range(2, n_dom)]
    far, flat, levels = lax.optimization_barrier((far, flat, levels))
    near = [block(0, 1), levels] + [block(c, 1) for c in range(1, n_chunks)]
    near = sent(jnp.concatenate(near, axis=0), 1)
    own = [block(c, 0) for c in range(n_chunks)]
    own[0] = jnp.concatenate([own[0], levels], axis=0)
    arrived = [[own[0], near] + [sent(x, m) for m, x in enumerate(far, start=2)]]
    for c in range(1, n_chunks):
        blocks = [own[c], near]
        for m in range(2, n_dom):
            x = block(c, m)
            arrived[c - 1][m - 1], x = lax.optimization_barrier((arrived[c - 1][m - 1], x))
            blocks.append(sent(x, m))
        arrived.append(blocks)
    for blocks in arrived:
        blocks[1] = arrived[0][1]
    diagonal = None
    done = []
    for c, blocks in enumerate(arrived):
        starts = [0] * n_dom
        starts[1] = c * size + (cells if c else 0)
        filtered = filter_orbitals(place, diagonal, blocks, starts, planes, rows)
        if diagonal is None:
            diagonal = filtered[n_dom]
        done.append(filtered[:n_dom])
    return [
        [(sent(x, m) if m else x).reshape(size, lanes) for m, x in enumerate(blocks)]
        for blocks in done
    ]


def plane_by_plane(panel, potential):
    n_dom = lax.axis_size("dom")
    diagonal = (potential + (SHIFT - CENTER_LEVEL)) * (2.0 / HALF_WIDTH)

    def twice_operator(field):
        low, high = shifted(field[:, -1:], -1), shifted(field[:, :1], 1)
        extended = jnp.concatenate([low, field, high], axis=1)
        near = extended[:, 2:] + extended[:, :-2]
        near += jnp.roll(field, 1, axis=2) + jnp.roll(field, -1, axis=2)
        padded = jnp.pad(field, ((0, 0), (0, 0), (0, 0), (1, 1)))
        near += padded[..., 2:] + padded[..., :-2]
        return diagonal * field - near / HALF_WIDTH

    def one_step(_, carry):
        before, current = carry
        return current, twice_operator(current) - before

    start = (panel, 0.5 * twice_operator(panel))
    return lax.fori_loop(0, DEGREE - 1, one_step, start)[1]


def on_device(panel, potential, point_offsets, point_coefs, correlation):
    orbitals, planes, rows, lanes = panel.shape
    n_dom, n_band, n_sub = (lax.axis_size(axis) for axis in ("dom", "band", "sub"))
    groups = n_band * n_sub
    me, band, sub = (lax.axis_index(axis) for axis in ("dom", "band", "sub"))
    place = jnp.stack([me, band, sub, band * n_sub + sub]).astype(jnp.int32)

    cells = planes * rows
    share = cells // n_band
    channels = correlation.shape[1]
    own_atoms = point_offsets.shape[0] // groups
    own_corr = lax.dynamic_slice_in_dim(
        correlation, (sub * n_band + band) * own_atoms, own_atoms, 0
    )
    same_atom = jnp.eye(own_atoms, dtype=jnp.float32)
    corr_matrix = (same_atom[:, None, :, None] * own_corr[:, :, None, :]).reshape(
        own_atoms * channels, own_atoms * channels
    )

    place, corr_matrix = lax.optimization_barrier((place, corr_matrix))

    def build(offsets):
        return build_projectors(n_band, n_sub, place, offsets, point_coefs, share, lanes)

    place, corr_matrix = lax.optimization_barrier((place, corr_matrix))

    def build(offsets):
        return build_projectors(n_band, n_sub, place, offsets, point_coefs, share, lanes)

    filtered, parts = [], []
    if n_dom in (2, 4) and orbitals % (n_dom * TOGETHER) == 0 and planes * n_dom % 2 == 0:
        chunks = whole_columns(panel, potential, place, me)
        chunks[-1][0], point_offsets = lax.optimization_barrier((chunks[-1][0], point_offsets))
        projectors = build(point_offsets)
        chunks[0], projectors = lax.optimization_barrier((chunks[0], projectors))
        filtered = orbital_first(place, n_dom, [piece for pieces in chunks for piece in pieces])
        parts = [cell_first(place, n_band, pieces) for pieces in chunks]
    else:
        projectors = build(point_offsets)
        filtered = plane_by_plane(panel, potential)
        by_cell = filtered.reshape(orbitals, cells, lanes).swapaxes(0, 1)
        parts = [
            [
                lax.dynamic_slice_in_dim(by_cell, (band ^ m) * share, share, 0)
                for m in range(n_band)
            ]
        ]
    filtered = filtered.reshape(panel.shape)
    chunks = len(parts)
    arrays = [x for by_band in parts for x in by_band[:1]]
    arrays += [
        swapped(by_band[m], "band", n_band, m) for by_band in parts for m in range(1, n_band)
    ]
    pieces = [jnp.concatenate(arrays[:chunks], axis=1)] + arrays[chunks:]
    arrays += [swapped(x, "sub", n_sub, k) for k in range(1, n_sub) for x in pieces]
    width = arrays[0].shape[1]
    spots = []
    for m in range(n_band):
        for k in range(n_sub):
            for c in range(chunks):
                at = chunks + c * (n_band - 1) + m - 1 if m else c
                if k == 0:
                    spots.append((at, 0, width))
                else:
                    base = chunks * n_band + (k - 1) * len(pieces)
                    if m:
                        spots.append((base + 1 + at - chunks, 0, width))
                    else:
                        spots.append((base, c * width, width))

    rows = own_atoms * channels * n_band
    outer = products(
        n_sub, 0, 2 * rows, 2 * n_band, False, place, projectors, arrays, spots
    )
    outer, place = lax.optimization_barrier((outer, place))
    grid_part, *inner = products(
        n_sub, 2 * rows, rows, n_band, True, place, projectors, arrays, spots
    )
    sums, seen = [], []
    for by, blocks in ((1, outer[:n_band]), (-1, outer[n_band:]), (0, inner)):
        for m, x in enumerate(blocks):
            if by == 0 and m == 0:
                continue
            pairs = [
                (d * n_band + b, (d - by) % n_dom * n_band + (b ^ m))
                for d in range(n_dom)
                for b in range(n_band)
            ]
            seen.append(m * n_sub)
            sums.append(lax.ppermute(x, ("dom", "band"), pairs))
    scale_point = 1.0 / (cells * lanes * n_dom)
    scale_atom = 1.0 / math.sqrt(own_atoms * groups * n_dom)
    shares = gram_share(
        (scale_point, scale_atom), groups, seen, place, corr_matrix, grid_part, inner[0], sums
    )
    gram_rows = added(
        [swapped(x, ("band", "sub"), groups, m) if m else x for m, x in enumerate(shares)]
    )
    if n_dom <= 4:
        gram_rows = added(
            [swapped(gram_rows, "dom", n_dom, m) if m else gram_rows for m in range(n_dom)]
        )
    else:
        by = 1
        while by < n_dom:
            gram_rows += swapped(gram_rows, "dom", n_dom, by)
            by *= 2
    return filtered, gram_rows


def solution(mesh):
    placed = (
        P(("slab", "band", "sub"), "dom", None, None),
        P(("slab", "dom"), None, None),
        P(("slab", "dom"), None, None),
        P(("slab", "dom"), None, None, None),
        P(("slab", "dom"), None, None),
    )
    return jax.shard_map(
        on_device,
        mesh=mesh,
        in_specs=placed,
        out_specs=(P(("slab", "band", "sub"), "dom", None, None), P(("slab", "band", "sub"), None)),
        check_vma=False,
    )
```

```python
import functools
import math

import jax
import jax.numpy as jnp
from jax import lax
from jax.experimental import pallas as pl
from jax.experimental.pallas import tpu as pltpu
from jax.sharding import PartitionSpec as P

DEGREE = 12

CENTER_LEVEL = 3.6
HALF_WIDTH = 3.4
SHIFT = 3.0

TOGETHER = 4
SUBLANES = 8
ME, BAND, SUB, GROUP = range(4)
MIB = 1024 * 1024

VMEM = pl.BlockSpec(memory_space=pltpu.VMEM)
SMEM = pl.BlockSpec(memory_space=pltpu.SMEM)
NT = (((1,), (1,)), ((), ()))
TN = (((0,), (0,)), ((), ()))


def params(mib):
    return pltpu.CompilerParams(vmem_limit_bytes=mib * MIB)


def split_bf16(x):
    high = x.astype(jnp.bfloat16)
    return high, (x - high.astype(jnp.float32)).astype(jnp.bfloat16)


def shifted(x, by):
    size = lax.axis_size("dom")
    return lax.ppermute(x, "dom", [(i, (i - by) % size) for i in range(size)])


def swapped(x, axes, size, by):
    return lax.ppermute(x, axes, [(i, i ^ by) for i in range(size)])


def pack_kernel(n_dom, size, contents, place, panel, *refs):
    levels, outs, sems = refs[0], refs[1:-1], refs[-1]
    copies = []
    for out, content in zip(outs, contents):
        at = 0
        for kind, c, m in content:
            if kind == "block":
                start = pl.multiple_of((c * n_dom + (place[ME] ^ m)) * size, SUBLANES)
                copies.append((panel.at[pl.ds(start, size)], out.at[pl.ds(at, size)]))
                at += size
            else:
                share = levels.shape[0] if kind == "levels" else out.shape[0] - at
                start = 0
                if kind == "share":
                    start = pl.multiple_of(place[SUB] * share, SUBLANES)
                copies.append((levels.at[pl.ds(start, share)], out.at[pl.ds(at, share)]))
                at += share
    copies = [pltpu.make_async_copy(a, b, sems.at[k]) for k, (a, b) in enumerate(copies)]
    for copy in copies:
        copy.start()
    for copy in copies:
        copy.wait()


def pack(place, n_dom, n_sub, size, panel, levels, contents):
    rows = {"block": size, "levels": levels.shape[0], "share": levels.shape[0] // n_sub}
    lanes = panel.shape[1]
    shapes = [
        jax.ShapeDtypeStruct((sum(rows[kind] for kind, _, _ in content), lanes), jnp.float32)
        for content in contents
    ]
    return pl.pallas_call(
        functools.partial(pack_kernel, n_dom, size, contents),
        out_shape=shapes,
        in_specs=[SMEM] + [pl.BlockSpec(memory_space=pltpu.HBM)] * 2,
        out_specs=[VMEM] * len(shapes),
        scratch_shapes=[pltpu.SemaphoreType.DMA((sum(len(x) for x in contents),))],
        compiler_params=params(6),
        name="pack",
    )(place, panel, levels)


def filter_kernel(n_dom, planes, rows, starts, n_levels, place, *refs):
    refs = list(refs)
    first = n_levels > 0
    given, refs = (refs[:n_levels], refs[n_levels:]) if first else (refs[:1], refs[1:])
    ins, outs = refs[:n_dom], refs[n_dom : 2 * n_dom]
    refs = refs[2 * n_dom :]
    diagonal = refs.pop(0) if first else given[0]
    even, odd, levels = refs
    half_planes = n_dom * planes // 2
    cells = planes * rows
    lanes = even.shape[3]
    scale = 1.0 / HALF_WIDTH
    mirrored = (place[ME] & 1) != 0
    plane_at = [jnp.where(mirrored, planes - 1 - i, i) for i in range(planes)]

    if first:
        levels[0] = given[0][...]
        levels[1] = ins[1][TOGETHER * cells : (TOGETHER + 1) * cells, :]
        n_sub = (n_levels - 1) // max(n_dom - 2, 1)
        for k, piece in enumerate(given[1:]):
            share = piece.shape[0]
            at = pl.multiple_of((place[SUB] ^ (k % n_sub)) * share, SUBLANES)
            levels[2 + k // n_sub, pl.ds(at, share), :] = piece[...]

    for x in range(half_planes):
        for half in range(2):
            m, i = divmod(half * half_planes + x, planes)
            part = slice(half * TOGETHER, (half + 1) * TOGETHER)
            base = starts[m] + plane_at[i] * rows
            for y in range(rows):
                even[x, y, part] = ins[m][pl.ds(base + y, TOGETHER, stride=cells), :]
                if first:
                    level = levels[m, pl.ds(plane_at[i] * rows + y, 1), :]
                    diagonal[x, y, part] = jnp.broadcast_to(
                        (level + (SHIFT - CENTER_LEVEL)) * (2.0 * scale), (TOGETHER, lanes)
                    )

    block = SUBLANES
    lane = lax.broadcasted_iota(jnp.int32, (block, SUBLANES, lanes), 2)
    at_start, at_end = lane == 0, lane == lanes - 1

    def twice_operator(source, x, y):
        here = slice(y, y + block)
        centre = source[x, here]
        if x == 0:
            near = pltpu.roll(source[half_planes - 1, here], TOGETHER, 1) + source[x + 1, here]
        elif x == half_planes - 1:
            near = pltpu.roll(source[0, here], TOGETHER, 1) + source[x - 1, here]
        else:
            near = source[x - 1, here] + source[x + 1, here]
        before = (y - 1) % rows
        after = (y + block) % rows
        near += jnp.concatenate([source[x, before : before + 1], centre[:-1]], axis=0)
        near += jnp.concatenate([centre[1:], source[x, after : after + 1]], axis=0)
        low = pltpu.roll(centre, 1, 2)
        high = pltpu.roll(centre, lanes - 1, 2)
        near += jnp.where(at_start, high, jnp.where(at_end, low, low + high))
        return diagonal[x, here] * centre - scale * near

    places = [(x, y) for x in range(half_planes) for y in range(0, rows, block)]

    def next_field(source, target):
        for x, y in places:
            target[x, y : y + block] = twice_operator(source, x, y) - target[x, y : y + block]

    for x, y in places:
        odd[x, y : y + block] = 0.5 * twice_operator(even, x, y)
    next_field(odd, even)

    def two_steps(_, carry):
        next_field(even, odd)
        next_field(odd, even)
        return carry

    lax.fori_loop(0, DEGREE // 2 - 1, two_steps, 0)
    for m in range(n_dom):
        for i in range(planes):
            half, x = divmod(m * planes + i, half_planes)
            part = slice(half * TOGETHER, (half + 1) * TOGETHER)
            for y in range(rows):
                here = slice(y * TOGETHER, (y + 1) * TOGETHER)
                outs[m][plane_at[i], here, :] = even[x, y, part]


def filter_orbitals(place, diagonal, levels, blocks, starts, planes, rows):
    n_dom = len(blocks)
    first = diagonal is None
    lanes = blocks[0].shape[1]
    field = (n_dom * planes // 2, rows, SUBLANES, lanes)
    out = jax.ShapeDtypeStruct((planes, rows * TOGETHER, lanes), jnp.float32)
    extra = [jax.ShapeDtypeStruct(field, jnp.float32)] if first else []
    given = levels if first else [diagonal]
    n_levels = len(levels) if first else 0
    size = n_dom * planes * rows * TOGETHER * lanes
    return pl.pallas_call(
        functools.partial(filter_kernel, n_dom, planes, rows, starts, n_levels),
        out_shape=[out] * n_dom + extra,
        in_specs=[SMEM] + [VMEM] * (n_dom + len(given)),
        out_specs=[VMEM] * (n_dom + len(extra)),
        scratch_shapes=[pltpu.VMEM(field, jnp.float32)] * 2
        + [pltpu.VMEM((n_dom, planes * rows, lanes), jnp.float32)],
        compiler_params=params(8),
        cost_estimate=pl.CostEstimate(
            flops=12 * DEGREE * size, bytes_accessed=8 * size, transcendentals=0
        ),
        name="chebyshev",
    )(place, *given, *blocks)


def cell_first_kernel(n_dom, n_band, place, *refs):
    pieces, parts = refs[:-n_band], refs[-n_band:]
    share = parts[0].shape[0]
    me = place[ME]
    together = SUBLANES // TOGETHER
    per_chunk = n_dom // together
    tiles = len(pieces) // together
    for p, part in enumerate(parts):
        base = pl.multiple_of((place[BAND] ^ p) * (share * TOGETHER), SUBLANES)
        for first in range(0, share, together):
            loaded = [piece[pl.ds(base + first * TOGETHER, SUBLANES), :] for piece in pieces]
            for k in range(together):
                here = slice(k * TOGETHER, (k + 1) * TOGETHER)
                for q in range(tiles):
                    tile = jnp.concatenate(
                        [loaded[q * together + i][here] for i in range(together)], axis=0
                    )
                    tile = jnp.where((me & 1) != 0, pltpu.roll(tile, TOGETHER, 0), tile)
                    chunk, half = divmod(q, per_chunk)
                    if (chunk + 1) * per_chunk <= tiles:
                        half = half ^ (me // together)
                    row = pl.multiple_of((chunk * per_chunk + half) * SUBLANES, SUBLANES)
                    part[first + k, pl.ds(row, SUBLANES), :] = tile


def cell_first(place, n_dom, n_band, pieces):
    rows, lanes = pieces[0].shape
    orbitals = len(pieces) * TOGETHER
    part = jax.ShapeDtypeStruct((rows // (TOGETHER * n_band), orbitals, lanes), jnp.float32)
    return pl.pallas_call(
        functools.partial(cell_first_kernel, n_dom, n_band),
        out_shape=[part] * n_band,
        in_specs=[SMEM] + [VMEM] * len(pieces),
        out_specs=[VMEM] * n_band,
        compiler_params=params(8),
        name="cell_first",
    )(place, *pieces)


def orbital_first_kernel(n_dom, place, *refs):
    *pieces, out = refs
    cells = out.shape[1]
    for k, piece in enumerate(pieces):
        chunk, m = divmod(k, n_dom)
        start = (chunk * n_dom + (place[ME] ^ m)) * TOGETHER
        for t in range(TOGETHER):
            out[start + t] = piece[pl.ds(t, cells, stride=TOGETHER), :]


def orbital_first(place, n_dom, pieces):
    rows, lanes = pieces[0].shape
    shape = (len(pieces) * TOGETHER, rows // TOGETHER, lanes)
    return pl.pallas_call(
        functools.partial(orbital_first_kernel, n_dom),
        out_shape=jax.ShapeDtypeStruct(shape, jnp.float32),
        in_specs=[SMEM] + [VMEM] * len(pieces),
        out_specs=VMEM,
        compiler_params=params(8),
        cost_estimate=pl.CostEstimate(
            flops=math.prod(shape), bytes_accessed=8 * math.prod(shape), transcendentals=0
        ),
        name="orbital_first",
    )(place, *pieces)


def projector_kernel(n_band, n_sub, place, offsets_ref, coefs_ref, high_out, low_out):
    atoms, shells, channels, spread = coefs_ref.shape
    own = atoms // (n_band * n_sub)
    lanes = spread
    cells = high_out.shape[1] // lanes
    pairs = own // 2
    row_index = lax.broadcasted_iota(jnp.int32, (cells, channels, spread), 0)
    row_index += place[BAND] * cells
    lane_index = lax.broadcasted_iota(jnp.int32, (lanes, spread), 0)

    def two_atoms(step, carry):
        shell = lax.rem(2 * (step // (n_band * pairs)), shells)
        seen = (step // pairs) % n_band
        seen = jnp.where(shell == 1, n_band - 1 - seen, seen)
        band = place[BAND] ^ seen
        first_atom = (place[SUB] * n_band + band) * own + 2 * (step % pairs)
        dense = []
        for i in range(2):
            offsets = offsets_ref[shell, pl.ds(first_atom + i, 1), :]
            coefs = coefs_ref[first_atom + i, shell]
            at_row = row_index == (offsets // lanes)[None]
            at_row &= (offsets >= 0)[None]
            left = [
                jnp.where(at_row, part.astype(jnp.float32)[None], 0.0)
                .reshape(cells * channels, spread)
                .astype(jnp.bfloat16)
                for part in split_bf16(coefs)
            ]
            at_lane = jnp.where(lane_index == (offsets & (lanes - 1)), 1.0, 0.0)
            at_lane = at_lane.astype(jnp.bfloat16)
            values = lax.dot_general(
                jnp.concatenate(left, axis=1),
                jnp.concatenate([at_lane, at_lane], axis=1),
                NT,
                preferred_element_type=jnp.float32,
            )
            dense.append(values.reshape(cells, channels, lanes))
        high, low = split_bf16(jnp.concatenate(dense, axis=1))
        rows = pl.ds(pl.multiple_of(step * 2 * channels, 2 * channels), 2 * channels)
        for cell in range(cells):
            high_out[rows, cell * lanes : (cell + 1) * lanes] = high[cell]
            low_out[rows, cell * lanes : (cell + 1) * lanes] = low[cell]
        return carry

    lax.fori_loop(0, shells * n_band * pairs, two_atoms, 0)


def build_projectors(n_band, n_sub, place, offsets, coefs, cells, lanes):
    atoms, shells, channels, spread = coefs.shape
    rows = atoms // n_sub * shells * channels
    shape = jax.ShapeDtypeStruct((rows, cells * lanes), jnp.bfloat16)
    return pl.pallas_call(
        functools.partial(projector_kernel, n_band, n_sub),
        out_shape=[shape, shape],
        in_specs=[SMEM, VMEM, VMEM],
        out_specs=[VMEM, VMEM],
        compiler_params=params(8),
        cost_estimate=pl.CostEstimate(
            flops=4 * rows * cells * lanes * spread,
            bytes_accessed=8 * rows * cells * lanes,
            transcendentals=0,
        ),
        name="projectors",
    )(place, offsets.swapaxes(0, 1), coefs)


def product_kernel(spots, n_sub, first_row, n_blocks, with_grid, place, w_high, w_low, *refs):
    refs, proj_out = refs[:-1], refs[-1]
    n_outs = n_blocks + (1 if with_grid else 0)
    arrays, outs = refs[:-n_outs], list(refs[-n_outs:])
    rows, orbitals = proj_out.shape
    cells, _, lanes = arrays[0].shape
    block = 12
    swap = (place[ME] & 2) != 0

    def parts(start):
        highs, lows = [], []
        for spot in spots:
            tiles = [
                arrays[at][pl.ds(start, block), first : first + width] for at, first, width in spot
            ]
            if len(tiles) == 2:
                near, far = tiles
                tiles = [jnp.where(swap, far, near), jnp.where(swap, near, far)]
            high, low = split_bf16(jnp.concatenate(tiles, axis=1))
            highs.append(jnp.concatenate([high[k] for k in range(block)], axis=1))
            lows.append(jnp.concatenate([low[k] for k in range(block)], axis=1))
        return jnp.concatenate(highs, axis=0), jnp.concatenate(lows, axis=0)

    def product(left_high, left_low, high, low):
        right = jnp.concatenate([high, low], axis=0)
        wide = lax.dot_general(left_high, right, NT, preferred_element_type=jnp.float32)
        narrow = lax.dot_general(left_low, high, NT, preferred_element_type=jnp.float32)
        return wide[:, :orbitals] + wide[:, orbitals:] + narrow

    if with_grid:
        grid_out = outs.pop(0)
        grid_out[...] = jnp.zeros_like(grid_out)

        def grid_block(step, carry):
            high, low = parts(place[SUB] * (cells // n_sub) + step * block)
            grid_out[...] += product(high, low, high, low)
            return carry

        lax.fori_loop(0, cells // (n_sub * block), grid_block, 0)

    def proj_block(step, carry):
        high, low = parts(step * block)
        depth = block * lanes
        here = pl.ds(pl.multiple_of(step * depth, depth), depth)
        some = slice(first_row, first_row + rows)
        proj_out[...] += product(w_high[some, here], w_low[some, here], high, low)
        return carry

    proj_out[...] = jnp.zeros_like(proj_out)
    lax.fori_loop(0, cells // block, proj_block, 0)
    for k, out in enumerate(outs):
        out[...] = proj_out[k * (rows // n_blocks) : (k + 1) * (rows // n_blocks), :]


def products(n_sub, first_row, rows, n_blocks, with_grid, place, projectors, arrays, spots):
    orbitals = sum(width for spot in spots for _, _, width in spot)
    grid = [jax.ShapeDtypeStruct((orbitals, orbitals), jnp.float32)] if with_grid else []
    block = jax.ShapeDtypeStruct((rows // n_blocks, orbitals), jnp.float32)
    flops = 12 * rows * orbitals * projectors[0].shape[1]
    return pl.pallas_call(
        functools.partial(product_kernel, spots, n_sub, first_row, n_blocks, with_grid),
        out_shape=grid + [block] * n_blocks,
        in_specs=[SMEM] + [VMEM] * (2 + len(arrays)),
        out_specs=[VMEM] * (len(grid) + n_blocks),
        scratch_shapes=[pltpu.VMEM((rows, orbitals), jnp.float32)],
        compiler_params=params(8),
        cost_estimate=pl.CostEstimate(
            flops=flops, bytes_accessed=4 * rows * projectors[0].shape[1], transcendentals=0
        ),
        name="products",
    )(place, *projectors, *arrays)


def reordered(x, width, by):
    span = width * by
    column = lax.broadcasted_iota(jnp.int32, x.shape, 1)
    up, down = pltpu.roll(x, span, 1), pltpu.roll(x, x.shape[1] - span, 1)
    return jnp.where((column & span) == 0, down, up)


def gram_kernel(scales, groups, seen, place, corr_ref, grid_ref, proj_ref, *refs):
    sums, outs = refs[: len(seen)], refs[len(seen) :]
    orbitals = grid_ref.shape[0]
    width = orbitals // groups
    bits = [1 << k for k in range(groups.bit_length() - 1)]
    projections = proj_ref[...]
    for part, by in zip(sums, seen):
        columns = part[...]
        for bit in bits:
            if by & bit:
                columns = reordered(columns, width, bit)
        projections += columns
    highest = lax.Precision.HIGHEST
    weighted = jnp.dot(
        corr_ref[...], projections, precision=highest, preferred_element_type=jnp.float32
    )
    atom_part = lax.dot_general(
        projections, weighted, TN, precision=highest, preferred_element_type=jnp.float32
    )
    share = grid_ref[...] * scales[0] + atom_part * scales[1]
    for bit in bits:
        share = jnp.where((place[GROUP] & bit) != 0, reordered(share, width, bit), share)
    for k, out in enumerate(outs):
        out[...] = share[k * width : (k + 1) * width]


def gram_share(scales, groups, seen, place, corr, grid_part, proj, sums):
    rows = jax.ShapeDtypeStruct((grid_part.shape[0] // groups, grid_part.shape[1]), jnp.float32)
    return pl.pallas_call(
        functools.partial(gram_kernel, scales, groups, seen),
        out_shape=[rows] * groups,
        in_specs=[SMEM] + [VMEM] * (3 + len(sums)),
        out_specs=[VMEM] * groups,
        compiler_params=params(8),
        name="gram_share",
    )(place, corr, grid_part, proj, *sums)


def added(terms):
    while len(terms) > 1:
        terms = [a + b for a, b in zip(terms[::2], terms[1::2])]
    return terms[0]


def whole_columns(panel, potential, place, early):
    n_dom, n_sub = lax.axis_size("dom"), lax.axis_size("sub")
    orbitals, planes, rows, lanes = panel.shape
    cells = planes * rows
    flat = panel.reshape(orbitals * cells, lanes)
    levels = potential.reshape(cells, lanes)
    size = TOGETHER * cells
    n_chunks = orbitals // (n_dom * TOGETHER)

    def sent(x, m):
        return swapped(x, "dom", n_dom, m)

    def packed(place, contents):
        return pack(place, n_dom, n_sub, size, flat, levels, contents)

    contents = [[("block", 0, 1), ("levels", 0, 0)] + [("block", c, 1) for c in range(1, n_chunks)]]
    for m in range(2, n_dom):
        contents.append([("block", 0, m)] + ([("share", 0, 0)] if m == 2 else []))
    near, *far = packed(place, contents)
    near, *far = [sent(x, m) for m, x in enumerate([near] + far, start=1)]
    given = [levels]
    if far:
        shares = [far[0][size:]]
        shares.append(sent(shares[0], 1))
        for x in shares:
            given += [x] + [swapped(x, "sub", n_sub, k) for k in range(1, n_sub)]
    contents = [[("block", c, 0)] for c in range(n_chunks)]
    contents += [[("block", c, m)] for c in range(1, n_chunks) for m in range(2, n_dom)]
    rest = packed(place, contents)
    own, rest = rest[:n_chunks], rest[n_chunks:]
    near, rest, early = lax.optimization_barrier((near, rest, early))
    arrived = [[own[0], near] + far]
    for c in range(1, n_chunks):
        blocks = [sent(x, m) for m, x in enumerate(rest[: n_dom - 2], start=2)]
        rest = rest[n_dom - 2 :]
        arrived.append([own[c], near] + blocks)
    diagonal = None
    done = []
    for c, blocks in enumerate(arrived):
        starts = [0] * n_dom
        starts[1] = c * size + (cells if c else 0)
        filtered = filter_orbitals(place, diagonal, given, blocks, starts, planes, rows)
        if diagonal is None:
            diagonal = filtered[n_dom]
        done.append(filtered[:n_dom])
    return [
        [(sent(x, m) if m else x).reshape(size, lanes) for m, x in enumerate(blocks)]
        for blocks in done
    ], early


def plane_by_plane(panel, potential):
    n_dom = lax.axis_size("dom")
    diagonal = (potential + (SHIFT - CENTER_LEVEL)) * (2.0 / HALF_WIDTH)

    def twice_operator(field):
        low, high = shifted(field[:, -1:], -1), shifted(field[:, :1], 1)
        extended = jnp.concatenate([low, field, high], axis=1)
        near = extended[:, 2:] + extended[:, :-2]
        near += jnp.roll(field, 1, axis=2) + jnp.roll(field, -1, axis=2)
        padded = jnp.pad(field, ((0, 0), (0, 0), (0, 0), (1, 1)))
        near += padded[..., 2:] + padded[..., :-2]
        return diagonal * field - near / HALF_WIDTH

    def one_step(_, carry):
        before, current = carry
        return current, twice_operator(current) - before

    start = (panel, 0.5 * twice_operator(panel))
    return lax.fori_loop(0, DEGREE - 1, one_step, start)[1]


def on_device(panel, potential, point_offsets, point_coefs, correlation):
    orbitals, planes, rows, lanes = panel.shape
    n_dom, n_band, n_sub = (lax.axis_size(axis) for axis in ("dom", "band", "sub"))
    groups = n_band * n_sub
    me, band, sub = (lax.axis_index(axis) for axis in ("dom", "band", "sub"))
    place = jnp.stack([me, band, sub, band * n_sub + sub]).astype(jnp.int32)

    cells = planes * rows
    share = cells // n_band
    channels = correlation.shape[1]
    own_atoms = point_offsets.shape[0] // groups
    own_corr = lax.dynamic_slice_in_dim(
        correlation, (sub * n_band + band) * own_atoms, own_atoms, 0
    )
    same_atom = jnp.eye(own_atoms, dtype=jnp.float32)
    corr_matrix = (same_atom[:, None, :, None] * own_corr[:, :, None, :]).reshape(
        own_atoms * channels, own_atoms * channels
    )

    def build(offsets):
        return build_projectors(n_band, n_sub, place, offsets, point_coefs, share, lanes)

    if n_dom in (2, 4) and orbitals % (n_dom * TOGETHER) == 0 and planes * n_dom % 2 == 0:
        chunks, corr_matrix = whole_columns(panel, potential, place, corr_matrix)
        chunks[-1][0], point_offsets = lax.optimization_barrier((chunks[-1][0], point_offsets))
        projectors = build(point_offsets)
        chunks[0], projectors = lax.optimization_barrier((chunks[0], projectors))
        filtered = orbital_first(place, n_dom, [piece for pieces in chunks for piece in pieces])
        parts = [cell_first(place, n_dom, n_band, pieces) for pieces in chunks]
        tiles = [[(c, 0, n_dom * TOGETHER)] for c in range(len(chunks))]
    else:
        projectors = build(point_offsets)
        filtered = plane_by_plane(panel, potential)
        by_cell = filtered.reshape(orbitals, cells, lanes).swapaxes(0, 1)
        parts = [
            [
                lax.dynamic_slice_in_dim(by_cell, (band ^ m) * share, share, 0)
                for m in range(n_band)
            ]
        ]
        tiles = [[(0, 0, orbitals)]]
    filtered = filtered.reshape(panel.shape)
    own = [part[0] for part in parts]
    pieces = [swapped(part[m], "band", n_band, m) for part in parts for m in range(1, n_band)]
    pieces[0], filtered = lax.optimization_barrier((pieces[0], filtered))
    arrays = own + pieces
    pieces = [jnp.concatenate(own, axis=1)] + pieces
    arrays += [swapped(x, "sub", n_sub, k) for k in range(1, n_sub) for x in pieces]
    starts = [sum(x.shape[1] for x in own[:at]) for at in range(len(own))]
    spots = []
    for m in range(n_band):
        for k in range(n_sub):
            for tile in tiles:
                spot = []
                for at, first, width in tile:
                    index = at
                    if m:
                        index = len(own) + at * (n_band - 1) + m - 1 + k * len(pieces)
                    elif k:
                        index = len(own) * n_band + (k - 1) * len(pieces)
                        first += starts[at]
                    spot.append((index, first, width))
                spots.append(spot)

    rows = own_atoms * channels
    n_sent = 3 * n_band - 1
    outgoing = products(
        n_sub, 0, n_sent * rows, n_sent, False, place, projectors, arrays, spots
    )
    outgoing, place = lax.optimization_barrier((outgoing, place))
    grid_part, own_proj = products(
        n_sub, n_sent * rows, rows, 1, True, place, projectors, arrays, spots
    )
    sums, seen = [], []
    to = [(by, m) for by in (1, -1) for m in range(n_band)]
    to += [(0, m) for m in range(n_band - 1, 0, -1)]
    for x, (by, m) in zip(outgoing, to):
        pairs = [
            (d * n_band + b, (d - by) % n_dom * n_band + (b ^ m))
            for d in range(n_dom)
            for b in range(n_band)
        ]
        seen.append(m * n_sub)
        sums.append(lax.ppermute(x, ("dom", "band"), pairs))
    scale_point = 1.0 / (cells * lanes * n_dom)
    scale_atom = 1.0 / math.sqrt(own_atoms * groups * n_dom)
    shares = gram_share(
        (scale_point, scale_atom), groups, seen, place, corr_matrix, grid_part, own_proj, sums
    )
    gram_rows = added(
        [swapped(x, ("band", "sub"), groups, m) if m else x for m, x in enumerate(shares)]
    )
    if n_dom <= 4:
        gram_rows = added(
            [swapped(gram_rows, "dom", n_dom, m) if m else gram_rows for m in range(n_dom)]
        )
    else:
        by = 1
        while by < n_dom:
            gram_rows += swapped(gram_rows, "dom", n_dom, by)
            by *= 2
    return filtered, gram_rows


def solution(mesh):
    placed = (
        P(("slab", "band", "sub"), "dom", None, None),
        P(("slab", "dom"), None, None),
        P(("slab", "dom"), None, None),
        P(("slab", "dom"), None, None, None),
        P(("slab", "dom"), None, None),
    )
    return jax.shard_map(
        on_device,
        mesh=mesh,
        in_specs=placed,
        out_specs=(P(("slab", "band", "sub"), "dom", None, None), P(("slab", "band", "sub"), None)),
        check_vma=False,
    )
```

```python
import functools
import math

import jax
import jax.numpy as jnp
from jax import lax
from jax.experimental import pallas as pl
from jax.experimental.pallas import tpu as pltpu
from jax.sharding import PartitionSpec as P

DEGREE = 12

CENTER_LEVEL = 3.6
HALF_WIDTH = 3.4
SHIFT = 3.0

TOGETHER = 4
SUBLANES = 8
ME, BAND, SUB, GROUP = range(4)
MIB = 1024 * 1024

VMEM = pl.BlockSpec(memory_space=pltpu.VMEM)
SMEM = pl.BlockSpec(memory_space=pltpu.SMEM)
NT = (((1,), (1,)), ((), ()))
TN = (((0,), (0,)), ((), ()))


def params(mib):
    return pltpu.CompilerParams(vmem_limit_bytes=mib * MIB)


def split_bf16(x):
    high = x.astype(jnp.bfloat16)
    return high, (x - high.astype(jnp.float32)).astype(jnp.bfloat16)


def shifted(x, by):
    size = lax.axis_size("dom")
    return lax.ppermute(x, "dom", [(i, (i - by) % size) for i in range(size)])


def swapped(x, axes, size, by):
    return lax.ppermute(x, axes, [(i, i ^ by) for i in range(size)])


def filter_kernel(n_dom, planes, rows, starts, first, place, *refs):
    refs = list(refs)
    given = None if first else refs.pop(0)
    ins, outs = refs[:n_dom], refs[n_dom : 2 * n_dom]
    refs = refs[2 * n_dom :]
    diagonal = refs.pop(0) if first else given
    even, odd = refs
    half_planes = n_dom * planes // 2
    cells = planes * rows
    lanes = even.shape[3]
    scale = 1.0 / HALF_WIDTH
    mirrored = (place[ME] & 1) != 0
    plane_at = [jnp.where(mirrored, planes - 1 - i, i) for i in range(planes)]

    for x in range(half_planes):
        for half in range(2):
            m, i = divmod(half * half_planes + x, planes)
            part = slice(half * TOGETHER, (half + 1) * TOGETHER)
            base = starts[m] + plane_at[i] * rows
            for y in range(rows):
                even[x, y, part] = ins[m][pl.ds(base + y, TOGETHER, stride=cells), :]
                if first:
                    level = ins[m][pl.ds(base + (TOGETHER * cells + y), 1), :]
                    diagonal[x, y, part] = jnp.broadcast_to(
                        (level + (SHIFT - CENTER_LEVEL)) * (2.0 * scale), (TOGETHER, lanes)
                    )

    block = SUBLANES
    lane = lax.broadcasted_iota(jnp.int32, (block, SUBLANES, lanes), 2)
    at_start, at_end = lane == 0, lane == lanes - 1

    def twice_operator(source, x, y):
        here = slice(y, y + block)
        centre = source[x, here]
        if x == 0:
            near = pltpu.roll(source[half_planes - 1, here], TOGETHER, 1) + source[x + 1, here]
        elif x == half_planes - 1:
            near = pltpu.roll(source[0, here], TOGETHER, 1) + source[x - 1, here]
        else:
            near = source[x - 1, here] + source[x + 1, here]
        before = (y - 1) % rows
        after = (y + block) % rows
        near += jnp.concatenate([source[x, before : before + 1], centre[:-1]], axis=0)
        near += jnp.concatenate([centre[1:], source[x, after : after + 1]], axis=0)
        low = pltpu.roll(centre, 1, 2)
        high = pltpu.roll(centre, lanes - 1, 2)
        near += jnp.where(at_start, high, jnp.where(at_end, low, low + high))
        return diagonal[x, here] * centre - scale * near

    places = [(x, y) for x in range(half_planes) for y in range(0, rows, block)]

    def next_field(source, target):
        for x, y in places:
            target[x, y : y + block] = twice_operator(source, x, y) - target[x, y : y + block]

    for x, y in places:
        odd[x, y : y + block] = 0.5 * twice_operator(even, x, y)
    next_field(odd, even)

    def two_steps(_, carry):
        next_field(even, odd)
        next_field(odd, even)
        return carry

    lax.fori_loop(0, DEGREE // 2 - 1, two_steps, 0)
    for m in range(n_dom):
        for i in range(planes):
            half, x = divmod(m * planes + i, half_planes)
            part = slice(half * TOGETHER, (half + 1) * TOGETHER)
            for y in range(rows):
                here = slice(y * TOGETHER, (y + 1) * TOGETHER)
                outs[m][plane_at[i], here, :] = even[x, y, part]


def filter_orbitals(place, diagonal, blocks, starts, planes, rows):
    n_dom = len(blocks)
    first = diagonal is None
    lanes = blocks[0].shape[1]
    field = (n_dom * planes // 2, rows, SUBLANES, lanes)
    out = jax.ShapeDtypeStruct((planes, rows * TOGETHER, lanes), jnp.float32)
    extra = [jax.ShapeDtypeStruct(field, jnp.float32)] if first else []
    given = [] if first else [diagonal]
    size = n_dom * planes * rows * TOGETHER * lanes
    return pl.pallas_call(
        functools.partial(filter_kernel, n_dom, planes, rows, starts, first),
        out_shape=[out] * n_dom + extra,
        in_specs=[SMEM] + [VMEM] * (n_dom + len(given)),
        out_specs=[VMEM] * (n_dom + len(extra)),
        scratch_shapes=[pltpu.VMEM(field, jnp.float32)] * 2,
        compiler_params=params(8),
        cost_estimate=pl.CostEstimate(
            flops=12 * DEGREE * size, bytes_accessed=8 * size, transcendentals=0
        ),
        name="chebyshev",
    )(place, *given, *blocks)


def cell_first_kernel(n_band, place, *refs):
    pieces, parts = refs[:-n_band], refs[-n_band:]
    share = parts[0].shape[0]
    me = place[ME]
    together = SUBLANES // TOGETHER
    tiles = len(pieces) // together
    for p, part in enumerate(parts):
        base = pl.multiple_of((place[BAND] ^ p) * (share * TOGETHER), SUBLANES)
        for first in range(0, share, together):
            loaded = [piece[pl.ds(base + first * TOGETHER, SUBLANES), :] for piece in pieces]
            for k in range(together):
                here = slice(k * TOGETHER, (k + 1) * TOGETHER)
                for q in range(tiles):
                    tile = jnp.concatenate(
                        [loaded[q * together + i][here] for i in range(together)], axis=0
                    )
                    tile = jnp.where((me & 1) != 0, pltpu.roll(tile, TOGETHER, 0), tile)
                    if tiles == 1:
                        part[first + k] = tile
                    else:
                        row = pl.multiple_of((q ^ (me // together)) * SUBLANES, SUBLANES)
                        part[first + k, pl.ds(row, SUBLANES), :] = tile


def cell_first(place, n_band, pieces):
    rows, lanes = pieces[0].shape
    orbitals = len(pieces) * TOGETHER
    part = jax.ShapeDtypeStruct((rows // (TOGETHER * n_band), orbitals, lanes), jnp.float32)
    return pl.pallas_call(
        functools.partial(cell_first_kernel, n_band),
        out_shape=[part] * n_band,
        in_specs=[SMEM] + [VMEM] * len(pieces),
        out_specs=[VMEM] * n_band,
        compiler_params=params(8),
        name="cell_first",
    )(place, *pieces)


def orbital_first_kernel(n_dom, place, *refs):
    *pieces, out = refs
    cells = out.shape[1]
    for k, piece in enumerate(pieces):
        chunk, m = divmod(k, n_dom)
        start = (chunk * n_dom + (place[ME] ^ m)) * TOGETHER
        for t in range(TOGETHER):
            out[start + t] = piece[pl.ds(t, cells, stride=TOGETHER), :]


def orbital_first(place, n_dom, pieces):
    rows, lanes = pieces[0].shape
    shape = (len(pieces) * TOGETHER, rows // TOGETHER, lanes)
    return pl.pallas_call(
        functools.partial(orbital_first_kernel, n_dom),
        out_shape=jax.ShapeDtypeStruct(shape, jnp.float32),
        in_specs=[SMEM] + [VMEM] * len(pieces),
        out_specs=VMEM,
        compiler_params=params(8),
        name="orbital_first",
    )(place, *pieces)


def projector_kernel(n_band, n_sub, place, offsets_ref, coefs_ref, high_out, low_out):
    atoms, shells, channels, spread = coefs_ref.shape
    own = atoms // (n_band * n_sub)
    lanes = spread
    cells = high_out.shape[1] // lanes
    pairs = own // 2
    row_index = lax.broadcasted_iota(jnp.int32, (cells, channels, spread), 0)
    row_index += place[BAND] * cells
    lane_index = lax.broadcasted_iota(jnp.int32, (lanes, spread), 0)

    def two_atoms(step, carry):
        shell = lax.rem(2 * (step // (n_band * pairs)), shells)
        seen = (step // pairs) % n_band
        seen = jnp.where(shell == 1, n_band - 1 - seen, seen)
        band = place[BAND] ^ seen
        first_atom = (place[SUB] * n_band + band) * own + 2 * (step % pairs)
        dense = []
        for i in range(2):
            offsets = offsets_ref[shell, pl.ds(first_atom + i, 1), :]
            coefs = coefs_ref[first_atom + i, shell]
            at_row = row_index == (offsets // lanes)[None]
            at_row &= (offsets >= 0)[None]
            left = [
                jnp.where(at_row, part.astype(jnp.float32)[None], 0.0)
                .reshape(cells * channels, spread)
                .astype(jnp.bfloat16)
                for part in split_bf16(coefs)
            ]
            at_lane = jnp.where(lane_index == (offsets & (lanes - 1)), 1.0, 0.0)
            at_lane = at_lane.astype(jnp.bfloat16)
            values = lax.dot_general(
                jnp.concatenate(left, axis=1),
                jnp.concatenate([at_lane, at_lane], axis=1),
                NT,
                preferred_element_type=jnp.float32,
            )
            dense.append(values.reshape(cells, channels, lanes))
        high, low = split_bf16(jnp.concatenate(dense, axis=1))
        rows = pl.ds(pl.multiple_of(step * 2 * channels, 2 * channels), 2 * channels)
        for cell in range(cells):
            high_out[rows, cell * lanes : (cell + 1) * lanes] = high[cell]
            low_out[rows, cell * lanes : (cell + 1) * lanes] = low[cell]
        return carry

    lax.fori_loop(0, shells * n_band * pairs, two_atoms, 0)


def build_projectors(n_band, n_sub, place, offsets, coefs, cells, lanes):
    atoms, shells, channels, spread = coefs.shape
    rows = atoms // n_sub * shells * channels
    shape = jax.ShapeDtypeStruct((rows, cells * lanes), jnp.bfloat16)
    return pl.pallas_call(
        functools.partial(projector_kernel, n_band, n_sub),
        out_shape=[shape, shape],
        in_specs=[SMEM, VMEM, VMEM],
        out_specs=[VMEM, VMEM],
        compiler_params=params(8),
        cost_estimate=pl.CostEstimate(
            flops=4 * rows * cells * lanes * spread,
            bytes_accessed=8 * rows * cells * lanes,
            transcendentals=0,
        ),
        name="projectors",
    )(place, offsets.swapaxes(0, 1), coefs)


def product_kernel(spots, n_sub, first_row, n_blocks, with_grid, place, w_high, w_low, *refs):
    refs, proj_out = refs[:-1], refs[-1]
    n_outs = n_blocks + (1 if with_grid else 0)
    arrays, outs = refs[:-n_outs], list(refs[-n_outs:])
    rows, orbitals = proj_out.shape
    cells, _, lanes = arrays[0].shape
    block = 12

    def parts(start):
        highs, lows = [], []
        for at, first, width in spots:
            high, low = split_bf16(arrays[at][pl.ds(start, block), first : first + width])
            highs.append(jnp.concatenate([high[k] for k in range(block)], axis=1))
            lows.append(jnp.concatenate([low[k] for k in range(block)], axis=1))
        return jnp.concatenate(highs, axis=0), jnp.concatenate(lows, axis=0)

    def product(left_high, left_low, high, low):
        right = jnp.concatenate([high, low], axis=0)
        wide = lax.dot_general(left_high, right, NT, preferred_element_type=jnp.float32)
        narrow = lax.dot_general(left_low, high, NT, preferred_element_type=jnp.float32)
        return wide[:, :orbitals] + wide[:, orbitals:] + narrow

    if with_grid:
        grid_out = outs.pop(0)
        grid_out[...] = jnp.zeros_like(grid_out)

        def grid_block(step, carry):
            high, low = parts(place[SUB] * (cells // n_sub) + step * block)
            grid_out[...] += product(high, low, high, low)
            return carry

        lax.fori_loop(0, cells // (n_sub * block), grid_block, 0)

    def proj_block(step, carry):
        high, low = parts(step * block)
        depth = block * lanes
        here = pl.ds(pl.multiple_of(step * depth, depth), depth)
        some = slice(first_row, first_row + rows)
        proj_out[...] += product(w_high[some, here], w_low[some, here], high, low)
        return carry

    proj_out[...] = jnp.zeros_like(proj_out)
    lax.fori_loop(0, cells // block, proj_block, 0)
    for k, out in enumerate(outs):
        out[...] = proj_out[k * (rows // n_blocks) : (k + 1) * (rows // n_blocks), :]


def products(n_sub, first_row, rows, n_blocks, with_grid, place, projectors, arrays, spots):
    orbitals = sum(width for _, _, width in spots)
    grid = [jax.ShapeDtypeStruct((orbitals, orbitals), jnp.float32)] if with_grid else []
    block = jax.ShapeDtypeStruct((rows // n_blocks, orbitals), jnp.float32)
    flops = 12 * rows * orbitals * projectors[0].shape[1]
    return pl.pallas_call(
        functools.partial(product_kernel, spots, n_sub, first_row, n_blocks, with_grid),
        out_shape=grid + [block] * n_blocks,
        in_specs=[SMEM] + [VMEM] * (2 + len(arrays)),
        out_specs=[VMEM] * (len(grid) + n_blocks),
        scratch_shapes=[pltpu.VMEM((rows, orbitals), jnp.float32)],
        compiler_params=params(8),
        cost_estimate=pl.CostEstimate(
            flops=flops, bytes_accessed=4 * rows * projectors[0].shape[1], transcendentals=0
        ),
        name="products",
    )(place, *projectors, *arrays)


def reordered(x, width, by):
    span = width * by
    column = lax.broadcasted_iota(jnp.int32, x.shape, 1)
    up, down = pltpu.roll(x, span, 1), pltpu.roll(x, x.shape[1] - span, 1)
    return jnp.where((column & span) == 0, down, up)


def gram_kernel(scales, groups, seen, place, corr_ref, grid_ref, proj_ref, *refs):
    sums, outs = refs[: len(seen)], refs[len(seen) :]
    orbitals = grid_ref.shape[0]
    width = orbitals // groups
    bits = [1 << k for k in range(groups.bit_length() - 1)]
    projections = proj_ref[...]
    for part, by in zip(sums, seen):
        columns = part[...]
        for bit in bits:
            if by & bit:
                columns = reordered(columns, width, bit)
        projections += columns
    highest = lax.Precision.HIGHEST
    weighted = jnp.dot(
        corr_ref[...], projections, precision=highest, preferred_element_type=jnp.float32
    )
    atom_part = lax.dot_general(
        projections, weighted, TN, precision=highest, preferred_element_type=jnp.float32
    )
    share = grid_ref[...] * scales[0] + atom_part * scales[1]
    for bit in bits:
        share = jnp.where((place[GROUP] & bit) != 0, reordered(share, width, bit), share)
    for k, out in enumerate(outs):
        out[...] = share[k * width : (k + 1) * width]


def gram_share(scales, groups, seen, place, corr, grid_part, proj, sums):
    rows = jax.ShapeDtypeStruct((grid_part.shape[0] // groups, grid_part.shape[1]), jnp.float32)
    return pl.pallas_call(
        functools.partial(gram_kernel, scales, groups, seen),
        out_shape=[rows] * groups,
        in_specs=[SMEM] + [VMEM] * (3 + len(sums)),
        out_specs=[VMEM] * groups,
        compiler_params=params(8),
        name="gram_share",
    )(place, corr, grid_part, proj, *sums)


def added(terms):
    while len(terms) > 1:
        terms = [a + b for a, b in zip(terms[::2], terms[1::2])]
    return terms[0]


def whole_columns(panel, potential, place, me):
    n_dom = lax.axis_size("dom")
    orbitals, planes, rows, lanes = panel.shape
    cells = planes * rows
    flat = panel.reshape(orbitals * cells, lanes)
    levels = potential.reshape(cells, lanes)
    size = TOGETHER * cells
    n_chunks = orbitals // (n_dom * TOGETHER)

    def block(c, m):
        return lax.dynamic_slice_in_dim(flat, (c * n_dom + (me ^ m)) * size, size, 0)

    def sent(x, m):
        return swapped(x, "dom", n_dom, m)

    own = []
    for m in range(n_dom):
        blocks = [block(c, m) for c in range(n_chunks)]
        blocks[0] = jnp.concatenate([blocks[0], levels], axis=0)
        own.append(blocks)
    near = sent(jnp.concatenate(own[1], axis=0), 1)
    arrived = [[own[0][0], near] + [sent(own[m][0], m) for m in range(2, n_dom)]]
    for c in range(1, n_chunks):
        far = [own[m][c] for m in range(2, n_dom)]
        near, far = lax.optimization_barrier((near, far))
        arrived.append([own[0][c], near] + [sent(x, m) for m, x in enumerate(far, start=2)])
    diagonal = None
    done = []
    for c, blocks in enumerate(arrived):
        starts = [0] * n_dom
        starts[1] = c * size + (cells if c else 0)
        filtered = filter_orbitals(place, diagonal, blocks, starts, planes, rows)
        if diagonal is None:
            diagonal = filtered[n_dom]
        done.append(filtered[:n_dom])
    return [
        [(sent(x, m) if m else x).reshape(size, lanes) for m, x in enumerate(blocks)]
        for blocks in done
    ]


def plane_by_plane(panel, potential):
    n_dom = lax.axis_size("dom")
    diagonal = (potential + (SHIFT - CENTER_LEVEL)) * (2.0 / HALF_WIDTH)

    def twice_operator(field):
        low, high = shifted(field[:, -1:], -1), shifted(field[:, :1], 1)
        extended = jnp.concatenate([low, field, high], axis=1)
        near = extended[:, 2:] + extended[:, :-2]
        near += jnp.roll(field, 1, axis=2) + jnp.roll(field, -1, axis=2)
        padded = jnp.pad(field, ((0, 0), (0, 0), (0, 0), (1, 1)))
        near += padded[..., 2:] + padded[..., :-2]
        return diagonal * field - near / HALF_WIDTH

    def one_step(_, carry):
        before, current = carry
        return current, twice_operator(current) - before

    start = (panel, 0.5 * twice_operator(panel))
    return lax.fori_loop(0, DEGREE - 1, one_step, start)[1]


def on_device(panel, potential, point_offsets, point_coefs, correlation):
    orbitals, planes, rows, lanes = panel.shape
    n_dom, n_band, n_sub = (lax.axis_size(axis) for axis in ("dom", "band", "sub"))
    groups = n_band * n_sub
    me, band, sub = (lax.axis_index(axis) for axis in ("dom", "band", "sub"))
    place = jnp.stack([me, band, sub, band * n_sub + sub]).astype(jnp.int32)

    cells = planes * rows
    share = cells // n_band
    channels = correlation.shape[1]
    own_atoms = point_offsets.shape[0] // groups
    own_corr = lax.dynamic_slice_in_dim(
        correlation, (sub * n_band + band) * own_atoms, own_atoms, 0
    )
    same_atom = jnp.eye(own_atoms, dtype=jnp.float32)
    corr_matrix = (same_atom[:, None, :, None] * own_corr[:, :, None, :]).reshape(
        own_atoms * channels, own_atoms * channels
    )

    place, corr_matrix = lax.optimization_barrier((place, corr_matrix))

    def build(offsets):
        return build_projectors(n_band, n_sub, place, offsets, point_coefs, share, lanes)

    if n_dom in (2, 4) and orbitals % (n_dom * TOGETHER) == 0 and planes * n_dom % 2 == 0:
        chunks = whole_columns(panel, potential, place, me)
        chunks[-1][0], point_offsets = lax.optimization_barrier((chunks[-1][0], point_offsets))
        projectors = build(point_offsets)
        chunks[0], projectors = lax.optimization_barrier((chunks[0], projectors))
        filtered = orbital_first(place, n_dom, [piece for pieces in chunks for piece in pieces])
        parts = [cell_first(place, n_band, pieces) for pieces in chunks]
    else:
        projectors = build(point_offsets)
        filtered = plane_by_plane(panel, potential)
        by_cell = filtered.reshape(orbitals, cells, lanes).swapaxes(0, 1)
        parts = [
            [
                lax.dynamic_slice_in_dim(by_cell, (band ^ m) * share, share, 0)
                for m in range(n_band)
            ]
        ]
    filtered = filtered.reshape(panel.shape)
    chunks = len(parts)
    arrays = [x for by_band in parts for x in by_band[:1]]
    arrays += [
        swapped(by_band[m], "band", n_band, m) for by_band in parts for m in range(1, n_band)
    ]
    arrays[chunks], filtered = lax.optimization_barrier((arrays[chunks], filtered))
    pieces = [jnp.concatenate(arrays[:chunks], axis=1)] + arrays[chunks:]
    arrays += [swapped(x, "sub", n_sub, k) for k in range(1, n_sub) for x in pieces]
    width = arrays[0].shape[1]
    spots = []
    for m in range(n_band):
        for k in range(n_sub):
            for c in range(chunks):
                at = chunks + c * (n_band - 1) + m - 1 if m else c
                if k == 0:
                    spots.append((at, 0, width))
                else:
                    base = chunks * n_band + (k - 1) * len(pieces)
                    if m:
                        spots.append((base + 1 + at - chunks, 0, width))
                    else:
                        spots.append((base, c * width, width))

    rows = own_atoms * channels
    n_sent = 3 * n_band - 1
    outgoing = products(
        n_sub, 0, n_sent * rows, n_sent, False, place, projectors, arrays, spots
    )
    outgoing, place = lax.optimization_barrier((outgoing, place))
    grid_part, own_proj = products(
        n_sub, n_sent * rows, rows, 1, True, place, projectors, arrays, spots
    )
    sums, seen = [], []
    to = [(by, m) for by in (1, -1) for m in range(n_band)]
    to += [(0, m) for m in range(n_band - 1, 0, -1)]
    for x, (by, m) in zip(outgoing, to):
        pairs = [
            (d * n_band + b, (d - by) % n_dom * n_band + (b ^ m))
            for d in range(n_dom)
            for b in range(n_band)
        ]
        seen.append(m * n_sub)
        sums.append(lax.ppermute(x, ("dom", "band"), pairs))
    scale_point = 1.0 / (cells * lanes * n_dom)
    scale_atom = 1.0 / math.sqrt(own_atoms * groups * n_dom)
    shares = gram_share(
        (scale_point, scale_atom), groups, seen, place, corr_matrix, grid_part, own_proj, sums
    )
    gram_rows = added(
        [swapped(x, ("band", "sub"), groups, m) if m else x for m, x in enumerate(shares)]
    )
    if n_dom <= 4:
        gram_rows = added(
            [swapped(gram_rows, "dom", n_dom, m) if m else gram_rows for m in range(n_dom)]
        )
    else:
        by = 1
        while by < n_dom:
            gram_rows += swapped(gram_rows, "dom", n_dom, by)
            by *= 2
    return filtered, gram_rows


def solution(mesh):
    placed = (
        P(("slab", "band", "sub"), "dom", None, None),
        P(("slab", "dom"), None, None),
        P(("slab", "dom"), None, None),
        P(("slab", "dom"), None, None, None),
        P(("slab", "dom"), None, None),
    )
    return jax.shard_map(
        on_device,
        mesh=mesh,
        in_specs=placed,
        out_specs=(P(("slab", "band", "sub"), "dom", None, None), P(("slab", "band", "sub"), None)),
        check_vma=False,
    )
```

```python
import functools
import math

import jax
import jax.numpy as jnp
from jax import lax
from jax.experimental import pallas as pl
from jax.experimental.pallas import tpu as pltpu
from jax.sharding import PartitionSpec as P

DEGREE = 12

CENTER_LEVEL = 3.6
HALF_WIDTH = 3.4
SHIFT = 3.0

TOGETHER = 4
SUBLANES = 8
ME, BAND, SUB, GROUP = range(4)
MIB = 1024 * 1024

VMEM = pl.BlockSpec(memory_space=pltpu.VMEM)
SMEM = pl.BlockSpec(memory_space=pltpu.SMEM)
NT = (((1,), (1,)), ((), ()))
TN = (((0,), (0,)), ((), ()))


def params(mib):
    return pltpu.CompilerParams(vmem_limit_bytes=mib * MIB)


def split_bf16(x):
    high = x.astype(jnp.bfloat16)
    return high, (x - high.astype(jnp.float32)).astype(jnp.bfloat16)


def shifted(x, by):
    size = lax.axis_size("dom")
    return lax.ppermute(x, "dom", [(i, (i - by) % size) for i in range(size)])


def swapped(x, axes, size, by):
    return lax.ppermute(x, axes, [(i, i ^ by) for i in range(size)])


def filter_kernel(n_dom, planes, rows, starts, first, n_levels, place, *refs):
    levels, refs = refs[:n_levels], list(refs[n_levels:])
    given = None if first else refs.pop(0)
    ins, outs = refs[:n_dom], refs[n_dom : 2 * n_dom]
    refs = refs[2 * n_dom :]
    diagonal = refs.pop(0) if first else given
    even, odd = refs
    half_planes = n_dom * planes // 2
    cells = planes * rows
    lanes = even.shape[3]
    scale = 1.0 / HALF_WIDTH
    mirrored = (place[ME] & 1) != 0
    plane_at = [jnp.where(mirrored, planes - 1 - i, i) for i in range(planes)]

    for x in range(half_planes):
        for half in range(2):
            m, i = divmod(half * half_planes + x, planes)
            part = slice(half * TOGETHER, (half + 1) * TOGETHER)
            base = starts[m] + plane_at[i] * rows
            for y in range(rows):
                even[x, y, part] = ins[m][pl.ds(base + y, TOGETHER, stride=cells), :]
                if first:
                    if m >= 3:
                        level = levels[m - 3][pl.ds(plane_at[i] * rows + y, 1), :]
                    else:
                        level = ins[m][pl.ds(base + (TOGETHER * cells + y), 1), :]
                    diagonal[x, y, part] = jnp.broadcast_to(
                        (level + (SHIFT - CENTER_LEVEL)) * (2.0 * scale), (TOGETHER, lanes)
                    )

    block = SUBLANES
    lane = lax.broadcasted_iota(jnp.int32, (block, SUBLANES, lanes), 2)
    at_start, at_end = lane == 0, lane == lanes - 1

    def twice_operator(source, x, y):
        here = slice(y, y + block)
        centre = source[x, here]
        if x == 0:
            near = pltpu.roll(source[half_planes - 1, here], TOGETHER, 1) + source[x + 1, here]
        elif x == half_planes - 1:
            near = pltpu.roll(source[0, here], TOGETHER, 1) + source[x - 1, here]
        else:
            near = source[x - 1, here] + source[x + 1, here]
        before = (y - 1) % rows
        after = (y + block) % rows
        near += jnp.concatenate([source[x, before : before + 1], centre[:-1]], axis=0)
        near += jnp.concatenate([centre[1:], source[x, after : after + 1]], axis=0)
        low = pltpu.roll(centre, 1, 2)
        high = pltpu.roll(centre, lanes - 1, 2)
        near += jnp.where(at_start, high, jnp.where(at_end, low, low + high))
        return diagonal[x, here] * centre - scale * near

    places = [(x, y) for x in range(half_planes) for y in range(0, rows, block)]

    def next_field(source, target):
        for x, y in places:
            target[x, y : y + block] = twice_operator(source, x, y) - target[x, y : y + block]

    for x, y in places:
        odd[x, y : y + block] = 0.5 * twice_operator(even, x, y)
    next_field(odd, even)

    def two_steps(_, carry):
        next_field(even, odd)
        next_field(odd, even)
        return carry

    lax.fori_loop(0, DEGREE // 2 - 1, two_steps, 0)
    for m in range(n_dom):
        for i in range(planes):
            half, x = divmod(m * planes + i, half_planes)
            part = slice(half * TOGETHER, (half + 1) * TOGETHER)
            for y in range(rows):
                here = slice(y * TOGETHER, (y + 1) * TOGETHER)
                outs[m][plane_at[i], here, :] = even[x, y, part]


def filter_orbitals(place, diagonal, levels, blocks, starts, planes, rows):
    n_dom = len(blocks)
    first = diagonal is None
    lanes = blocks[0].shape[1]
    field = (n_dom * planes // 2, rows, SUBLANES, lanes)
    out = jax.ShapeDtypeStruct((planes, rows * TOGETHER, lanes), jnp.float32)
    extra = [jax.ShapeDtypeStruct(field, jnp.float32)] if first else []
    given = [] if first else [diagonal]
    size = n_dom * planes * rows * TOGETHER * lanes
    return pl.pallas_call(
        functools.partial(filter_kernel, n_dom, planes, rows, starts, first, len(levels)),
        out_shape=[out] * n_dom + extra,
        in_specs=[SMEM] + [VMEM] * (len(levels) + n_dom + len(given)),
        out_specs=[VMEM] * (n_dom + len(extra)),
        scratch_shapes=[pltpu.VMEM(field, jnp.float32)] * 2,
        compiler_params=params(8),
        cost_estimate=pl.CostEstimate(
            flops=12 * DEGREE * size, bytes_accessed=8 * size, transcendentals=0
        ),
        name="chebyshev",
    )(place, *levels, *given, *blocks)


def cell_first_kernel(n_band, place, *refs):
    pieces, parts = refs[:-n_band], refs[-n_band:]
    share = parts[0].shape[0]
    me = place[ME]
    together = SUBLANES // TOGETHER
    tiles = len(pieces) // together
    for p, part in enumerate(parts):
        base = pl.multiple_of((place[BAND] ^ p) * (share * TOGETHER), SUBLANES)
        for first in range(0, share, together):
            loaded = [piece[pl.ds(base + first * TOGETHER, SUBLANES), :] for piece in pieces]
            for k in range(together):
                here = slice(k * TOGETHER, (k + 1) * TOGETHER)
                for q in range(tiles):
                    tile = jnp.concatenate(
                        [loaded[q * together + i][here] for i in range(together)], axis=0
                    )
                    tile = jnp.where((me & 1) != 0, pltpu.roll(tile, TOGETHER, 0), tile)
                    if tiles == 1:
                        part[first + k] = tile
                    else:
                        row = pl.multiple_of((q ^ (me // together)) * SUBLANES, SUBLANES)
                        part[first + k, pl.ds(row, SUBLANES), :] = tile


def cell_first(place, n_band, pieces):
    rows, lanes = pieces[0].shape
    orbitals = len(pieces) * TOGETHER
    part = jax.ShapeDtypeStruct((rows // (TOGETHER * n_band), orbitals, lanes), jnp.float32)
    return pl.pallas_call(
        functools.partial(cell_first_kernel, n_band),
        out_shape=[part] * n_band,
        in_specs=[SMEM] + [VMEM] * len(pieces),
        out_specs=[VMEM] * n_band,
        compiler_params=params(8),
        name="cell_first",
    )(place, *pieces)


def orbital_first_kernel(n_dom, place, *refs):
    *pieces, out = refs
    cells = out.shape[1]
    for k, piece in enumerate(pieces):
        chunk, m = divmod(k, n_dom)
        start = (chunk * n_dom + (place[ME] ^ m)) * TOGETHER
        for t in range(TOGETHER):
            out[start + t] = piece[pl.ds(t, cells, stride=TOGETHER), :]


def orbital_first(place, n_dom, pieces):
    rows, lanes = pieces[0].shape
    shape = (len(pieces) * TOGETHER, rows // TOGETHER, lanes)
    return pl.pallas_call(
        functools.partial(orbital_first_kernel, n_dom),
        out_shape=jax.ShapeDtypeStruct(shape, jnp.float32),
        in_specs=[SMEM] + [VMEM] * len(pieces),
        out_specs=VMEM,
        compiler_params=params(8),
        name="orbital_first",
    )(place, *pieces)


def projector_kernel(n_band, n_sub, place, offsets_ref, coefs_ref, high_out, low_out):
    atoms, shells, channels, spread = coefs_ref.shape
    own = atoms // (n_band * n_sub)
    lanes = spread
    cells = high_out.shape[1] // lanes
    pairs = own // 2
    row_index = lax.broadcasted_iota(jnp.int32, (cells, channels, spread), 0)
    row_index += place[BAND] * cells
    lane_index = lax.broadcasted_iota(jnp.int32, (lanes, spread), 0)

    def two_atoms(step, carry):
        shell = lax.rem(2 * (step // (n_band * pairs)), shells)
        seen = (step // pairs) % n_band
        seen = jnp.where(shell == 1, n_band - 1 - seen, seen)
        band = place[BAND] ^ seen
        first_atom = (place[SUB] * n_band + band) * own + 2 * (step % pairs)
        dense = []
        for i in range(2):
            offsets = offsets_ref[shell, pl.ds(first_atom + i, 1), :]
            coefs = coefs_ref[first_atom + i, shell]
            at_row = row_index == (offsets // lanes)[None]
            at_row &= (offsets >= 0)[None]
            left = [
                jnp.where(at_row, part.astype(jnp.float32)[None], 0.0)
                .reshape(cells * channels, spread)
                .astype(jnp.bfloat16)
                for part in split_bf16(coefs)
            ]
            at_lane = jnp.where(lane_index == (offsets & (lanes - 1)), 1.0, 0.0)
            at_lane = at_lane.astype(jnp.bfloat16)
            values = lax.dot_general(
                jnp.concatenate(left, axis=1),
                jnp.concatenate([at_lane, at_lane], axis=1),
                NT,
                preferred_element_type=jnp.float32,
            )
            dense.append(values.reshape(cells, channels, lanes))
        high, low = split_bf16(jnp.concatenate(dense, axis=1))
        rows = pl.ds(pl.multiple_of(step * 2 * channels, 2 * channels), 2 * channels)
        for cell in range(cells):
            high_out[rows, cell * lanes : (cell + 1) * lanes] = high[cell]
            low_out[rows, cell * lanes : (cell + 1) * lanes] = low[cell]
        return carry

    lax.fori_loop(0, shells * n_band * pairs, two_atoms, 0)


def build_projectors(n_band, n_sub, place, offsets, coefs, cells, lanes):
    atoms, shells, channels, spread = coefs.shape
    rows = atoms // n_sub * shells * channels
    shape = jax.ShapeDtypeStruct((rows, cells * lanes), jnp.bfloat16)
    return pl.pallas_call(
        functools.partial(projector_kernel, n_band, n_sub),
        out_shape=[shape, shape],
        in_specs=[SMEM, VMEM, VMEM],
        out_specs=[VMEM, VMEM],
        compiler_params=params(8),
        cost_estimate=pl.CostEstimate(
            flops=4 * rows * cells * lanes * spread,
            bytes_accessed=8 * rows * cells * lanes,
            transcendentals=0,
        ),
        name="projectors",
    )(place, offsets.swapaxes(0, 1), coefs)


def product_kernel(spots, n_sub, first_row, n_blocks, with_grid, place, w_high, w_low, *refs):
    refs, proj_out = refs[:-1], refs[-1]
    n_outs = n_blocks + (1 if with_grid else 0)
    arrays, outs = refs[:-n_outs], list(refs[-n_outs:])
    rows, orbitals = proj_out.shape
    cells, _, lanes = arrays[0].shape
    block = 12

    def parts(start):
        highs, lows = [], []
        for at, first, width in spots:
            high, low = split_bf16(arrays[at][pl.ds(start, block), first : first + width])
            highs.append(jnp.concatenate([high[k] for k in range(block)], axis=1))
            lows.append(jnp.concatenate([low[k] for k in range(block)], axis=1))
        return jnp.concatenate(highs, axis=0), jnp.concatenate(lows, axis=0)

    def product(left_high, left_low, high, low):
        right = jnp.concatenate([high, low], axis=0)
        wide = lax.dot_general(left_high, right, NT, preferred_element_type=jnp.float32)
        narrow = lax.dot_general(left_low, high, NT, preferred_element_type=jnp.float32)
        return wide[:, :orbitals] + wide[:, orbitals:] + narrow

    if with_grid:
        grid_out = outs.pop(0)
        grid_out[...] = jnp.zeros_like(grid_out)

        def grid_block(step, carry):
            high, low = parts(place[SUB] * (cells // n_sub) + step * block)
            grid_out[...] += product(high, low, high, low)
            return carry

        lax.fori_loop(0, cells // (n_sub * block), grid_block, 0)

    def proj_block(step, carry):
        high, low = parts(step * block)
        depth = block * lanes
        here = pl.ds(pl.multiple_of(step * depth, depth), depth)
        some = slice(first_row, first_row + rows)
        proj_out[...] += product(w_high[some, here], w_low[some, here], high, low)
        return carry

    proj_out[...] = jnp.zeros_like(proj_out)
    lax.fori_loop(0, cells // block, proj_block, 0)
    for k, out in enumerate(outs):
        out[...] = proj_out[k * (rows // n_blocks) : (k + 1) * (rows // n_blocks), :]


def products(n_sub, first_row, rows, n_blocks, with_grid, place, projectors, arrays, spots):
    orbitals = sum(width for _, _, width in spots)
    grid = [jax.ShapeDtypeStruct((orbitals, orbitals), jnp.float32)] if with_grid else []
    block = jax.ShapeDtypeStruct((rows // n_blocks, orbitals), jnp.float32)
    flops = 12 * rows * orbitals * projectors[0].shape[1]
    return pl.pallas_call(
        functools.partial(product_kernel, spots, n_sub, first_row, n_blocks, with_grid),
        out_shape=grid + [block] * n_blocks,
        in_specs=[SMEM] + [VMEM] * (2 + len(arrays)),
        out_specs=[VMEM] * (len(grid) + n_blocks),
        scratch_shapes=[pltpu.VMEM((rows, orbitals), jnp.float32)],
        compiler_params=params(8),
        cost_estimate=pl.CostEstimate(
            flops=flops, bytes_accessed=4 * rows * projectors[0].shape[1], transcendentals=0
        ),
        name="products",
    )(place, *projectors, *arrays)


def reordered(x, width, by):
    span = width * by
    column = lax.broadcasted_iota(jnp.int32, x.shape, 1)
    up, down = pltpu.roll(x, span, 1), pltpu.roll(x, x.shape[1] - span, 1)
    return jnp.where((column & span) == 0, down, up)


def gram_kernel(scales, groups, seen, place, corr_ref, grid_ref, proj_ref, *refs):
    sums, outs = refs[: len(seen)], refs[len(seen) :]
    orbitals = grid_ref.shape[0]
    width = orbitals // groups
    bits = [1 << k for k in range(groups.bit_length() - 1)]
    projections = proj_ref[...]
    for part, by in zip(sums, seen):
        columns = part[...]
        for bit in bits:
            if by & bit:
                columns = reordered(columns, width, bit)
        projections += columns
    highest = lax.Precision.HIGHEST
    weighted = jnp.dot(
        corr_ref[...], projections, precision=highest, preferred_element_type=jnp.float32
    )
    atom_part = lax.dot_general(
        projections, weighted, TN, precision=highest, preferred_element_type=jnp.float32
    )
    share = grid_ref[...] * scales[0] + atom_part * scales[1]
    for bit in bits:
        share = jnp.where((place[GROUP] & bit) != 0, reordered(share, width, bit), share)
    for k, out in enumerate(outs):
        out[...] = share[k * width : (k + 1) * width]


def gram_share(scales, groups, seen, place, corr, grid_part, proj, sums):
    rows = jax.ShapeDtypeStruct((grid_part.shape[0] // groups, grid_part.shape[1]), jnp.float32)
    return pl.pallas_call(
        functools.partial(gram_kernel, scales, groups, seen),
        out_shape=[rows] * groups,
        in_specs=[SMEM] + [VMEM] * (3 + len(sums)),
        out_specs=[VMEM] * groups,
        compiler_params=params(8),
        name="gram_share",
    )(place, corr, grid_part, proj, *sums)


def added(terms):
    while len(terms) > 1:
        terms = [a + b for a, b in zip(terms[::2], terms[1::2])]
    return terms[0]


def whole_columns(panel, potential, place, me):
    n_dom = lax.axis_size("dom")
    orbitals, planes, rows, lanes = panel.shape
    cells = planes * rows
    flat = panel.reshape(orbitals * cells, lanes)
    levels = potential.reshape(cells, lanes)
    size = TOGETHER * cells
    n_chunks = orbitals // (n_dom * TOGETHER)

    def block(c, m):
        return lax.dynamic_slice_in_dim(flat, (c * n_dom + (me ^ m)) * size, size, 0)

    def sent(x, m):
        return swapped(x, "dom", n_dom, m)

    own = []
    for m in range(n_dom):
        blocks = [block(c, m) for c in range(n_chunks)]
        if m < 3:
            blocks[0] = jnp.concatenate([blocks[0], levels], axis=0)
        own.append(blocks)
    near = sent(jnp.concatenate(own[1], axis=0), 1)
    arrived = [[own[0][0], near] + [sent(own[m][0], m) for m in range(2, n_dom)]]
    handed_on = [sent(arrived[0][2][size:], 1)] if n_dom > 3 else []
    for c in range(1, n_chunks):
        far = [own[m][c] for m in range(2, n_dom)]
        near, far = lax.optimization_barrier((near, far))
        arrived.append([own[0][c], near] + [sent(x, m) for m, x in enumerate(far, start=2)])
    diagonal = None
    done = []
    for c, blocks in enumerate(arrived):
        starts = [0] * n_dom
        starts[1] = c * size + (cells if c else 0)
        filtered = filter_orbitals(
            place, diagonal, [] if c else handed_on, blocks, starts, planes, rows
        )
        if diagonal is None:
            diagonal = filtered[n_dom]
        done.append(filtered[:n_dom])
    return [
        [(sent(x, m) if m else x).reshape(size, lanes) for m, x in enumerate(blocks)]
        for blocks in done
    ]


def plane_by_plane(panel, potential):
    n_dom = lax.axis_size("dom")
    diagonal = (potential + (SHIFT - CENTER_LEVEL)) * (2.0 / HALF_WIDTH)

    def twice_operator(field):
        low, high = shifted(field[:, -1:], -1), shifted(field[:, :1], 1)
        extended = jnp.concatenate([low, field, high], axis=1)
        near = extended[:, 2:] + extended[:, :-2]
        near += jnp.roll(field, 1, axis=2) + jnp.roll(field, -1, axis=2)
        padded = jnp.pad(field, ((0, 0), (0, 0), (0, 0), (1, 1)))
        near += padded[..., 2:] + padded[..., :-2]
        return diagonal * field - near / HALF_WIDTH

    def one_step(_, carry):
        before, current = carry
        return current, twice_operator(current) - before

    start = (panel, 0.5 * twice_operator(panel))
    return lax.fori_loop(0, DEGREE - 1, one_step, start)[1]


def on_device(panel, potential, point_offsets, point_coefs, correlation):
    orbitals, planes, rows, lanes = panel.shape
    n_dom, n_band, n_sub = (lax.axis_size(axis) for axis in ("dom", "band", "sub"))
    groups = n_band * n_sub
    me, band, sub = (lax.axis_index(axis) for axis in ("dom", "band", "sub"))
    place = jnp.stack([me, band, sub, band * n_sub + sub]).astype(jnp.int32)

    cells = planes * rows
    share = cells // n_band
    channels = correlation.shape[1]
    own_atoms = point_offsets.shape[0] // groups
    own_corr = lax.dynamic_slice_in_dim(
        correlation, (sub * n_band + band) * own_atoms, own_atoms, 0
    )
    same_atom = jnp.eye(own_atoms, dtype=jnp.float32)
    corr_matrix = (same_atom[:, None, :, None] * own_corr[:, :, None, :]).reshape(
        own_atoms * channels, own_atoms * channels
    )

    place, corr_matrix = lax.optimization_barrier((place, corr_matrix))

    def build(offsets):
        return build_projectors(n_band, n_sub, place, offsets, point_coefs, share, lanes)

    if n_dom in (2, 4) and orbitals % (n_dom * TOGETHER) == 0 and planes * n_dom % 2 == 0:
        chunks = whole_columns(panel, potential, place, me)
        chunks[-1][0], point_offsets = lax.optimization_barrier((chunks[-1][0], point_offsets))
        projectors = build(point_offsets)
        chunks[0], projectors = lax.optimization_barrier((chunks[0], projectors))
        filtered = orbital_first(place, n_dom, [piece for pieces in chunks for piece in pieces])
        parts = [cell_first(place, n_band, pieces) for pieces in chunks]
    else:
        projectors = build(point_offsets)
        filtered = plane_by_plane(panel, potential)
        by_cell = filtered.reshape(orbitals, cells, lanes).swapaxes(0, 1)
        parts = [
            [
                lax.dynamic_slice_in_dim(by_cell, (band ^ m) * share, share, 0)
                for m in range(n_band)
            ]
        ]
    filtered = filtered.reshape(panel.shape)
    chunks = len(parts)
    arrays = [x for by_band in parts for x in by_band[:1]]
    arrays += [
        swapped(by_band[m], "band", n_band, m) for by_band in parts for m in range(1, n_band)
    ]
    arrays[chunks], filtered = lax.optimization_barrier((arrays[chunks], filtered))
    pieces = [jnp.concatenate(arrays[:chunks], axis=1)] + arrays[chunks:]
    arrays += [swapped(x, "sub", n_sub, k) for k in range(1, n_sub) for x in pieces]
    width = arrays[0].shape[1]
    spots = []
    for m in range(n_band):
        for k in range(n_sub):
            for c in range(chunks):
                at = chunks + c * (n_band - 1) + m - 1 if m else c
                if k == 0:
                    spots.append((at, 0, width))
                else:
                    base = chunks * n_band + (k - 1) * len(pieces)
                    if m:
                        spots.append((base + 1 + at - chunks, 0, width))
                    else:
                        spots.append((base, c * width, width))

    rows = own_atoms * channels
    n_sent = 3 * n_band - 1
    outgoing = products(
        n_sub, 0, n_sent * rows, n_sent, False, place, projectors, arrays, spots
    )
    outgoing, place = lax.optimization_barrier((outgoing, place))
    grid_part, own_proj = products(
        n_sub, n_sent * rows, rows, 1, True, place, projectors, arrays, spots
    )
    sums, seen = [], []
    to = [(by, m) for by in (1, -1) for m in range(n_band)]
    to += [(0, m) for m in range(n_band - 1, 0, -1)]
    for x, (by, m) in zip(outgoing, to):
        pairs = [
            (d * n_band + b, (d - by) % n_dom * n_band + (b ^ m))
            for d in range(n_dom)
            for b in range(n_band)
        ]
        seen.append(m * n_sub)
        sums.append(lax.ppermute(x, ("dom", "band"), pairs))
    scale_point = 1.0 / (cells * lanes * n_dom)
    scale_atom = 1.0 / math.sqrt(own_atoms * groups * n_dom)
    shares = gram_share(
        (scale_point, scale_atom), groups, seen, place, corr_matrix, grid_part, own_proj, sums
    )
    gram_rows = added(
        [swapped(x, ("band", "sub"), groups, m) if m else x for m, x in enumerate(shares)]
    )
    if n_dom <= 4:
        gram_rows = added(
            [swapped(gram_rows, "dom", n_dom, m) if m else gram_rows for m in range(n_dom)]
        )
    else:
        by = 1
        while by < n_dom:
            gram_rows += swapped(gram_rows, "dom", n_dom, by)
            by *= 2
    return filtered, gram_rows


def solution(mesh):
    placed = (
        P(("slab", "band", "sub"), "dom", None, None),
        P(("slab", "dom"), None, None),
        P(("slab", "dom"), None, None),
        P(("slab", "dom"), None, None, None),
        P(("slab", "dom"), None, None),
    )
    return jax.shard_map(
        on_device,
        mesh=mesh,
        in_specs=placed,
        out_specs=(P(("slab", "band", "sub"), "dom", None, None), P(("slab", "band", "sub"), None)),
        check_vma=False,
    )
```

```python
import functools
import math

import jax
import jax.numpy as jnp
from jax import lax
from jax.experimental import pallas as pl
from jax.experimental.pallas import tpu as pltpu
from jax.sharding import PartitionSpec as P

DEGREE = 12

CENTER_LEVEL = 3.6
HALF_WIDTH = 3.4
SHIFT = 3.0

TOGETHER = 4
SUBLANES = 8
ME, BAND, SUB, GROUP = range(4)
MIB = 1024 * 1024

VMEM = pl.BlockSpec(memory_space=pltpu.VMEM)
SMEM = pl.BlockSpec(memory_space=pltpu.SMEM)
NT = (((1,), (1,)), ((), ()))
TN = (((0,), (0,)), ((), ()))


def params(mib):
    return pltpu.CompilerParams(vmem_limit_bytes=mib * MIB)


def split_bf16(x):
    high = x.astype(jnp.bfloat16)
    return high, (x - high.astype(jnp.float32)).astype(jnp.bfloat16)


def shifted(x, by):
    size = lax.axis_size("dom")
    return lax.ppermute(x, "dom", [(i, (i - by) % size) for i in range(size)])


def swapped(x, axes, size, by):
    return lax.ppermute(x, axes, [(i, i ^ by) for i in range(size)])


def filter_kernel(n_dom, planes, rows, starts, first, n_levels, place, *refs):
    levels, refs = refs[:n_levels], list(refs[n_levels:])
    given = None if first else refs.pop(0)
    ins, outs = refs[:n_dom], refs[n_dom : 2 * n_dom]
    refs = refs[2 * n_dom :]
    diagonal = refs.pop(0) if first else given
    even, odd = refs
    half_planes = n_dom * planes // 2
    cells = planes * rows
    lanes = even.shape[3]
    scale = 1.0 / HALF_WIDTH
    mirrored = (place[ME] & 1) != 0
    plane_at = [jnp.where(mirrored, planes - 1 - i, i) for i in range(planes)]

    for x in range(half_planes):
        for half in range(2):
            m, i = divmod(half * half_planes + x, planes)
            part = slice(half * TOGETHER, (half + 1) * TOGETHER)
            base = starts[m] + plane_at[i] * rows
            for y in range(rows):
                even[x, y, part] = ins[m][pl.ds(base + y, TOGETHER, stride=cells), :]
                if first:
                    if m >= 3:
                        level = levels[m - 3][pl.ds(plane_at[i] * rows + y, 1), :]
                    else:
                        level = ins[m][pl.ds(base + (TOGETHER * cells + y), 1), :]
                    diagonal[x, y, part] = jnp.broadcast_to(
                        (level + (SHIFT - CENTER_LEVEL)) * (2.0 * scale), (TOGETHER, lanes)
                    )

    block = SUBLANES
    lane = lax.broadcasted_iota(jnp.int32, (block, SUBLANES, lanes), 2)
    at_start, at_end = lane == 0, lane == lanes - 1

    def twice_operator(source, x, y):
        here = slice(y, y + block)
        centre = source[x, here]
        if x == 0:
            near = pltpu.roll(source[half_planes - 1, here], TOGETHER, 1) + source[x + 1, here]
        elif x == half_planes - 1:
            near = pltpu.roll(source[0, here], TOGETHER, 1) + source[x - 1, here]
        else:
            near = source[x - 1, here] + source[x + 1, here]
        before = (y - 1) % rows
        after = (y + block) % rows
        near += jnp.concatenate([source[x, before : before + 1], centre[:-1]], axis=0)
        near += jnp.concatenate([centre[1:], source[x, after : after + 1]], axis=0)
        low = pltpu.roll(centre, 1, 2)
        high = pltpu.roll(centre, lanes - 1, 2)
        near += jnp.where(at_start, high, jnp.where(at_end, low, low + high))
        return diagonal[x, here] * centre - scale * near

    places = [(x, y) for x in range(half_planes) for y in range(0, rows, block)]

    def next_field(source, target):
        for x, y in places:
            target[x, y : y + block] = twice_operator(source, x, y) - target[x, y : y + block]

    for x, y in places:
        odd[x, y : y + block] = 0.5 * twice_operator(even, x, y)
    next_field(odd, even)

    def two_steps(_, carry):
        next_field(even, odd)
        next_field(odd, even)
        return carry

    lax.fori_loop(0, DEGREE // 2 - 1, two_steps, 0)
    for m in range(n_dom):
        for i in range(planes):
            half, x = divmod(m * planes + i, half_planes)
            part = slice(half * TOGETHER, (half + 1) * TOGETHER)
            for y in range(rows):
                here = slice(y * TOGETHER, (y + 1) * TOGETHER)
                outs[m][plane_at[i], here, :] = even[x, y, part]


def filter_orbitals(place, diagonal, levels, blocks, starts, planes, rows):
    n_dom = len(blocks)
    first = diagonal is None
    lanes = blocks[0].shape[1]
    field = (n_dom * planes // 2, rows, SUBLANES, lanes)
    out = jax.ShapeDtypeStruct((planes, rows * TOGETHER, lanes), jnp.float32)
    extra = [jax.ShapeDtypeStruct(field, jnp.float32)] if first else []
    given = [] if first else [diagonal]
    size = n_dom * planes * rows * TOGETHER * lanes
    return pl.pallas_call(
        functools.partial(filter_kernel, n_dom, planes, rows, starts, first, len(levels)),
        out_shape=[out] * n_dom + extra,
        in_specs=[SMEM] + [VMEM] * (len(levels) + n_dom + len(given)),
        out_specs=[VMEM] * (n_dom + len(extra)),
        scratch_shapes=[pltpu.VMEM(field, jnp.float32)] * 2,
        compiler_params=params(8),
        cost_estimate=pl.CostEstimate(
            flops=12 * DEGREE * size, bytes_accessed=8 * size, transcendentals=0
        ),
        name="chebyshev",
    )(place, *levels, *given, *blocks)


def cell_first_kernel(n_band, place, *refs):
    pieces, parts = refs[:-n_band], refs[-n_band:]
    share = parts[0].shape[0]
    me = place[ME]
    together = SUBLANES // TOGETHER
    tiles = len(pieces) // together
    for p, part in enumerate(parts):
        base = pl.multiple_of((place[BAND] ^ p) * (share * TOGETHER), SUBLANES)
        for first in range(0, share, together):
            loaded = [piece[pl.ds(base + first * TOGETHER, SUBLANES), :] for piece in pieces]
            for k in range(together):
                here = slice(k * TOGETHER, (k + 1) * TOGETHER)
                for q in range(tiles):
                    tile = jnp.concatenate(
                        [loaded[q * together + i][here] for i in range(together)], axis=0
                    )
                    tile = jnp.where((me & 1) != 0, pltpu.roll(tile, TOGETHER, 0), tile)
                    if tiles == 1:
                        part[first + k] = tile
                    else:
                        row = pl.multiple_of((q ^ (me // together)) * SUBLANES, SUBLANES)
                        part[first + k, pl.ds(row, SUBLANES), :] = tile


def cell_first(place, n_band, pieces):
    rows, lanes = pieces[0].shape
    orbitals = len(pieces) * TOGETHER
    part = jax.ShapeDtypeStruct((rows // (TOGETHER * n_band), orbitals, lanes), jnp.float32)
    return pl.pallas_call(
        functools.partial(cell_first_kernel, n_band),
        out_shape=[part] * n_band,
        in_specs=[SMEM] + [VMEM] * len(pieces),
        out_specs=[VMEM] * n_band,
        compiler_params=params(8),
        name="cell_first",
    )(place, *pieces)


def orbital_first_kernel(n_dom, place, *refs):
    *pieces, out = refs
    cells = out.shape[1]
    for k, piece in enumerate(pieces):
        chunk, m = divmod(k, n_dom)
        start = (chunk * n_dom + (place[ME] ^ m)) * TOGETHER
        for t in range(TOGETHER):
            out[start + t] = piece[pl.ds(t, cells, stride=TOGETHER), :]


def orbital_first(place, n_dom, pieces):
    rows, lanes = pieces[0].shape
    shape = (len(pieces) * TOGETHER, rows // TOGETHER, lanes)
    return pl.pallas_call(
        functools.partial(orbital_first_kernel, n_dom),
        out_shape=jax.ShapeDtypeStruct(shape, jnp.float32),
        in_specs=[SMEM] + [VMEM] * len(pieces),
        out_specs=VMEM,
        compiler_params=params(8),
        name="orbital_first",
    )(place, *pieces)


def projector_kernel(n_band, n_sub, place, offsets_ref, coefs_ref, high_out, low_out):
    atoms, shells, channels, spread = coefs_ref.shape
    own = atoms // (n_band * n_sub)
    lanes = spread
    cells = high_out.shape[1] // lanes
    pairs = own // 2
    row_index = lax.broadcasted_iota(jnp.int32, (cells, channels, spread), 0)
    row_index += place[BAND] * cells
    lane_index = lax.broadcasted_iota(jnp.int32, (lanes, spread), 0)

    def two_atoms(step, carry):
        shell = lax.rem(2 * (step // (n_band * pairs)), shells)
        seen = (step // pairs) % n_band
        seen = jnp.where(shell == 1, n_band - 1 - seen, seen)
        band = place[BAND] ^ seen
        first_atom = (place[SUB] * n_band + band) * own + 2 * (step % pairs)
        dense = []
        for i in range(2):
            offsets = offsets_ref[shell, pl.ds(first_atom + i, 1), :]
            coefs = coefs_ref[first_atom + i, shell]
            at_row = row_index == (offsets // lanes)[None]
            at_row &= (offsets >= 0)[None]
            left = [
                jnp.where(at_row, part.astype(jnp.float32)[None], 0.0)
                .reshape(cells * channels, spread)
                .astype(jnp.bfloat16)
                for part in split_bf16(coefs)
            ]
            at_lane = jnp.where(lane_index == (offsets & (lanes - 1)), 1.0, 0.0)
            at_lane = at_lane.astype(jnp.bfloat16)
            values = lax.dot_general(
                jnp.concatenate(left, axis=1),
                jnp.concatenate([at_lane, at_lane], axis=1),
                NT,
                preferred_element_type=jnp.float32,
            )
            dense.append(values.reshape(cells, channels, lanes))
        high, low = split_bf16(jnp.concatenate(dense, axis=1))
        rows = pl.ds(pl.multiple_of(step * 2 * channels, 2 * channels), 2 * channels)
        for cell in range(cells):
            high_out[rows, cell * lanes : (cell + 1) * lanes] = high[cell]
            low_out[rows, cell * lanes : (cell + 1) * lanes] = low[cell]
        return carry

    lax.fori_loop(0, shells * n_band * pairs, two_atoms, 0)


def build_projectors(n_band, n_sub, place, offsets, coefs, cells, lanes):
    atoms, shells, channels, spread = coefs.shape
    rows = atoms // n_sub * shells * channels
    shape = jax.ShapeDtypeStruct((rows, cells * lanes), jnp.bfloat16)
    return pl.pallas_call(
        functools.partial(projector_kernel, n_band, n_sub),
        out_shape=[shape, shape],
        in_specs=[SMEM, VMEM, VMEM],
        out_specs=[VMEM, VMEM],
        compiler_params=params(8),
        cost_estimate=pl.CostEstimate(
            flops=4 * rows * cells * lanes * spread,
            bytes_accessed=8 * rows * cells * lanes,
            transcendentals=0,
        ),
        name="projectors",
    )(place, offsets.swapaxes(0, 1), coefs)


def product_kernel(spots, n_sub, first_row, n_blocks, with_grid, place, w_high, w_low, *refs):
    refs, proj_out = refs[:-1], refs[-1]
    n_outs = n_blocks + (1 if with_grid else 0)
    arrays, outs = refs[:-n_outs], list(refs[-n_outs:])
    rows, orbitals = proj_out.shape
    cells, _, lanes = arrays[0].shape
    block = 12

    def parts(start):
        highs, lows = [], []
        for at, first, width in spots:
            high, low = split_bf16(arrays[at][pl.ds(start, block), first : first + width])
            highs.append(jnp.concatenate([high[k] for k in range(block)], axis=1))
            lows.append(jnp.concatenate([low[k] for k in range(block)], axis=1))
        return jnp.concatenate(highs, axis=0), jnp.concatenate(lows, axis=0)

    def product(left_high, left_low, high, low):
        right = jnp.concatenate([high, low], axis=0)
        wide = lax.dot_general(left_high, right, NT, preferred_element_type=jnp.float32)
        narrow = lax.dot_general(left_low, high, NT, preferred_element_type=jnp.float32)
        return wide[:, :orbitals] + wide[:, orbitals:] + narrow

    if with_grid:
        grid_out = outs.pop(0)
        grid_out[...] = jnp.zeros_like(grid_out)

        def grid_block(step, carry):
            high, low = parts(place[SUB] * (cells // n_sub) + step * block)
            grid_out[...] += product(high, low, high, low)
            return carry

        lax.fori_loop(0, cells // (n_sub * block), grid_block, 0)

    def proj_block(step, carry):
        high, low = parts(step * block)
        depth = block * lanes
        here = pl.ds(pl.multiple_of(step * depth, depth), depth)
        some = slice(first_row, first_row + rows)
        proj_out[...] += product(w_high[some, here], w_low[some, here], high, low)
        return carry

    proj_out[...] = jnp.zeros_like(proj_out)
    lax.fori_loop(0, cells // block, proj_block, 0)
    for k, out in enumerate(outs):
        out[...] = proj_out[k * (rows // n_blocks) : (k + 1) * (rows // n_blocks), :]


def products(n_sub, first_row, rows, n_blocks, with_grid, place, projectors, arrays, spots):
    orbitals = sum(width for _, _, width in spots)
    grid = [jax.ShapeDtypeStruct((orbitals, orbitals), jnp.float32)] if with_grid else []
    block = jax.ShapeDtypeStruct((rows // n_blocks, orbitals), jnp.float32)
    flops = 12 * rows * orbitals * projectors[0].shape[1]
    return pl.pallas_call(
        functools.partial(product_kernel, spots, n_sub, first_row, n_blocks, with_grid),
        out_shape=grid + [block] * n_blocks,
        in_specs=[SMEM] + [VMEM] * (2 + len(arrays)),
        out_specs=[VMEM] * (len(grid) + n_blocks),
        scratch_shapes=[pltpu.VMEM((rows, orbitals), jnp.float32)],
        compiler_params=params(8),
        cost_estimate=pl.CostEstimate(
            flops=flops, bytes_accessed=4 * rows * projectors[0].shape[1], transcendentals=0
        ),
        name="products",
    )(place, *projectors, *arrays)


def reordered(x, width, by):
    span = width * by
    column = lax.broadcasted_iota(jnp.int32, x.shape, 1)
    up, down = pltpu.roll(x, span, 1), pltpu.roll(x, x.shape[1] - span, 1)
    return jnp.where((column & span) == 0, down, up)


def gram_kernel(scales, groups, seen, place, corr_ref, grid_ref, proj_ref, *refs):
    sums, outs = refs[: len(seen)], refs[len(seen) :]
    orbitals = grid_ref.shape[0]
    width = orbitals // groups
    bits = [1 << k for k in range(groups.bit_length() - 1)]
    projections = proj_ref[...]
    for part, by in zip(sums, seen):
        columns = part[...]
        for bit in bits:
            if by & bit:
                columns = reordered(columns, width, bit)
        projections += columns
    highest = lax.Precision.HIGHEST
    weighted = jnp.dot(
        corr_ref[...], projections, precision=highest, preferred_element_type=jnp.float32
    )
    atom_part = lax.dot_general(
        projections, weighted, TN, precision=highest, preferred_element_type=jnp.float32
    )
    share = grid_ref[...] * scales[0] + atom_part * scales[1]
    for bit in bits:
        share = jnp.where((place[GROUP] & bit) != 0, reordered(share, width, bit), share)
    for k, out in enumerate(outs):
        out[...] = share[k * width : (k + 1) * width]


def gram_share(scales, groups, seen, place, corr, grid_part, proj, sums):
    rows = jax.ShapeDtypeStruct((grid_part.shape[0] // groups, grid_part.shape[1]), jnp.float32)
    return pl.pallas_call(
        functools.partial(gram_kernel, scales, groups, seen),
        out_shape=[rows] * groups,
        in_specs=[SMEM] + [VMEM] * (3 + len(sums)),
        out_specs=[VMEM] * groups,
        compiler_params=params(8),
        name="gram_share",
    )(place, corr, grid_part, proj, *sums)


def added(terms):
    while len(terms) > 1:
        terms = [a + b for a, b in zip(terms[::2], terms[1::2])]
    return terms[0]


def whole_columns(panel, potential, place, me, build):
    n_dom = lax.axis_size("dom")
    orbitals, planes, rows, lanes = panel.shape
    cells = planes * rows
    flat = panel.reshape(orbitals * cells, lanes)
    levels = potential.reshape(cells, lanes)
    size = TOGETHER * cells
    n_chunks = orbitals // (n_dom * TOGETHER)

    def block(c, m):
        return lax.dynamic_slice_in_dim(flat, (c * n_dom + (me ^ m)) * size, size, 0)

    def sent(x, m):
        return swapped(x, "dom", n_dom, m)

    own = []
    for m in range(n_dom):
        blocks = [block(c, m) for c in range(n_chunks)]
        if m < 3:
            blocks[0] = jnp.concatenate([blocks[0], levels], axis=0)
        own.append(blocks)
    near = sent(jnp.concatenate(own[1], axis=0), 1)
    arrived = [[own[0][0], near] + [sent(own[m][0], m) for m in range(2, n_dom)]]
    handed_on = [sent(arrived[0][2][size:], 1)] if n_dom > 3 else []
    for c in range(1, n_chunks):
        far = [own[m][c] for m in range(2, n_dom)]
        near, far = lax.optimization_barrier((near, far))
        arrived.append([own[0][c], near] + [sent(x, m) for m, x in enumerate(far, start=2)])
    diagonal = None
    done = []
    for c, blocks in enumerate(arrived):
        starts = [0] * n_dom
        starts[1] = c * size + (cells if c else 0)
        filtered = filter_orbitals(
            place, diagonal, [] if c else handed_on, blocks, starts, planes, rows
        )
        if diagonal is None:
            diagonal = filtered[n_dom]
        done.append(list(filtered[:n_dom]))
        if c == 0:
            done[0][0], place = lax.optimization_barrier((done[0][0], place))
            place, projectors = lax.optimization_barrier((place, build(place)))
    return [
        [(sent(x, m) if m else x).reshape(size, lanes) for m, x in enumerate(blocks)]
        for blocks in done
    ], projectors


def plane_by_plane(panel, potential):
    n_dom = lax.axis_size("dom")
    diagonal = (potential + (SHIFT - CENTER_LEVEL)) * (2.0 / HALF_WIDTH)

    def twice_operator(field):
        low, high = shifted(field[:, -1:], -1), shifted(field[:, :1], 1)
        extended = jnp.concatenate([low, field, high], axis=1)
        near = extended[:, 2:] + extended[:, :-2]
        near += jnp.roll(field, 1, axis=2) + jnp.roll(field, -1, axis=2)
        padded = jnp.pad(field, ((0, 0), (0, 0), (0, 0), (1, 1)))
        near += padded[..., 2:] + padded[..., :-2]
        return diagonal * field - near / HALF_WIDTH

    def one_step(_, carry):
        before, current = carry
        return current, twice_operator(current) - before

    start = (panel, 0.5 * twice_operator(panel))
    return lax.fori_loop(0, DEGREE - 1, one_step, start)[1]


def on_device(panel, potential, point_offsets, point_coefs, correlation):
    orbitals, planes, rows, lanes = panel.shape
    n_dom, n_band, n_sub = (lax.axis_size(axis) for axis in ("dom", "band", "sub"))
    groups = n_band * n_sub
    me, band, sub = (lax.axis_index(axis) for axis in ("dom", "band", "sub"))
    place = jnp.stack([me, band, sub, band * n_sub + sub]).astype(jnp.int32)

    cells = planes * rows
    share = cells // n_band
    channels = correlation.shape[1]
    own_atoms = point_offsets.shape[0] // groups
    own_corr = lax.dynamic_slice_in_dim(
        correlation, (sub * n_band + band) * own_atoms, own_atoms, 0
    )
    same_atom = jnp.eye(own_atoms, dtype=jnp.float32)
    corr_matrix = (same_atom[:, None, :, None] * own_corr[:, :, None, :]).reshape(
        own_atoms * channels, own_atoms * channels
    )

    place, corr_matrix = lax.optimization_barrier((place, corr_matrix))

    def build(place):
        return build_projectors(n_band, n_sub, place, point_offsets, point_coefs, share, lanes)

    if n_dom in (2, 4) and orbitals % (n_dom * TOGETHER) == 0 and planes * n_dom % 2 == 0:
        chunks, projectors = whole_columns(panel, potential, place, me, build)
        filtered = orbital_first(place, n_dom, [piece for pieces in chunks for piece in pieces])
        parts = [cell_first(place, n_band, pieces) for pieces in chunks]
    else:
        projectors = build(place)
        filtered = plane_by_plane(panel, potential)
        by_cell = filtered.reshape(orbitals, cells, lanes).swapaxes(0, 1)
        parts = [
            [
                lax.dynamic_slice_in_dim(by_cell, (band ^ m) * share, share, 0)
                for m in range(n_band)
            ]
        ]
    filtered = filtered.reshape(panel.shape)
    chunks = len(parts)
    arrays = [x for by_band in parts for x in by_band[:1]]
    arrays += [
        swapped(by_band[m], "band", n_band, m) for by_band in parts for m in range(1, n_band)
    ]
    arrays[chunks], filtered = lax.optimization_barrier((arrays[chunks], filtered))
    pieces = [jnp.concatenate(arrays[:chunks], axis=1)] + arrays[chunks:]
    arrays += [swapped(x, "sub", n_sub, k) for k in range(1, n_sub) for x in pieces]
    width = arrays[0].shape[1]
    spots = []
    for m in range(n_band):
        for k in range(n_sub):
            for c in range(chunks):
                at = chunks + c * (n_band - 1) + m - 1 if m else c
                if k == 0:
                    spots.append((at, 0, width))
                else:
                    base = chunks * n_band + (k - 1) * len(pieces)
                    if m:
                        spots.append((base + 1 + at - chunks, 0, width))
                    else:
                        spots.append((base, c * width, width))

    rows = own_atoms * channels
    n_sent = 3 * n_band - 1
    outgoing = products(
        n_sub, 0, n_sent * rows, n_sent, False, place, projectors, arrays, spots
    )
    outgoing, place = lax.optimization_barrier((outgoing, place))
    grid_part, own_proj = products(
        n_sub, n_sent * rows, rows, 1, True, place, projectors, arrays, spots
    )
    sums, seen = [], []
    to = [(by, m) for by in (1, -1) for m in range(n_band)]
    to += [(0, m) for m in range(n_band - 1, 0, -1)]
    for x, (by, m) in zip(outgoing, to):
        pairs = [
            (d * n_band + b, (d - by) % n_dom * n_band + (b ^ m))
            for d in range(n_dom)
            for b in range(n_band)
        ]
        seen.append(m * n_sub)
        sums.append(lax.ppermute(x, ("dom", "band"), pairs))
    scale_point = 1.0 / (cells * lanes * n_dom)
    scale_atom = 1.0 / math.sqrt(own_atoms * groups * n_dom)
    shares = gram_share(
        (scale_point, scale_atom), groups, seen, place, corr_matrix, grid_part, own_proj, sums
    )
    gram_rows = added(
        [swapped(x, ("band", "sub"), groups, m) if m else x for m, x in enumerate(shares)]
    )
    if n_dom <= 4:
        gram_rows = added(
            [swapped(gram_rows, "dom", n_dom, m) if m else gram_rows for m in range(n_dom)]
        )
    else:
        by = 1
        while by < n_dom:
            gram_rows += swapped(gram_rows, "dom", n_dom, by)
            by *= 2
    return filtered, gram_rows


def solution(mesh):
    placed = (
        P(("slab", "band", "sub"), "dom", None, None),
        P(("slab", "dom"), None, None),
        P(("slab", "dom"), None, None),
        P(("slab", "dom"), None, None, None),
        P(("slab", "dom"), None, None),
    )
    return jax.shard_map(
        on_device,
        mesh=mesh,
        in_specs=placed,
        out_specs=(P(("slab", "band", "sub"), "dom", None, None), P(("slab", "band", "sub"), None)),
        check_vma=False,
    )
```

```python
import functools
import math

import jax
import jax.numpy as jnp
from jax import lax
from jax.experimental import pallas as pl
from jax.experimental.pallas import tpu as pltpu
from jax.sharding import PartitionSpec as P

DEGREE = 12

CENTER_LEVEL = 3.6
HALF_WIDTH = 3.4
SHIFT = 3.0

TOGETHER = 4
SUBLANES = 8
ME, BAND, SUB, GROUP = range(4)
MIB = 1024 * 1024

VMEM = pl.BlockSpec(memory_space=pltpu.VMEM)
SMEM = pl.BlockSpec(memory_space=pltpu.SMEM)
NT = (((1,), (1,)), ((), ()))
TN = (((0,), (0,)), ((), ()))


def params(mib):
    return pltpu.CompilerParams(vmem_limit_bytes=mib * MIB)


def split_bf16(x):
    high = x.astype(jnp.bfloat16)
    return high, (x - high.astype(jnp.float32)).astype(jnp.bfloat16)


def shifted(x, by):
    size = lax.axis_size("dom")
    return lax.ppermute(x, "dom", [(i, (i - by) % size) for i in range(size)])


def swapped(x, axes, size, by):
    return lax.ppermute(x, axes, [(i, i ^ by) for i in range(size)])


def filter_kernel(n_dom, planes, rows, starts, first, n_levels, place, *refs):
    levels, refs = refs[:n_levels], list(refs[n_levels:])
    given = None if first else refs.pop(0)
    ins, outs = refs[:n_dom], refs[n_dom : 2 * n_dom]
    refs = refs[2 * n_dom :]
    diagonal = refs.pop(0) if first else given
    even, odd = refs
    half_planes = n_dom * planes // 2
    cells = planes * rows
    lanes = even.shape[3]
    scale = 1.0 / HALF_WIDTH
    mirrored = (place[ME] & 1) != 0
    plane_at = [jnp.where(mirrored, planes - 1 - i, i) for i in range(planes)]

    for x in range(half_planes):
        for half in range(2):
            m, i = divmod(half * half_planes + x, planes)
            part = slice(half * TOGETHER, (half + 1) * TOGETHER)
            base = starts[m] + plane_at[i] * rows
            for y in range(rows):
                even[x, y, part] = ins[m][pl.ds(base + y, TOGETHER, stride=cells), :]
                if first:
                    if m >= 3:
                        level = levels[m - 3][pl.ds(plane_at[i] * rows + y, 1), :]
                    else:
                        level = ins[m][pl.ds(base + (TOGETHER * cells + y), 1), :]
                    diagonal[x, y, part] = jnp.broadcast_to(
                        (level + (SHIFT - CENTER_LEVEL)) * (2.0 * scale), (TOGETHER, lanes)
                    )

    block = SUBLANES
    lane = lax.broadcasted_iota(jnp.int32, (block, SUBLANES, lanes), 2)
    at_start, at_end = lane == 0, lane == lanes - 1

    def twice_operator(source, x, y):
        here = slice(y, y + block)
        centre = source[x, here]
        if x == 0:
            near = pltpu.roll(source[half_planes - 1, here], TOGETHER, 1) + source[x + 1, here]
        elif x == half_planes - 1:
            near = pltpu.roll(source[0, here], TOGETHER, 1) + source[x - 1, here]
        else:
            near = source[x - 1, here] + source[x + 1, here]
        before = (y - 1) % rows
        after = (y + block) % rows
        near += jnp.concatenate([source[x, before : before + 1], centre[:-1]], axis=0)
        near += jnp.concatenate([centre[1:], source[x, after : after + 1]], axis=0)
        low = pltpu.roll(centre, 1, 2)
        high = pltpu.roll(centre, lanes - 1, 2)
        near += jnp.where(at_start, high, jnp.where(at_end, low, low + high))
        return diagonal[x, here] * centre - scale * near

    places = [(x, y) for x in range(half_planes) for y in range(0, rows, block)]

    def next_field(source, target):
        for x, y in places:
            target[x, y : y + block] = twice_operator(source, x, y) - target[x, y : y + block]

    for x, y in places:
        odd[x, y : y + block] = 0.5 * twice_operator(even, x, y)
    next_field(odd, even)

    def two_steps(_, carry):
        next_field(even, odd)
        next_field(odd, even)
        return carry

    lax.fori_loop(0, DEGREE // 2 - 1, two_steps, 0)
    for m in range(n_dom):
        for i in range(planes):
            half, x = divmod(m * planes + i, half_planes)
            part = slice(half * TOGETHER, (half + 1) * TOGETHER)
            for y in range(rows):
                here = slice(y * TOGETHER, (y + 1) * TOGETHER)
                outs[m][plane_at[i], here, :] = even[x, y, part]


def filter_orbitals(place, diagonal, levels, blocks, starts, planes, rows):
    n_dom = len(blocks)
    first = diagonal is None
    lanes = blocks[0].shape[1]
    field = (n_dom * planes // 2, rows, SUBLANES, lanes)
    out = jax.ShapeDtypeStruct((planes, rows * TOGETHER, lanes), jnp.float32)
    extra = [jax.ShapeDtypeStruct(field, jnp.float32)] if first else []
    given = [] if first else [diagonal]
    size = n_dom * planes * rows * TOGETHER * lanes
    return pl.pallas_call(
        functools.partial(filter_kernel, n_dom, planes, rows, starts, first, len(levels)),
        out_shape=[out] * n_dom + extra,
        in_specs=[SMEM] + [VMEM] * (len(levels) + n_dom + len(given)),
        out_specs=[VMEM] * (n_dom + len(extra)),
        scratch_shapes=[pltpu.VMEM(field, jnp.float32)] * 2,
        compiler_params=params(8),
        cost_estimate=pl.CostEstimate(
            flops=12 * DEGREE * size, bytes_accessed=8 * size, transcendentals=0
        ),
        name="chebyshev",
    )(place, *levels, *given, *blocks)


def cell_first_kernel(n_band, place, *refs):
    pieces, parts = refs[:-n_band], refs[-n_band:]
    share = parts[0].shape[0]
    me = place[ME]
    together = SUBLANES // TOGETHER
    tiles = len(pieces) // together
    for p, part in enumerate(parts):
        base = pl.multiple_of((place[BAND] ^ p) * (share * TOGETHER), SUBLANES)
        for first in range(0, share, together):
            loaded = [piece[pl.ds(base + first * TOGETHER, SUBLANES), :] for piece in pieces]
            for k in range(together):
                here = slice(k * TOGETHER, (k + 1) * TOGETHER)
                for q in range(tiles):
                    tile = jnp.concatenate(
                        [loaded[q * together + i][here] for i in range(together)], axis=0
                    )
                    tile = jnp.where((me & 1) != 0, pltpu.roll(tile, TOGETHER, 0), tile)
                    if tiles == 1:
                        part[first + k] = tile
                    else:
                        row = pl.multiple_of((q ^ (me // together)) * SUBLANES, SUBLANES)
                        part[first + k, pl.ds(row, SUBLANES), :] = tile


def cell_first(place, n_band, pieces):
    rows, lanes = pieces[0].shape
    orbitals = len(pieces) * TOGETHER
    part = jax.ShapeDtypeStruct((rows // (TOGETHER * n_band), orbitals, lanes), jnp.float32)
    return pl.pallas_call(
        functools.partial(cell_first_kernel, n_band),
        out_shape=[part] * n_band,
        in_specs=[SMEM] + [VMEM] * len(pieces),
        out_specs=[VMEM] * n_band,
        compiler_params=params(8),
        name="cell_first",
    )(place, *pieces)


def orbital_first_kernel(n_dom, which, place, *refs):
    pieces, (out, laid_out, sems) = refs[: len(which)], refs[-3:]
    cells = out.shape[1]
    copies = []
    for k, (chunk, m) in enumerate(which):
        for t in range(TOGETHER):
            laid_out[k * TOGETHER + t] = pieces[k][pl.ds(t, cells, stride=TOGETHER), :]
        start = (chunk * n_dom + (place[ME] ^ m)) * TOGETHER
        copies.append(
            pltpu.make_async_copy(
                laid_out.at[pl.ds(k * TOGETHER, TOGETHER)],
                out.at[pl.ds(start, TOGETHER)],
                sems.at[k],
            )
        )
        copies[-1].start()
    for copy in copies:
        copy.wait()


def orbital_first(place, n_dom, orbitals, pieces, which, onto=None):
    rows, lanes = pieces[0].shape
    cells = rows // TOGETHER
    hbm = pl.BlockSpec(memory_space=pltpu.HBM)
    given = [] if onto is None else [onto]
    return pl.pallas_call(
        functools.partial(orbital_first_kernel, n_dom, which),
        out_shape=jax.ShapeDtypeStruct((orbitals, cells, lanes), jnp.float32),
        in_specs=[SMEM] + [VMEM] * len(pieces) + [hbm] * len(given),
        out_specs=hbm,
        input_output_aliases={len(pieces) + 1: 0} if given else {},
        scratch_shapes=[
            pltpu.VMEM((len(pieces) * TOGETHER, cells, lanes), jnp.float32),
            pltpu.SemaphoreType.DMA((len(pieces),)),
        ],
        compiler_params=params(8),
        name="orbital_first",
    )(place, *pieces, *given)


def projector_kernel(n_band, n_sub, place, offsets_ref, coefs_ref, high_out, low_out):
    atoms, shells, channels, spread = coefs_ref.shape
    own = atoms // (n_band * n_sub)
    lanes = spread
    cells = high_out.shape[1] // lanes
    pairs = own // 2
    row_index = lax.broadcasted_iota(jnp.int32, (cells, channels, spread), 0)
    row_index += place[BAND] * cells
    lane_index = lax.broadcasted_iota(jnp.int32, (lanes, spread), 0)

    def two_atoms(step, carry):
        shell = lax.rem(2 * (step // (n_band * pairs)), shells)
        seen = (step // pairs) % n_band
        seen = jnp.where(shell == 1, n_band - 1 - seen, seen)
        band = place[BAND] ^ seen
        first_atom = (place[SUB] * n_band + band) * own + 2 * (step % pairs)
        dense = []
        for i in range(2):
            offsets = offsets_ref[shell, pl.ds(first_atom + i, 1), :]
            coefs = coefs_ref[first_atom + i, shell]
            at_row = row_index == (offsets // lanes)[None]
            at_row &= (offsets >= 0)[None]
            left = [
                jnp.where(at_row, part.astype(jnp.float32)[None], 0.0)
                .reshape(cells * channels, spread)
                .astype(jnp.bfloat16)
                for part in split_bf16(coefs)
            ]
            at_lane = jnp.where(lane_index == (offsets & (lanes - 1)), 1.0, 0.0)
            at_lane = at_lane.astype(jnp.bfloat16)
            values = lax.dot_general(
                jnp.concatenate(left, axis=1),
                jnp.concatenate([at_lane, at_lane], axis=1),
                NT,
                preferred_element_type=jnp.float32,
            )
            dense.append(values.reshape(cells, channels, lanes))
        high, low = split_bf16(jnp.concatenate(dense, axis=1))
        rows = pl.ds(pl.multiple_of(step * 2 * channels, 2 * channels), 2 * channels)
        for cell in range(cells):
            high_out[rows, cell * lanes : (cell + 1) * lanes] = high[cell]
            low_out[rows, cell * lanes : (cell + 1) * lanes] = low[cell]
        return carry

    lax.fori_loop(0, shells * n_band * pairs, two_atoms, 0)


def build_projectors(n_band, n_sub, place, offsets, coefs, cells, lanes):
    atoms, shells, channels, spread = coefs.shape
    rows = atoms // n_sub * shells * channels
    shape = jax.ShapeDtypeStruct((rows, cells * lanes), jnp.bfloat16)
    return pl.pallas_call(
        functools.partial(projector_kernel, n_band, n_sub),
        out_shape=[shape, shape],
        in_specs=[SMEM, VMEM, VMEM],
        out_specs=[VMEM, VMEM],
        compiler_params=params(8),
        cost_estimate=pl.CostEstimate(
            flops=4 * rows * cells * lanes * spread,
            bytes_accessed=8 * rows * cells * lanes,
            transcendentals=0,
        ),
        name="projectors",
    )(place, offsets.swapaxes(0, 1), coefs)


def product_kernel(spots, n_sub, first_row, n_blocks, with_grid, place, w_high, w_low, *refs):
    refs, proj_out = refs[:-1], refs[-1]
    n_outs = n_blocks + (1 if with_grid else 0)
    arrays, outs = refs[:-n_outs], list(refs[-n_outs:])
    rows, orbitals = proj_out.shape
    cells, _, lanes = arrays[0].shape
    block = 12
    swap = (place[ME] & 2) != 0

    def parts(start):
        highs, lows = [], []
        for spot in spots:
            tiles = [
                arrays[at][pl.ds(start, block), first : first + width] for at, first, width in spot
            ]
            if len(tiles) == 2:
                near, far = tiles
                tiles = [jnp.where(swap, far, near), jnp.where(swap, near, far)]
            high, low = split_bf16(jnp.concatenate(tiles, axis=1))
            highs.append(jnp.concatenate([high[k] for k in range(block)], axis=1))
            lows.append(jnp.concatenate([low[k] for k in range(block)], axis=1))
        return jnp.concatenate(highs, axis=0), jnp.concatenate(lows, axis=0)

    def product(left_high, left_low, high, low):
        right = jnp.concatenate([high, low], axis=0)
        wide = lax.dot_general(left_high, right, NT, preferred_element_type=jnp.float32)
        narrow = lax.dot_general(left_low, high, NT, preferred_element_type=jnp.float32)
        return wide[:, :orbitals] + wide[:, orbitals:] + narrow

    if with_grid:
        grid_out = outs.pop(0)
        grid_out[...] = jnp.zeros_like(grid_out)

        def grid_block(step, carry):
            high, low = parts(place[SUB] * (cells // n_sub) + step * block)
            grid_out[...] += product(high, low, high, low)
            return carry

        lax.fori_loop(0, cells // (n_sub * block), grid_block, 0)

    def proj_block(step, carry):
        high, low = parts(step * block)
        depth = block * lanes
        here = pl.ds(pl.multiple_of(step * depth, depth), depth)
        some = slice(first_row, first_row + rows)
        proj_out[...] += product(w_high[some, here], w_low[some, here], high, low)
        return carry

    proj_out[...] = jnp.zeros_like(proj_out)
    lax.fori_loop(0, cells // block, proj_block, 0)
    for k, out in enumerate(outs):
        out[...] = proj_out[k * (rows // n_blocks) : (k + 1) * (rows // n_blocks), :]


def products(n_sub, first_row, rows, n_blocks, with_grid, place, projectors, arrays, spots):
    orbitals = sum(width for spot in spots for _, _, width in spot)
    grid = [jax.ShapeDtypeStruct((orbitals, orbitals), jnp.float32)] if with_grid else []
    block = jax.ShapeDtypeStruct((rows // n_blocks, orbitals), jnp.float32)
    flops = 12 * rows * orbitals * projectors[0].shape[1]
    return pl.pallas_call(
        functools.partial(product_kernel, spots, n_sub, first_row, n_blocks, with_grid),
        out_shape=grid + [block] * n_blocks,
        in_specs=[SMEM] + [VMEM] * (2 + len(arrays)),
        out_specs=[VMEM] * (len(grid) + n_blocks),
        scratch_shapes=[pltpu.VMEM((rows, orbitals), jnp.float32)],
        compiler_params=params(8),
        cost_estimate=pl.CostEstimate(
            flops=flops, bytes_accessed=4 * rows * projectors[0].shape[1], transcendentals=0
        ),
        name="products",
    )(place, *projectors, *arrays)


def reordered(x, width, by):
    span = width * by
    column = lax.broadcasted_iota(jnp.int32, x.shape, 1)
    up, down = pltpu.roll(x, span, 1), pltpu.roll(x, x.shape[1] - span, 1)
    return jnp.where((column & span) == 0, down, up)


def gram_kernel(scales, groups, seen, place, corr_ref, grid_ref, proj_ref, *refs):
    sums, outs = refs[: len(seen)], refs[len(seen) :]
    orbitals = grid_ref.shape[0]
    width = orbitals // groups
    bits = [1 << k for k in range(groups.bit_length() - 1)]
    projections = proj_ref[...]
    for part, by in zip(sums, seen):
        columns = part[...]
        for bit in bits:
            if by & bit:
                columns = reordered(columns, width, bit)
        projections += columns
    highest = lax.Precision.HIGHEST
    weighted = jnp.dot(
        corr_ref[...], projections, precision=highest, preferred_element_type=jnp.float32
    )
    atom_part = lax.dot_general(
        projections, weighted, TN, precision=highest, preferred_element_type=jnp.float32
    )
    share = grid_ref[...] * scales[0] + atom_part * scales[1]
    for bit in bits:
        share = jnp.where((place[GROUP] & bit) != 0, reordered(share, width, bit), share)
    for k, out in enumerate(outs):
        out[...] = share[k * width : (k + 1) * width]


def gram_share(scales, groups, seen, place, corr, grid_part, proj, sums):
    rows = jax.ShapeDtypeStruct((grid_part.shape[0] // groups, grid_part.shape[1]), jnp.float32)
    return pl.pallas_call(
        functools.partial(gram_kernel, scales, groups, seen),
        out_shape=[rows] * groups,
        in_specs=[SMEM] + [VMEM] * (3 + len(sums)),
        out_specs=[VMEM] * groups,
        compiler_params=params(8),
        name="gram_share",
    )(place, corr, grid_part, proj, *sums)


def added(terms):
    while len(terms) > 1:
        terms = [a + b for a, b in zip(terms[::2], terms[1::2])]
    return terms[0]


def whole_columns(panel, potential, place, me, build):
    n_dom = lax.axis_size("dom")
    orbitals, planes, rows, lanes = panel.shape
    cells = planes * rows
    flat = panel.reshape(orbitals * cells, lanes)
    levels = potential.reshape(cells, lanes)
    size = TOGETHER * cells
    n_chunks = orbitals // (n_dom * TOGETHER)

    def block(c, m):
        return lax.dynamic_slice_in_dim(flat, (c * n_dom + (me ^ m)) * size, size, 0)

    def sent(x, m):
        return swapped(x, "dom", n_dom, m)

    own = []
    for m in range(n_dom):
        blocks = [block(c, m) for c in range(n_chunks)]
        if m < 3:
            blocks[0] = jnp.concatenate([blocks[0], levels], axis=0)
        own.append(blocks)
    near = sent(jnp.concatenate(own[1], axis=0), 1)
    arrived = [[own[0][0], near] + [sent(own[m][0], m) for m in range(2, n_dom)]]
    handed_on = [sent(arrived[0][2][size:], 1)] if n_dom > 3 else []
    for c in range(1, n_chunks):
        far = [own[m][c] for m in range(2, n_dom)]
        near, far = lax.optimization_barrier((near, far))
        arrived.append([own[0][c], near] + [sent(x, m) for m, x in enumerate(far, start=2)])
    diagonal = None
    done = []
    for c, blocks in enumerate(arrived):
        starts = [0] * n_dom
        starts[1] = c * size + (cells if c else 0)
        filtered = filter_orbitals(
            place, diagonal, [] if c else handed_on, blocks, starts, planes, rows
        )
        if diagonal is None:
            diagonal = filtered[n_dom]
        done.append(list(filtered[:n_dom]))
        if c == 0:
            done[0][0], place = lax.optimization_barrier((done[0][0], place))
            place, projectors = lax.optimization_barrier((place, build(place)))
    return [
        [(sent(x, m) if m else x).reshape(size, lanes) for m, x in enumerate(blocks)]
        for blocks in done
    ], projectors


def plane_by_plane(panel, potential):
    n_dom = lax.axis_size("dom")
    diagonal = (potential + (SHIFT - CENTER_LEVEL)) * (2.0 / HALF_WIDTH)

    def twice_operator(field):
        low, high = shifted(field[:, -1:], -1), shifted(field[:, :1], 1)
        extended = jnp.concatenate([low, field, high], axis=1)
        near = extended[:, 2:] + extended[:, :-2]
        near += jnp.roll(field, 1, axis=2) + jnp.roll(field, -1, axis=2)
        padded = jnp.pad(field, ((0, 0), (0, 0), (0, 0), (1, 1)))
        near += padded[..., 2:] + padded[..., :-2]
        return diagonal * field - near / HALF_WIDTH

    def one_step(_, carry):
        before, current = carry
        return current, twice_operator(current) - before

    start = (panel, 0.5 * twice_operator(panel))
    return lax.fori_loop(0, DEGREE - 1, one_step, start)[1]


def on_device(panel, potential, point_offsets, point_coefs, correlation):
    orbitals, planes, rows, lanes = panel.shape
    n_dom, n_band, n_sub = (lax.axis_size(axis) for axis in ("dom", "band", "sub"))
    groups = n_band * n_sub
    me, band, sub = (lax.axis_index(axis) for axis in ("dom", "band", "sub"))
    place = jnp.stack([me, band, sub, band * n_sub + sub]).astype(jnp.int32)

    cells = planes * rows
    share = cells // n_band
    channels = correlation.shape[1]
    own_atoms = point_offsets.shape[0] // groups
    own_corr = lax.dynamic_slice_in_dim(
        correlation, (sub * n_band + band) * own_atoms, own_atoms, 0
    )
    same_atom = jnp.eye(own_atoms, dtype=jnp.float32)
    corr_matrix = (same_atom[:, None, :, None] * own_corr[:, :, None, :]).reshape(
        own_atoms * channels, own_atoms * channels
    )

    place, corr_matrix = lax.optimization_barrier((place, corr_matrix))

    def build(place):
        return build_projectors(n_band, n_sub, place, point_offsets, point_coefs, share, lanes)

    if n_dom in (2, 4) and orbitals % (n_dom * TOGETHER) == 0 and planes * n_dom % 2 == 0:
        chunks, projectors = whole_columns(panel, potential, place, me, build)
        sooner = place
        which = [(c, m) for c in range(len(chunks)) for m in range(n_dom)]
        pieces = [chunks[c][m] for c, m in which]
        n_late = 2 if n_dom == 4 else 0
        first = len(pieces) - n_late
        filtered = orbital_first(place, n_dom, orbitals, pieces[:first], which[:first])
        early, place = lax.optimization_barrier((filtered, place))
        if n_late:
            filtered = orbital_first(
                place, n_dom, orbitals, pieces[first:], which[first:], early
            )
        parts = [cell_first(sooner, n_band, pieces) for pieces in chunks[:-1]]
        tiles = [[c] for c in range(len(chunks))]
        last = [chunks[-1]]
        if n_dom == 4:
            last = [chunks[-1][:2], chunks[-1][2:]]
            tiles[-1].append(len(chunks))
        if len(parts) and len(last) == 2:
            parts[-1], last[0] = lax.optimization_barrier((parts[-1], last[0]))
        parts.append(cell_first(place, n_band, last[0]))
        if len(last) == 2:
            near = parts[-1]
            crossed = [swapped(x, "band", n_band, m) if m else x for m, x in enumerate(near)]
            crossed, last[1] = lax.optimization_barrier((crossed, last[1]))
            parts.append(cell_first(place, n_band, last[1]))
            parts[-2] = crossed
    else:
        projectors = build(place)
        filtered = plane_by_plane(panel, potential)
        by_cell = filtered.reshape(orbitals, cells, lanes).swapaxes(0, 1)
        parts = [
            [
                lax.dynamic_slice_in_dim(by_cell, (band ^ m) * share, share, 0)
                for m in range(n_band)
            ]
        ]
        tiles = [[0]]
    filtered = filtered.reshape(panel.shape)
    own = [part[0] for part in parts]
    pieces = []
    for at, part in enumerate(parts):
        crossed = len(tiles[-1]) == 2 and at == len(parts) - 2
        for m in range(1, n_band):
            pieces.append(part[m] if crossed else swapped(part[m], "band", n_band, m))
    arrays = own + pieces
    pieces = [jnp.concatenate(own, axis=1)] + pieces
    arrays += [swapped(x, "sub", n_sub, k) for k in range(1, n_sub) for x in pieces]
    starts = [sum(x.shape[1] for x in own[:at]) for at in range(len(own))]
    spots = []
    for m in range(n_band):
        for k in range(n_sub):
            for tile in tiles:
                spot = []
                for at in tile:
                    index, first = at, 0
                    if m:
                        index = len(own) + at * (n_band - 1) + m - 1 + k * len(pieces)
                    elif k:
                        index = len(own) * n_band + (k - 1) * len(pieces)
                        first = starts[at]
                    spot.append((index, first, own[at].shape[1]))
                spots.append(spot)

    rows = own_atoms * channels
    n_sent = 3 * n_band - 1
    outgoing = products(
        n_sub, 0, n_sent * rows, n_sent, False, place, projectors, arrays, spots
    )
    outgoing, place = lax.optimization_barrier((outgoing, place))
    grid_part, own_proj = products(
        n_sub, n_sent * rows, rows, 1, True, place, projectors, arrays, spots
    )
    sums, seen = [], []
    to = [(by, m) for by in (1, -1) for m in range(n_band)]
    to += [(0, m) for m in range(n_band - 1, 0, -1)]
    for x, (by, m) in zip(outgoing, to):
        pairs = [
            (d * n_band + b, (d - by) % n_dom * n_band + (b ^ m))
            for d in range(n_dom)
            for b in range(n_band)
        ]
        seen.append(m * n_sub)
        sums.append(lax.ppermute(x, ("dom", "band"), pairs))
    scale_point = 1.0 / (cells * lanes * n_dom)
    scale_atom = 1.0 / math.sqrt(own_atoms * groups * n_dom)
    shares = gram_share(
        (scale_point, scale_atom), groups, seen, place, corr_matrix, grid_part, own_proj, sums
    )
    gram_rows = added(
        [swapped(x, ("band", "sub"), groups, m) if m else x for m, x in enumerate(shares)]
    )
    if n_dom <= 4:
        gram_rows = added(
            [swapped(gram_rows, "dom", n_dom, m) if m else gram_rows for m in range(n_dom)]
        )
    else:
        by = 1
        while by < n_dom:
            gram_rows += swapped(gram_rows, "dom", n_dom, by)
            by *= 2
    return filtered, gram_rows


def solution(mesh):
    placed = (
        P(("slab", "band", "sub"), "dom", None, None),
        P(("slab", "dom"), None, None),
        P(("slab", "dom"), None, None),
        P(("slab", "dom"), None, None, None),
        P(("slab", "dom"), None, None),
    )
    return jax.shard_map(
        on_device,
        mesh=mesh,
        in_specs=placed,
        out_specs=(P(("slab", "band", "sub"), "dom", None, None), P(("slab", "band", "sub"), None)),
        check_vma=False,
    )
```

```python
import functools
import math

import jax
import jax.numpy as jnp
from jax import lax
from jax.experimental import pallas as pl
from jax.experimental.pallas import tpu as pltpu
from jax.sharding import PartitionSpec as P

DEGREE = 12

CENTER_LEVEL = 3.6
HALF_WIDTH = 3.4
SHIFT = 3.0

TOGETHER = 4
SUBLANES = 8
ME, BAND, SUB, GROUP = range(4)
MIB = 1024 * 1024

VMEM = pl.BlockSpec(memory_space=pltpu.VMEM)
SMEM = pl.BlockSpec(memory_space=pltpu.SMEM)
NT = (((1,), (1,)), ((), ()))
TN = (((0,), (0,)), ((), ()))


def params(mib):
    return pltpu.CompilerParams(vmem_limit_bytes=mib * MIB)


def split_bf16(x):
    high = x.astype(jnp.bfloat16)
    return high, (x - high.astype(jnp.float32)).astype(jnp.bfloat16)


def shifted(x, by):
    size = lax.axis_size("dom")
    return lax.ppermute(x, "dom", [(i, (i - by) % size) for i in range(size)])


def swapped(x, axes, size, by):
    return lax.ppermute(x, axes, [(i, i ^ by) for i in range(size)])


def filter_kernel(n_dom, planes, rows, starts, first, n_levels, place, *refs):
    levels, refs = refs[:n_levels], list(refs[n_levels:])
    given = None if first else refs.pop(0)
    ins, outs = refs[:n_dom], refs[n_dom : 2 * n_dom]
    refs = refs[2 * n_dom :]
    diagonal = refs.pop(0) if first else given
    even, odd = refs
    half_planes = n_dom * planes // 2
    cells = planes * rows
    lanes = even.shape[3]
    scale = 1.0 / HALF_WIDTH
    mirrored = (place[ME] & 1) != 0
    plane_at = [jnp.where(mirrored, planes - 1 - i, i) for i in range(planes)]

    for x in range(half_planes):
        for half in range(2):
            m, i = divmod(half * half_planes + x, planes)
            part = slice(half * TOGETHER, (half + 1) * TOGETHER)
            base = starts[m] + plane_at[i] * rows
            for y in range(rows):
                even[x, y, part] = ins[m][pl.ds(base + y, TOGETHER, stride=cells), :]
                if first:
                    if m >= 3:
                        level = levels[m - 3][pl.ds(plane_at[i] * rows + y, 1), :]
                    else:
                        level = ins[m][pl.ds(base + (TOGETHER * cells + y), 1), :]
                    diagonal[x, y, part] = jnp.broadcast_to(
                        (level + (SHIFT - CENTER_LEVEL)) * (2.0 * scale), (TOGETHER, lanes)
                    )

    block = SUBLANES
    lane = lax.broadcasted_iota(jnp.int32, (block, SUBLANES, lanes), 2)
    at_start, at_end = lane == 0, lane == lanes - 1

    def twice_operator(source, x, y):
        here = slice(y, y + block)
        centre = source[x, here]
        if x == 0:
            near = pltpu.roll(source[half_planes - 1, here], TOGETHER, 1) + source[x + 1, here]
        elif x == half_planes - 1:
            near = pltpu.roll(source[0, here], TOGETHER, 1) + source[x - 1, here]
        else:
            near = source[x - 1, here] + source[x + 1, here]
        before = (y - 1) % rows
        after = (y + block) % rows
        near += jnp.concatenate([source[x, before : before + 1], centre[:-1]], axis=0)
        near += jnp.concatenate([centre[1:], source[x, after : after + 1]], axis=0)
        low = pltpu.roll(centre, 1, 2)
        high = pltpu.roll(centre, lanes - 1, 2)
        near += jnp.where(at_start, high, jnp.where(at_end, low, low + high))
        return diagonal[x, here] * centre - scale * near

    places = [(x, y) for x in range(half_planes) for y in range(0, rows, block)]

    def next_field(source, target):
        for x, y in places:
            target[x, y : y + block] = twice_operator(source, x, y) - target[x, y : y + block]

    for x, y in places:
        odd[x, y : y + block] = 0.5 * twice_operator(even, x, y)
    next_field(odd, even)

    def two_steps(_, carry):
        next_field(even, odd)
        next_field(odd, even)
        return carry

    lax.fori_loop(0, DEGREE // 2 - 1, two_steps, 0)
    for m in range(n_dom):
        for i in range(planes):
            half, x = divmod(m * planes + i, half_planes)
            part = slice(half * TOGETHER, (half + 1) * TOGETHER)
            for y in range(rows):
                here = slice(y * TOGETHER, (y + 1) * TOGETHER)
                outs[m][plane_at[i], here, :] = even[x, y, part]


def filter_orbitals(place, diagonal, levels, blocks, starts, planes, rows):
    n_dom = len(blocks)
    first = diagonal is None
    lanes = blocks[0].shape[1]
    field = (n_dom * planes // 2, rows, SUBLANES, lanes)
    out = jax.ShapeDtypeStruct((planes, rows * TOGETHER, lanes), jnp.float32)
    extra = [jax.ShapeDtypeStruct(field, jnp.float32)] if first else []
    given = [] if first else [diagonal]
    size = n_dom * planes * rows * TOGETHER * lanes
    return pl.pallas_call(
        functools.partial(filter_kernel, n_dom, planes, rows, starts, first, len(levels)),
        out_shape=[out] * n_dom + extra,
        in_specs=[SMEM] + [VMEM] * (len(levels) + n_dom + len(given)),
        out_specs=[VMEM] * (n_dom + len(extra)),
        scratch_shapes=[pltpu.VMEM(field, jnp.float32)] * 2,
        compiler_params=params(8),
        cost_estimate=pl.CostEstimate(
            flops=12 * DEGREE * size, bytes_accessed=8 * size, transcendentals=0
        ),
        name="chebyshev",
    )(place, *levels, *given, *blocks)


def cell_first_kernel(n_band, place, *refs):
    pieces, parts = refs[:-n_band], refs[-n_band:]
    share = parts[0].shape[0]
    me = place[ME]
    together = SUBLANES // TOGETHER
    tiles = len(pieces) // together
    for p, part in enumerate(parts):
        base = pl.multiple_of((place[BAND] ^ p) * (share * TOGETHER), SUBLANES)
        for first in range(0, share, together):
            loaded = [piece[pl.ds(base + first * TOGETHER, SUBLANES), :] for piece in pieces]
            for k in range(together):
                here = slice(k * TOGETHER, (k + 1) * TOGETHER)
                for q in range(tiles):
                    tile = jnp.concatenate(
                        [loaded[q * together + i][here] for i in range(together)], axis=0
                    )
                    tile = jnp.where((me & 1) != 0, pltpu.roll(tile, TOGETHER, 0), tile)
                    if tiles == 1:
                        part[first + k] = tile
                    else:
                        row = pl.multiple_of((q ^ (me // together)) * SUBLANES, SUBLANES)
                        part[first + k, pl.ds(row, SUBLANES), :] = tile


def cell_first(place, n_band, pieces):
    rows, lanes = pieces[0].shape
    orbitals = len(pieces) * TOGETHER
    part = jax.ShapeDtypeStruct((rows // (TOGETHER * n_band), orbitals, lanes), jnp.float32)
    return pl.pallas_call(
        functools.partial(cell_first_kernel, n_band),
        out_shape=[part] * n_band,
        in_specs=[SMEM] + [VMEM] * len(pieces),
        out_specs=[VMEM] * n_band,
        compiler_params=params(8),
        name="cell_first",
    )(place, *pieces)


def orbital_first_kernel(n_dom, which, place, *refs):
    pieces, (out, laid_out, sems) = refs[: len(which)], refs[-3:]
    cells = out.shape[1]
    copies = []
    for k, (chunk, m) in enumerate(which):
        for t in range(TOGETHER):
            laid_out[k * TOGETHER + t] = pieces[k][pl.ds(t, cells, stride=TOGETHER), :]
        start = (chunk * n_dom + (place[ME] ^ m)) * TOGETHER
        copies.append(
            pltpu.make_async_copy(
                laid_out.at[pl.ds(k * TOGETHER, TOGETHER)],
                out.at[pl.ds(start, TOGETHER)],
                sems.at[k],
            )
        )
        copies[-1].start()
    for copy in copies:
        copy.wait()


def orbital_first(place, n_dom, orbitals, pieces, which, onto=None):
    rows, lanes = pieces[0].shape
    cells = rows // TOGETHER
    hbm = pl.BlockSpec(memory_space=pltpu.HBM)
    given = [] if onto is None else [onto]
    return pl.pallas_call(
        functools.partial(orbital_first_kernel, n_dom, which),
        out_shape=jax.ShapeDtypeStruct((orbitals, cells, lanes), jnp.float32),
        in_specs=[SMEM] + [VMEM] * len(pieces) + [hbm] * len(given),
        out_specs=hbm,
        input_output_aliases={len(pieces) + 1: 0} if given else {},
        scratch_shapes=[
            pltpu.VMEM((len(pieces) * TOGETHER, cells, lanes), jnp.float32),
            pltpu.SemaphoreType.DMA((len(pieces),)),
        ],
        compiler_params=params(8),
        name="orbital_first",
    )(place, *pieces, *given)


def projector_kernel(n_band, n_sub, place, offsets_ref, coefs_ref, high_out, low_out):
    atoms, shells, channels, spread = coefs_ref.shape
    own = atoms // (n_band * n_sub)
    lanes = spread
    cells = high_out.shape[1] // lanes
    pairs = own // 2
    row_index = lax.broadcasted_iota(jnp.int32, (cells, channels, spread), 0)
    row_index += place[BAND] * cells
    lane_index = lax.broadcasted_iota(jnp.int32, (lanes, spread), 0)

    def two_atoms(step, carry):
        shell = lax.rem(2 * (step // (n_band * pairs)), shells)
        seen = (step // pairs) % n_band
        seen = jnp.where(shell == 1, n_band - 1 - seen, seen)
        band = place[BAND] ^ seen
        first_atom = (place[SUB] * n_band + band) * own + 2 * (step % pairs)
        dense = []
        for i in range(2):
            offsets = offsets_ref[shell, pl.ds(first_atom + i, 1), :]
            coefs = coefs_ref[first_atom + i, shell]
            at_row = row_index == (offsets // lanes)[None]
            at_row &= (offsets >= 0)[None]
            left = [
                jnp.where(at_row, part.astype(jnp.float32)[None], 0.0)
                .reshape(cells * channels, spread)
                .astype(jnp.bfloat16)
                for part in split_bf16(coefs)
            ]
            at_lane = jnp.where(lane_index == (offsets & (lanes - 1)), 1.0, 0.0)
            at_lane = at_lane.astype(jnp.bfloat16)
            values = lax.dot_general(
                jnp.concatenate(left, axis=1),
                jnp.concatenate([at_lane, at_lane], axis=1),
                NT,
                preferred_element_type=jnp.float32,
            )
            dense.append(values.reshape(cells, channels, lanes))
        high, low = split_bf16(jnp.concatenate(dense, axis=1))
        rows = pl.ds(pl.multiple_of(step * 2 * channels, 2 * channels), 2 * channels)
        for cell in range(cells):
            high_out[rows, cell * lanes : (cell + 1) * lanes] = high[cell]
            low_out[rows, cell * lanes : (cell + 1) * lanes] = low[cell]
        return carry

    lax.fori_loop(0, shells * n_band * pairs, two_atoms, 0)


def build_projectors(n_band, n_sub, place, offsets, coefs, cells, lanes):
    atoms, shells, channels, spread = coefs.shape
    rows = atoms // n_sub * shells * channels
    shape = jax.ShapeDtypeStruct((rows, cells * lanes), jnp.bfloat16)
    return pl.pallas_call(
        functools.partial(projector_kernel, n_band, n_sub),
        out_shape=[shape, shape],
        in_specs=[SMEM, VMEM, VMEM],
        out_specs=[VMEM, VMEM],
        compiler_params=params(8),
        cost_estimate=pl.CostEstimate(
            flops=4 * rows * cells * lanes * spread,
            bytes_accessed=8 * rows * cells * lanes,
            transcendentals=0,
        ),
        name="projectors",
    )(place, offsets.swapaxes(0, 1), coefs)


CELLS = 12


def split_orbitals(spots, place, arrays, start):
    swap = (place[ME] & 2) != 0
    highs, lows = [], []
    for spot in spots:
        tiles = [arrays[at][pl.ds(start, CELLS), f : f + width] for at, f, width in spot]
        if len(tiles) == 2:
            near, far = tiles
            tiles = [jnp.where(swap, far, near), jnp.where(swap, near, far)]
        high, low = split_bf16(jnp.concatenate(tiles, axis=1))
        highs.append(jnp.concatenate([high[k] for k in range(CELLS)], axis=1))
        lows.append(jnp.concatenate([low[k] for k in range(CELLS)], axis=1))
    return jnp.concatenate(highs, axis=0), jnp.concatenate(lows, axis=0)


def product(left_high, left_low, high, low):
    orbitals = high.shape[0]
    right = jnp.concatenate([high, low], axis=0)
    wide = lax.dot_general(left_high, right, NT, preferred_element_type=jnp.float32)
    narrow = lax.dot_general(left_low, high, NT, preferred_element_type=jnp.float32)
    return wide[:, :orbitals] + wide[:, orbitals:] + narrow


def product_kernel(spots, n_blocks, place, w_high, w_low, *refs):
    arrays, outs, total = refs[: -n_blocks - 1], refs[-n_blocks - 1 : -1], refs[-1]
    cells, _, lanes = arrays[0].shape

    def one_block(step, carry):
        high, low = split_orbitals(spots, place, arrays, step * CELLS)
        depth = CELLS * lanes
        here = pl.ds(pl.multiple_of(step * depth, depth), depth)
        total[...] += product(w_high[:, here], w_low[:, here], high, low)
        return carry

    total[...] = jnp.zeros_like(total)
    lax.fori_loop(0, cells // CELLS, one_block, 0)
    rows = outs[0].shape[0]
    for k, out in enumerate(outs):
        out[...] = total[k * rows : (k + 1) * rows, :]


def products(n_sub, n_blocks, place, projectors, arrays, spots):
    orbitals = sum(width for spot in spots for _, _, width in spot)
    rows = projectors[0].shape[0]
    block = jax.ShapeDtypeStruct((rows // n_blocks, orbitals), jnp.float32)
    return pl.pallas_call(
        functools.partial(product_kernel, spots, n_blocks),
        out_shape=[block] * n_blocks,
        in_specs=[SMEM] + [VMEM] * (2 + len(arrays)),
        out_specs=[VMEM] * n_blocks,
        scratch_shapes=[pltpu.VMEM((rows, orbitals), jnp.float32)],
        compiler_params=params(8),
        name="products",
    )(place, *projectors, *arrays)


def grid_kernel(spots, n_sub, place, *refs):
    *arrays, out = refs
    share = arrays[0].shape[0] // n_sub
    out[...] = jnp.zeros_like(out)

    def one_block(step, carry):
        high, low = split_orbitals(spots, place, arrays, place[SUB] * share + step * CELLS)
        out[...] += product(high, low, high, low)
        return carry

    lax.fori_loop(0, share // CELLS, one_block, 0)


def grid_sums(n_sub, place, arrays, spots):
    orbitals = sum(width for spot in spots for _, _, width in spot)
    return pl.pallas_call(
        functools.partial(grid_kernel, spots, n_sub),
        out_shape=jax.ShapeDtypeStruct((orbitals, orbitals), jnp.float32),
        in_specs=[SMEM] + [VMEM] * len(arrays),
        out_specs=VMEM,
        compiler_params=params(8),
        name="grid_sums",
    )(place, *arrays)


def reordered(x, width, by):
    span = width * by
    column = lax.broadcasted_iota(jnp.int32, x.shape, 1)
    up, down = pltpu.roll(x, span, 1), pltpu.roll(x, x.shape[1] - span, 1)
    return jnp.where((column & span) == 0, down, up)


def gram_kernel(scales, groups, seen, place, corr_ref, grid_ref, proj_ref, *refs):
    sums, outs = refs[: len(seen)], refs[len(seen) :]
    orbitals = grid_ref.shape[0]
    width = orbitals // groups
    bits = [1 << k for k in range(groups.bit_length() - 1)]
    projections = proj_ref[...]
    for part, by in zip(sums, seen):
        columns = part[...]
        for bit in bits:
            if by & bit:
                columns = reordered(columns, width, bit)
        projections += columns
    corr, rows = split_bf16(corr_ref[...]), split_bf16(projections)
    weighted = jnp.dot(
        jnp.concatenate([corr[0], corr[0], corr[1]], axis=1),
        jnp.concatenate([rows[0], rows[1], rows[0]], axis=0),
        preferred_element_type=jnp.float32,
    )
    parts = split_bf16(weighted)
    atom_part = lax.dot_general(
        jnp.concatenate([rows[0], rows[0], rows[1]], axis=0),
        jnp.concatenate([parts[0], parts[1], parts[0]], axis=0),
        TN,
        preferred_element_type=jnp.float32,
    )
    share = grid_ref[...] * scales[0] + atom_part * scales[1]
    for bit in bits:
        share = jnp.where((place[GROUP] & bit) != 0, reordered(share, width, bit), share)
    for k, out in enumerate(outs):
        out[...] = share[k * width : (k + 1) * width]


def gram_share(scales, groups, seen, place, corr, grid_part, proj, sums):
    rows = jax.ShapeDtypeStruct((grid_part.shape[0] // groups, grid_part.shape[1]), jnp.float32)
    return pl.pallas_call(
        functools.partial(gram_kernel, scales, groups, seen),
        out_shape=[rows] * groups,
        in_specs=[SMEM] + [VMEM] * (3 + len(sums)),
        out_specs=[VMEM] * groups,
        compiler_params=params(8),
        name="gram_share",
    )(place, corr, grid_part, proj, *sums)


def added(terms):
    while len(terms) > 1:
        terms = [a + b for a, b in zip(terms[::2], terms[1::2])]
    return terms[0]


def whole_columns(panel, potential, place, me, build):
    n_dom = lax.axis_size("dom")
    orbitals, planes, rows, lanes = panel.shape
    cells = planes * rows
    flat = panel.reshape(orbitals * cells, lanes)
    levels = potential.reshape(cells, lanes)
    size = TOGETHER * cells
    n_chunks = orbitals // (n_dom * TOGETHER)

    def block(c, m):
        return lax.dynamic_slice_in_dim(flat, (c * n_dom + (me ^ m)) * size, size, 0)

    def sent(x, m):
        return swapped(x, "dom", n_dom, m)

    own = []
    for m in range(n_dom):
        blocks = [block(c, m) for c in range(n_chunks)]
        if m < 3:
            blocks[0] = jnp.concatenate([blocks[0], levels], axis=0)
        own.append(blocks)
    near = sent(jnp.concatenate(own[1], axis=0), 1)
    arrived = [[own[0][0], near] + [sent(own[m][0], m) for m in range(2, n_dom)]]
    handed_on = [sent(arrived[0][2][size:], 1)] if n_dom > 3 else []
    for c in range(1, n_chunks):
        far = [own[m][c] for m in range(2, n_dom)]
        near, far = lax.optimization_barrier((near, far))
        arrived.append([own[0][c], near] + [sent(x, m) for m, x in enumerate(far, start=2)])
    diagonal = None
    done = []
    for c, blocks in enumerate(arrived):
        starts = [0] * n_dom
        starts[1] = c * size + (cells if c else 0)
        filtered = filter_orbitals(
            place, diagonal, [] if c else handed_on, blocks, starts, planes, rows
        )
        if diagonal is None:
            diagonal = filtered[n_dom]
        done.append(list(filtered[:n_dom]))
        if c == 0:
            done[0][0], place = lax.optimization_barrier((done[0][0], place))
            place, projectors = lax.optimization_barrier((place, build(place)))
    return [
        [(sent(x, m) if m else x).reshape(size, lanes) for m, x in enumerate(blocks)]
        for blocks in done
    ], projectors


def plane_by_plane(panel, potential):
    n_dom = lax.axis_size("dom")
    diagonal = (potential + (SHIFT - CENTER_LEVEL)) * (2.0 / HALF_WIDTH)

    def twice_operator(field):
        low, high = shifted(field[:, -1:], -1), shifted(field[:, :1], 1)
        extended = jnp.concatenate([low, field, high], axis=1)
        near = extended[:, 2:] + extended[:, :-2]
        near += jnp.roll(field, 1, axis=2) + jnp.roll(field, -1, axis=2)
        padded = jnp.pad(field, ((0, 0), (0, 0), (0, 0), (1, 1)))
        near += padded[..., 2:] + padded[..., :-2]
        return diagonal * field - near / HALF_WIDTH

    def one_step(_, carry):
        before, current = carry
        return current, twice_operator(current) - before

    start = (panel, 0.5 * twice_operator(panel))
    return lax.fori_loop(0, DEGREE - 1, one_step, start)[1]


def on_device(panel, potential, point_offsets, point_coefs, correlation):
    orbitals, planes, rows, lanes = panel.shape
    n_dom, n_band, n_sub = (lax.axis_size(axis) for axis in ("dom", "band", "sub"))
    groups = n_band * n_sub
    me, band, sub = (lax.axis_index(axis) for axis in ("dom", "band", "sub"))
    place = jnp.stack([me, band, sub, band * n_sub + sub]).astype(jnp.int32)

    cells = planes * rows
    share = cells // n_band
    channels = correlation.shape[1]
    own_atoms = point_offsets.shape[0] // groups
    own_corr = lax.dynamic_slice_in_dim(
        correlation, (sub * n_band + band) * own_atoms, own_atoms, 0
    )
    same_atom = jnp.eye(own_atoms, dtype=jnp.float32)
    corr_matrix = (same_atom[:, None, :, None] * own_corr[:, :, None, :]).reshape(
        own_atoms * channels, own_atoms * channels
    )

    place, corr_matrix = lax.optimization_barrier((place, corr_matrix))

    def build(place):
        return build_projectors(n_band, n_sub, place, point_offsets, point_coefs, share, lanes)

    if n_dom in (2, 4) and orbitals % (n_dom * TOGETHER) == 0 and planes * n_dom % 2 == 0:
        chunks, projectors = whole_columns(panel, potential, place, me, build)
        sooner = place
        which = [(c, m) for c in range(len(chunks)) for m in range(n_dom)]
        pieces = [chunks[c][m] for c, m in which]
        n_late = 2 if n_dom == 4 else 0
        first = len(pieces) - n_late
        filtered = orbital_first(place, n_dom, orbitals, pieces[:first], which[:first])
        early, place = lax.optimization_barrier((filtered, place))
        if n_late:
            filtered = orbital_first(
                place, n_dom, orbitals, pieces[first:], which[first:], early
            )
        parts = [cell_first(sooner, n_band, pieces) for pieces in chunks[:-1]]
        tiles = [[c] for c in range(len(chunks))]
        last = [chunks[-1]]
        if n_dom == 4:
            last = [chunks[-1][:2], chunks[-1][2:]]
            tiles[-1].append(len(chunks))
        if len(parts) and len(last) == 2:
            parts[-1], last[0] = lax.optimization_barrier((parts[-1], last[0]))
        parts.append(cell_first(place, n_band, last[0]))
        if len(last) == 2:
            near = parts[-1]
            crossed = [swapped(x, "band", n_band, m) if m else x for m, x in enumerate(near)]
            crossed, last[1] = lax.optimization_barrier((crossed, last[1]))
            parts.append(cell_first(place, n_band, last[1]))
            parts[-2] = crossed
    else:
        projectors = build(place)
        filtered = plane_by_plane(panel, potential)
        by_cell = filtered.reshape(orbitals, cells, lanes).swapaxes(0, 1)
        parts = [
            [
                lax.dynamic_slice_in_dim(by_cell, (band ^ m) * share, share, 0)
                for m in range(n_band)
            ]
        ]
        tiles = [[0]]
    filtered = filtered.reshape(panel.shape)
    own = [part[0] for part in parts]
    pieces = []
    for at, part in enumerate(parts):
        crossed = len(tiles[-1]) == 2 and at == len(parts) - 2
        for m in range(1, n_band):
            pieces.append(part[m] if crossed else swapped(part[m], "band", n_band, m))
    sooner = own
    firsts = [sum(x.shape[1] for x in own[:at]) for at in range(len(sooner))]
    over_sub = [(jnp.concatenate(sooner, axis=1), [(at, 0, f) for at, f in enumerate(firsts)])]
    over_sub += [(x, [(len(sooner), 0, 0)]) for x in own[len(sooner) :]]
    over_sub += [
        (x, [(k // (n_band - 1), k % (n_band - 1) + 1, 0)]) for k, x in enumerate(pieces)
    ]
    arrays, where = [], {}
    for at, x in enumerate(own):
        where[at, 0, 0] = (len(arrays), 0)
        arrays.append(x)
    for x, held in over_sub[len(over_sub) - len(pieces) :]:
        where[held[0][0], held[0][1], 0] = (len(arrays), 0)
        arrays.append(x)
    for k in range(1, n_sub):
        for x, held in over_sub:
            for at, m, first in held:
                where[at, m, k] = (len(arrays), first)
            arrays.append(swapped(x, "sub", n_sub, k))
    spots = [
        [where[at, m, k] + (own[at].shape[1],) for at in tile]
        for m in range(n_band)
        for k in range(n_sub)
        for tile in tiles
    ]

    rows = own_atoms * channels
    n_sent = 3 * n_band - 1
    *outgoing, own_proj = products(n_sub, n_sent + 1, place, projectors, arrays, spots)
    outgoing, place = lax.optimization_barrier((outgoing, place))
    grid_part = grid_sums(n_sub, place, arrays, spots)
    sums, seen = [], []
    to = [(by, m) for by in (1, -1) for m in range(n_band)]
    to += [(0, m) for m in range(n_band - 1, 0, -1)]
    for x, (by, m) in zip(outgoing, to):
        pairs = [
            (d * n_band + b, (d - by) % n_dom * n_band + (b ^ m))
            for d in range(n_dom)
            for b in range(n_band)
        ]
        seen.append(m * n_sub)
        sums.append(lax.ppermute(x, ("dom", "band"), pairs))
    scale_point = 1.0 / (cells * lanes * n_dom)
    scale_atom = 1.0 / math.sqrt(own_atoms * groups * n_dom)
    shares = gram_share(
        (scale_point, scale_atom), groups, seen, place, corr_matrix, grid_part, own_proj, sums
    )
    gram_rows = added(
        [swapped(x, ("band", "sub"), groups, m) if m else x for m, x in enumerate(shares)]
    )
    if n_dom <= 4:
        gram_rows = added(
            [swapped(gram_rows, "dom", n_dom, m) if m else gram_rows for m in range(n_dom)]
        )
    else:
        by = 1
        while by < n_dom:
            gram_rows += swapped(gram_rows, "dom", n_dom, by)
            by *= 2
    return filtered, gram_rows


def solution(mesh):
    placed = (
        P(("slab", "band", "sub"), "dom", None, None),
        P(("slab", "dom"), None, None),
        P(("slab", "dom"), None, None),
        P(("slab", "dom"), None, None, None),
        P(("slab", "dom"), None, None),
    )
    return jax.shard_map(
        on_device,
        mesh=mesh,
        in_specs=placed,
        out_specs=(P(("slab", "band", "sub"), "dom", None, None), P(("slab", "band", "sub"), None)),
        check_vma=False,
    )
```

```python
import functools
import math

import jax
import jax.numpy as jnp
from jax import lax
from jax.experimental import pallas as pl
from jax.experimental.pallas import tpu as pltpu
from jax.sharding import PartitionSpec as P

DEGREE = 12

CENTER_LEVEL = 3.6
HALF_WIDTH = 3.4
SHIFT = 3.0

TOGETHER = 4
SUBLANES = 8
ME, BAND, SUB, GROUP = range(4)
MIB = 1024 * 1024

VMEM = pl.BlockSpec(memory_space=pltpu.VMEM)
SMEM = pl.BlockSpec(memory_space=pltpu.SMEM)
NT = (((1,), (1,)), ((), ()))
TN = (((0,), (0,)), ((), ()))


def params(mib):
    return pltpu.CompilerParams(vmem_limit_bytes=mib * MIB)


def split_bf16(x):
    high = x.astype(jnp.bfloat16)
    return high, (x - high.astype(jnp.float32)).astype(jnp.bfloat16)


def shifted(x, by):
    size = lax.axis_size("dom")
    return lax.ppermute(x, "dom", [(i, (i - by) % size) for i in range(size)])


def swapped(x, axes, size, by):
    return lax.ppermute(x, axes, [(i, i ^ by) for i in range(size)])


def slot_partners(n_dom, odd):
    partners = list(range(1, n_dom))
    return partners[1::-1] + partners[2:] if odd else partners


def sent(x, slot):
    n_dom, n_sub = lax.axis_size("dom"), lax.axis_size("sub")
    pairs = [
        (d * n_sub + k, (d ^ slot_partners(n_dom, k % 2)[slot]) * n_sub + k)
        for d in range(n_dom)
        for k in range(n_sub)
    ]
    return lax.ppermute(x, ("dom", "sub"), pairs)


def by_partner(slots, odd):
    partners = slot_partners(len(slots), odd)
    return slots[:1] + [slots[1 + partners.index(m)] for m in range(1, len(slots))]


def for_each_order(place, body):
    for odd in range(2):
        pl.when((place[SUB] & 1) == odd)(functools.partial(body, odd))


def filter_kernel(n_dom, planes, rows, first, n_levels, place, *refs):
    levels, refs = refs[:n_levels], list(refs[n_levels:])
    given = None if first else refs.pop(0)
    ins, outs = refs[:n_dom], refs[n_dom : 2 * n_dom]
    refs = refs[2 * n_dom :]
    diagonal = refs.pop(0) if first else given
    even, odd = refs
    half_planes = n_dom * planes // 2
    cells = planes * rows
    lanes = even.shape[3]
    scale = 1.0 / HALF_WIDTH
    mirrored = (place[ME] & 1) != 0
    plane_at = [jnp.where(mirrored, planes - 1 - i, i) for i in range(planes)]

    def take(odd):
        blocks = by_partner(list(ins), odd)
        for x in range(half_planes):
            for half in range(2):
                m, i = divmod(half * half_planes + x, planes)
                part = slice(half * TOGETHER, (half + 1) * TOGETHER)
                base = plane_at[i] * rows
                for y in range(rows):
                    even[x, y, part] = blocks[m][pl.ds(base + y, TOGETHER, stride=cells), :]
                    if not first:
                        continue
                    if m >= 3:
                        level = levels[m - 3][pl.ds(base + y, 1), :]
                    else:
                        level = blocks[m][pl.ds(base + (TOGETHER * cells + y), 1), :]
                    diagonal[x, y, part] = jnp.broadcast_to(
                        (level + (SHIFT - CENTER_LEVEL)) * (2.0 * scale), (TOGETHER, lanes)
                    )

    for_each_order(place, take)
    block = SUBLANES
    lane = lax.broadcasted_iota(jnp.int32, (block, SUBLANES, lanes), 2)
    at_start, at_end = lane == 0, lane == lanes - 1

    def twice_operator(source, x, y):
        here = slice(y, y + block)
        centre = source[x, here]
        if x == 0:
            near = pltpu.roll(source[half_planes - 1, here], TOGETHER, 1) + source[x + 1, here]
        elif x == half_planes - 1:
            near = pltpu.roll(source[0, here], TOGETHER, 1) + source[x - 1, here]
        else:
            near = source[x - 1, here] + source[x + 1, here]
        before = (y - 1) % rows
        after = (y + block) % rows
        near += jnp.concatenate([source[x, before : before + 1], centre[:-1]], axis=0)
        near += jnp.concatenate([centre[1:], source[x, after : after + 1]], axis=0)
        low = pltpu.roll(centre, 1, 2)
        high = pltpu.roll(centre, lanes - 1, 2)
        near += jnp.where(at_start, high, jnp.where(at_end, low, low + high))
        return diagonal[x, here] * centre - scale * near

    places = [(x, y) for x in range(half_planes) for y in range(0, rows, block)]

    def next_field(source, target):
        for x, y in places:
            target[x, y : y + block] = twice_operator(source, x, y) - target[x, y : y + block]

    for x, y in places:
        odd[x, y : y + block] = 0.5 * twice_operator(even, x, y)
    next_field(odd, even)

    def two_steps(_, carry):
        next_field(even, odd)
        next_field(odd, even)
        return carry

    lax.fori_loop(0, DEGREE // 2 - 1, two_steps, 0)

    def give(odd):
        blocks = by_partner(list(outs), odd)
        for m in range(n_dom):
            for i in range(planes):
                half, x = divmod(m * planes + i, half_planes)
                part = slice(half * TOGETHER, (half + 1) * TOGETHER)
                for y in range(rows):
                    here = slice(y * TOGETHER, (y + 1) * TOGETHER)
                    blocks[m][plane_at[i], here, :] = even[x, y, part]

    for_each_order(place, give)


def filter_orbitals(place, diagonal, levels, blocks, planes, rows):
    n_dom = len(blocks)
    first = diagonal is None
    lanes = blocks[0].shape[1]
    field = (n_dom * planes // 2, rows, SUBLANES, lanes)
    out = jax.ShapeDtypeStruct((planes, rows * TOGETHER, lanes), jnp.float32)
    extra = [jax.ShapeDtypeStruct(field, jnp.float32)] if first else []
    given = [] if first else [diagonal]
    size = n_dom * planes * rows * TOGETHER * lanes
    return pl.pallas_call(
        functools.partial(filter_kernel, n_dom, planes, rows, first, len(levels)),
        out_shape=[out] * n_dom + extra,
        in_specs=[SMEM] + [VMEM] * (len(levels) + n_dom + len(given)),
        out_specs=[VMEM] * (n_dom + len(extra)),
        scratch_shapes=[pltpu.VMEM(field, jnp.float32)] * 2,
        compiler_params=params(8),
        cost_estimate=pl.CostEstimate(
            flops=12 * DEGREE * size, bytes_accessed=8 * size, transcendentals=0
        ),
        name="chebyshev",
    )(place, *levels, *given, *blocks)


def cell_first_kernel(n_band, chosen, place, *refs):
    given, parts = list(refs[:-n_band]), refs[-n_band:]

    def body(odd):
        pieces = [by_partner(given, odd)[m] for m in chosen]
        cell_first_pieces(place, pieces, parts)

    for_each_order(place, body)


def cell_first_pieces(place, pieces, parts):
    share = parts[0].shape[0]
    me = place[ME]
    together = SUBLANES // TOGETHER
    tiles = len(pieces) // together
    for p, part in enumerate(parts):
        base = pl.multiple_of((place[BAND] ^ p) * (share * TOGETHER), SUBLANES)
        for first in range(0, share, together):
            loaded = [piece[pl.ds(base + first * TOGETHER, SUBLANES), :] for piece in pieces]
            for k in range(together):
                here = slice(k * TOGETHER, (k + 1) * TOGETHER)
                for q in range(tiles):
                    tile = jnp.concatenate(
                        [loaded[q * together + i][here] for i in range(together)], axis=0
                    )
                    tile = jnp.where((me & 1) != 0, pltpu.roll(tile, TOGETHER, 0), tile)
                    if tiles == 1:
                        part[first + k] = tile
                    else:
                        row = pl.multiple_of((q ^ (me // together)) * SUBLANES, SUBLANES)
                        part[first + k, pl.ds(row, SUBLANES), :] = tile


def cell_first(place, n_band, chosen, pieces):
    rows, lanes = pieces[0].shape
    orbitals = len(chosen) * TOGETHER
    part = jax.ShapeDtypeStruct((rows // (TOGETHER * n_band), orbitals, lanes), jnp.float32)
    return pl.pallas_call(
        functools.partial(cell_first_kernel, n_band, chosen),
        out_shape=[part] * n_band,
        in_specs=[SMEM] + [VMEM] * len(pieces),
        out_specs=[VMEM] * n_band,
        compiler_params=params(8),
        name="cell_first",
    )(place, *pieces)


def orbital_first_kernel(n_dom, counts, which, place, *refs):
    given, (out, laid_out, sems) = list(refs[: sum(counts)]), refs[-3:]
    cells = out.shape[1]

    def body(odd):
        pieces, at = [], 0
        for count in counts:
            some = given[at : at + count]
            pieces.append(by_partner(some + [None] * (n_dom - count), odd))
            at += count
        for k, (at, chunk, m) in enumerate(which):
            for t in range(TOGETHER):
                laid_out[k * TOGETHER + t] = pieces[at][m][pl.ds(t, cells, stride=TOGETHER), :]

    for_each_order(place, body)
    copies = []
    for k, (_, chunk, m) in enumerate(which):
        start = (chunk * n_dom + (place[ME] ^ m)) * TOGETHER
        copies.append(
            pltpu.make_async_copy(
                laid_out.at[pl.ds(k * TOGETHER, TOGETHER)],
                out.at[pl.ds(start, TOGETHER)],
                sems.at[k],
            )
        )
        copies[-1].start()
    for copy in copies:
        copy.wait()


def orbital_first(place, n_dom, orbitals, chunks, which, onto=None):
    rows, lanes = chunks[0][0].shape
    cells = rows // TOGETHER
    hbm = pl.BlockSpec(memory_space=pltpu.HBM)
    pieces = [piece for chunk in chunks for piece in chunk]
    given = [] if onto is None else [onto]
    return pl.pallas_call(
        functools.partial(orbital_first_kernel, n_dom, [len(x) for x in chunks], which),
        out_shape=jax.ShapeDtypeStruct((orbitals, cells, lanes), jnp.float32),
        in_specs=[SMEM] + [VMEM] * len(pieces) + [hbm] * len(given),
        out_specs=hbm,
        input_output_aliases={len(pieces) + 1: 0} if given else {},
        scratch_shapes=[
            pltpu.VMEM((len(which) * TOGETHER, cells, lanes), jnp.float32),
            pltpu.SemaphoreType.DMA((len(which),)),
        ],
        compiler_params=params(8),
        name="orbital_first",
    )(place, *pieces, *given)


def projector_kernel(n_band, n_sub, place, offsets_ref, coefs_ref, high_out, low_out):
    atoms, shells, channels, spread = coefs_ref.shape
    own = atoms // (n_band * n_sub)
    lanes = spread
    cells = high_out.shape[1] // lanes
    pairs = own // 2
    row_index = lax.broadcasted_iota(jnp.int32, (cells, channels, spread), 0)
    row_index += place[BAND] * cells
    lane_index = lax.broadcasted_iota(jnp.int32, (lanes, spread), 0)

    def two_atoms(step, carry):
        shell = lax.rem(2 * (step // (n_band * pairs)), shells)
        seen = (step // pairs) % n_band
        seen = jnp.where(shell == 1, n_band - 1 - seen, seen)
        band = place[BAND] ^ seen
        first_atom = (place[SUB] * n_band + band) * own + 2 * (step % pairs)
        dense = []
        for i in range(2):
            offsets = offsets_ref[shell, pl.ds(first_atom + i, 1), :]
            coefs = coefs_ref[first_atom + i, shell]
            at_row = row_index == (offsets // lanes)[None]
            at_row &= (offsets >= 0)[None]
            left = [
                jnp.where(at_row, part.astype(jnp.float32)[None], 0.0)
                .reshape(cells * channels, spread)
                .astype(jnp.bfloat16)
                for part in split_bf16(coefs)
            ]
            at_lane = jnp.where(lane_index == (offsets & (lanes - 1)), 1.0, 0.0)
            at_lane = at_lane.astype(jnp.bfloat16)
            values = lax.dot_general(
                jnp.concatenate(left, axis=1),
                jnp.concatenate([at_lane, at_lane], axis=1),
                NT,
                preferred_element_type=jnp.float32,
            )
            dense.append(values.reshape(cells, channels, lanes))
        high, low = split_bf16(jnp.concatenate(dense, axis=1))
        rows = pl.ds(pl.multiple_of(step * 2 * channels, 2 * channels), 2 * channels)
        for cell in range(cells):
            high_out[rows, cell * lanes : (cell + 1) * lanes] = high[cell]
            low_out[rows, cell * lanes : (cell + 1) * lanes] = low[cell]
        return carry

    lax.fori_loop(0, shells * n_band * pairs, two_atoms, 0)


def build_projectors(n_band, n_sub, place, offsets, coefs, cells, lanes):
    atoms, shells, channels, spread = coefs.shape
    rows = atoms // n_sub * shells * channels
    shape = jax.ShapeDtypeStruct((rows, cells * lanes), jnp.bfloat16)
    return pl.pallas_call(
        functools.partial(projector_kernel, n_band, n_sub),
        out_shape=[shape, shape],
        in_specs=[SMEM, VMEM, VMEM],
        out_specs=[VMEM, VMEM],
        compiler_params=params(8),
        cost_estimate=pl.CostEstimate(
            flops=4 * rows * cells * lanes * spread,
            bytes_accessed=8 * rows * cells * lanes,
            transcendentals=0,
        ),
        name="projectors",
    )(place, offsets.swapaxes(0, 1), coefs)


CELLS = 12


def split_orbitals(spots, place, arrays, start):
    swap = (place[ME] & 2) != 0
    highs, lows = [], []
    for spot in spots:
        tiles = [arrays[at][pl.ds(start, CELLS), f : f + width] for at, f, width in spot]
        if len(tiles) == 2:
            near, far = tiles
            tiles = [jnp.where(swap, far, near), jnp.where(swap, near, far)]
        high, low = split_bf16(jnp.concatenate(tiles, axis=1))
        highs.append(jnp.concatenate([high[k] for k in range(CELLS)], axis=1))
        lows.append(jnp.concatenate([low[k] for k in range(CELLS)], axis=1))
    return jnp.concatenate(highs, axis=0), jnp.concatenate(lows, axis=0)


def product(left_high, left_low, high, low):
    orbitals = high.shape[0]
    right = jnp.concatenate([high, low], axis=0)
    wide = lax.dot_general(left_high, right, NT, preferred_element_type=jnp.float32)
    narrow = lax.dot_general(left_low, high, NT, preferred_element_type=jnp.float32)
    return wide[:, :orbitals] + wide[:, orbitals:] + narrow


def product_kernel(spots, n_blocks, place, w_high, w_low, *refs):
    arrays, outs, total = refs[: -n_blocks - 1], refs[-n_blocks - 1 : -1], refs[-1]
    cells, _, lanes = arrays[0].shape

    def one_block(step, carry):
        high, low = split_orbitals(spots, place, arrays, step * CELLS)
        depth = CELLS * lanes
        here = pl.ds(pl.multiple_of(step * depth, depth), depth)
        total[...] += product(w_high[:, here], w_low[:, here], high, low)
        return carry

    total[...] = jnp.zeros_like(total)
    lax.fori_loop(0, cells // CELLS, one_block, 0)
    rows = outs[0].shape[0]
    for k, out in enumerate(outs):
        out[...] = total[k * rows : (k + 1) * rows, :]


def products(n_sub, n_blocks, place, projectors, arrays, spots):
    orbitals = sum(width for spot in spots for _, _, width in spot)
    rows = projectors[0].shape[0]
    block = jax.ShapeDtypeStruct((rows // n_blocks, orbitals), jnp.float32)
    return pl.pallas_call(
        functools.partial(product_kernel, spots, n_blocks),
        out_shape=[block] * n_blocks,
        in_specs=[SMEM] + [VMEM] * (2 + len(arrays)),
        out_specs=[VMEM] * n_blocks,
        scratch_shapes=[pltpu.VMEM((rows, orbitals), jnp.float32)],
        compiler_params=params(8),
        name="products",
    )(place, *projectors, *arrays)


def grid_kernel(spots, n_sub, place, *refs):
    *arrays, out = refs
    share = arrays[0].shape[0] // n_sub
    out[...] = jnp.zeros_like(out)

    def one_block(step, carry):
        high, low = split_orbitals(spots, place, arrays, place[SUB] * share + step * CELLS)
        out[...] += product(high, low, high, low)
        return carry

    lax.fori_loop(0, share // CELLS, one_block, 0)


def grid_sums(n_sub, place, arrays, spots):
    orbitals = sum(width for spot in spots for _, _, width in spot)
    return pl.pallas_call(
        functools.partial(grid_kernel, spots, n_sub),
        out_shape=jax.ShapeDtypeStruct((orbitals, orbitals), jnp.float32),
        in_specs=[SMEM] + [VMEM] * len(arrays),
        out_specs=VMEM,
        compiler_params=params(8),
        name="grid_sums",
    )(place, *arrays)


def reordered(x, width, by):
    span = width * by
    column = lax.broadcasted_iota(jnp.int32, x.shape, 1)
    up, down = pltpu.roll(x, span, 1), pltpu.roll(x, x.shape[1] - span, 1)
    return jnp.where((column & span) == 0, down, up)


def gram_kernel(scales, groups, seen, place, corr_ref, grid_ref, proj_ref, *refs):
    sums, outs = refs[: len(seen)], refs[len(seen) :]
    orbitals = grid_ref.shape[0]
    width = orbitals // groups
    bits = [1 << k for k in range(groups.bit_length() - 1)]
    projections = proj_ref[...]
    for part, by in zip(sums, seen):
        columns = part[...]
        for bit in bits:
            if by & bit:
                columns = reordered(columns, width, bit)
        projections += columns
    corr, rows = split_bf16(corr_ref[...]), split_bf16(projections)
    weighted = jnp.dot(
        jnp.concatenate([corr[0], corr[0], corr[1]], axis=1),
        jnp.concatenate([rows[0], rows[1], rows[0]], axis=0),
        preferred_element_type=jnp.float32,
    )
    parts = split_bf16(weighted)
    atom_part = lax.dot_general(
        jnp.concatenate([rows[0], rows[0], rows[1]], axis=0),
        jnp.concatenate([parts[0], parts[1], parts[0]], axis=0),
        TN,
        preferred_element_type=jnp.float32,
    )
    share = grid_ref[...] * scales[0] + atom_part * scales[1]
    for bit in bits:
        share = jnp.where((place[GROUP] & bit) != 0, reordered(share, width, bit), share)
    for k, out in enumerate(outs):
        out[...] = share[k * width : (k + 1) * width]


def gram_share(scales, groups, seen, place, corr, grid_part, proj, sums):
    rows = jax.ShapeDtypeStruct((grid_part.shape[0] // groups, grid_part.shape[1]), jnp.float32)
    return pl.pallas_call(
        functools.partial(gram_kernel, scales, groups, seen),
        out_shape=[rows] * groups,
        in_specs=[SMEM] + [VMEM] * (3 + len(sums)),
        out_specs=[VMEM] * groups,
        compiler_params=params(8),
        name="gram_share",
    )(place, corr, grid_part, proj, *sums)


def added(terms):
    while len(terms) > 1:
        terms = [a + b for a, b in zip(terms[::2], terms[1::2])]
    return terms[0]


def whole_columns(panel, potential, place, me, build):
    n_dom = lax.axis_size("dom")
    orbitals, planes, rows, lanes = panel.shape
    cells = planes * rows
    flat = panel.reshape(orbitals * cells, lanes)
    levels = potential.reshape(cells, lanes)
    size = TOGETHER * cells
    n_chunks = orbitals // (n_dom * TOGETHER)

    def block(c, m):
        return lax.dynamic_slice_in_dim(flat, (c * n_dom + (me ^ m)) * size, size, 0)

    odd = lax.axis_index("sub") & 1
    partners = [
        jnp.where(odd == 1, b, a)
        for a, b in zip(slot_partners(n_dom, 0), slot_partners(n_dom, 1))
    ]
    own = [block(c, 0) for c in range(n_chunks)]
    own[0] = jnp.concatenate([own[0], levels], axis=0)
    blocks = [block(0, m) for m in partners]
    blocks[:2] = [jnp.concatenate([x, levels], axis=0) for x in blocks[:2]]
    arrived = [own[:1] + [sent(x, slot) for slot, x in enumerate(blocks)]]
    handed_on = []
    if n_dom > 3:
        far = jnp.where(odd == 1, arrived[0][1][size:], arrived[0][2][size:])
        handed_on = [swapped(far, "dom", n_dom, 1)]
    for c in range(1, n_chunks):
        blocks = [block(c, m) for m in partners]
        arrived[0][1], blocks = lax.optimization_barrier((arrived[0][1], blocks))
        arrived.append([own[c]] + [sent(x, slot) for slot, x in enumerate(blocks)])
    place, projectors = lax.optimization_barrier((place, build(place)))
    diagonal = None
    done = []
    for c, blocks in enumerate(arrived):
        filtered = filter_orbitals(
            place, diagonal, [] if c else handed_on, blocks, planes, rows
        )
        if diagonal is None:
            diagonal = filtered[n_dom]
        done.append(list(filtered[:n_dom]))
    return [
        [(sent(x, at - 1) if at else x).reshape(size, lanes) for at, x in enumerate(blocks)]
        for blocks in done
    ], projectors


def plane_by_plane(panel, potential):
    n_dom = lax.axis_size("dom")
    diagonal = (potential + (SHIFT - CENTER_LEVEL)) * (2.0 / HALF_WIDTH)

    def twice_operator(field):
        low, high = shifted(field[:, -1:], -1), shifted(field[:, :1], 1)
        extended = jnp.concatenate([low, field, high], axis=1)
        near = extended[:, 2:] + extended[:, :-2]
        near += jnp.roll(field, 1, axis=2) + jnp.roll(field, -1, axis=2)
        padded = jnp.pad(field, ((0, 0), (0, 0), (0, 0), (1, 1)))
        near += padded[..., 2:] + padded[..., :-2]
        return diagonal * field - near / HALF_WIDTH

    def one_step(_, carry):
        before, current = carry
        return current, twice_operator(current) - before

    start = (panel, 0.5 * twice_operator(panel))
    return lax.fori_loop(0, DEGREE - 1, one_step, start)[1]


def on_device(panel, potential, point_offsets, point_coefs, correlation):
    orbitals, planes, rows, lanes = panel.shape
    n_dom, n_band, n_sub = (lax.axis_size(axis) for axis in ("dom", "band", "sub"))
    groups = n_band * n_sub
    me, band, sub = (lax.axis_index(axis) for axis in ("dom", "band", "sub"))
    place = jnp.stack([me, band, sub, band * n_sub + sub]).astype(jnp.int32)

    cells = planes * rows
    share = cells // n_band
    channels = correlation.shape[1]
    own_atoms = point_offsets.shape[0] // groups
    own_corr = lax.dynamic_slice_in_dim(
        correlation, (sub * n_band + band) * own_atoms, own_atoms, 0
    )
    same_atom = jnp.eye(own_atoms, dtype=jnp.float32)
    corr_matrix = (same_atom[:, None, :, None] * own_corr[:, :, None, :]).reshape(
        own_atoms * channels, own_atoms * channels
    )

    place, corr_matrix = lax.optimization_barrier((place, corr_matrix))

    def build(place):
        return build_projectors(n_band, n_sub, place, point_offsets, point_coefs, share, lanes)

    if n_dom in (2, 4) and orbitals % (n_dom * TOGETHER) == 0 and planes * n_dom % 2 == 0:
        chunks, projectors = whole_columns(panel, potential, place, me, build)
        sooner = place
        which = [(c, c, m) for c in range(len(chunks)) for m in range(n_dom)]
        n_late = 2 if n_dom == 4 else 0
        sooner = chunks[:-1] + [chunks[-1][: n_dom - n_late // 2]]
        count = len(which) - n_late
        filtered = orbital_first(place, n_dom, orbitals, sooner, which[:count])
        written, later = lax.optimization_barrier((filtered, place))
        parts = [cell_first(place, n_band, range(n_dom), pieces) for pieces in chunks[:-1]]
        tiles = [[c] for c in range(len(chunks))]
        if n_late:
            filtered = orbital_first(
                place, n_dom, orbitals, chunks[-1:], [(0,) + x[1:] for x in which[count:]], written
            )
            tiles[-1].append(len(chunks))
            pieces = sooner[-1]
            if parts:
                parts[-1], pieces = lax.optimization_barrier((parts[-1], pieces))
            near = cell_first(later, n_band, (0, 1), pieces)
            crossed = [swapped(x, "band", n_band, m) if m else x for m, x in enumerate(near)]
            crossed, pieces = lax.optimization_barrier((crossed, chunks[-1]))
            parts.append(crossed)
            parts.append(cell_first(later, n_band, (2, 3), pieces))
        else:
            parts.append(cell_first(later, n_band, range(n_dom), chunks[-1]))
    else:
        projectors = build(place)
        filtered = plane_by_plane(panel, potential)
        by_cell = filtered.reshape(orbitals, cells, lanes).swapaxes(0, 1)
        parts = [
            [
                lax.dynamic_slice_in_dim(by_cell, (band ^ m) * share, share, 0)
                for m in range(n_band)
            ]
        ]
        tiles = [[0]]
    filtered = filtered.reshape(panel.shape)
    own = [part[0] for part in parts]
    pieces = []
    for at, part in enumerate(parts):
        crossed = len(tiles[-1]) == 2 and at == len(parts) - 2
        for m in range(1, n_band):
            pieces.append(part[m] if crossed else swapped(part[m], "band", n_band, m))
    sooner = own
    firsts = [sum(x.shape[1] for x in own[:at]) for at in range(len(sooner))]
    over_sub = [(jnp.concatenate(sooner, axis=1), [(at, 0, f) for at, f in enumerate(firsts)])]
    over_sub += [(x, [(len(sooner), 0, 0)]) for x in own[len(sooner) :]]
    over_sub += [
        (x, [(k // (n_band - 1), k % (n_band - 1) + 1, 0)]) for k, x in enumerate(pieces)
    ]
    arrays, where = [], {}
    for at, x in enumerate(own):
        where[at, 0, 0] = (len(arrays), 0)
        arrays.append(x)
    for x, held in over_sub[len(over_sub) - len(pieces) :]:
        where[held[0][0], held[0][1], 0] = (len(arrays), 0)
        arrays.append(x)
    for k in range(1, n_sub):
        for x, held in over_sub:
            for at, m, first in held:
                where[at, m, k] = (len(arrays), first)
            arrays.append(swapped(x, "sub", n_sub, k))
    spots = [
        [where[at, m, k] + (own[at].shape[1],) for at in tile]
        for m in range(n_band)
        for k in range(n_sub)
        for tile in tiles
    ]

    rows = own_atoms * channels
    n_sent = 3 * n_band - 1
    *outgoing, own_proj = products(n_sub, n_sent + 1, place, projectors, arrays, spots)
    outgoing, place = lax.optimization_barrier((outgoing, place))
    grid_part = grid_sums(n_sub, place, arrays, spots)
    sums, seen = [], []
    to = [(by, m) for by in (1, -1) for m in range(n_band)]
    to += [(0, m) for m in range(n_band - 1, 0, -1)]
    for x, (by, m) in zip(outgoing, to):
        pairs = [
            (d * n_band + b, (d - by) % n_dom * n_band + (b ^ m))
            for d in range(n_dom)
            for b in range(n_band)
        ]
        seen.append(m * n_sub)
        sums.append(lax.ppermute(x, ("dom", "band"), pairs))
    scale_point = 1.0 / (cells * lanes * n_dom)
    scale_atom = 1.0 / math.sqrt(own_atoms * groups * n_dom)
    shares = gram_share(
        (scale_point, scale_atom), groups, seen, place, corr_matrix, grid_part, own_proj, sums
    )
    gram_rows = added(
        [swapped(x, ("band", "sub"), groups, m) if m else x for m, x in enumerate(shares)]
    )
    if n_dom <= 4:
        gram_rows = added(
            [swapped(gram_rows, "dom", n_dom, m) if m else gram_rows for m in range(n_dom)]
        )
    else:
        by = 1
        while by < n_dom:
            gram_rows += swapped(gram_rows, "dom", n_dom, by)
            by *= 2
    return filtered, gram_rows


def solution(mesh):
    placed = (
        P(("slab", "band", "sub"), "dom", None, None),
        P(("slab", "dom"), None, None),
        P(("slab", "dom"), None, None),
        P(("slab", "dom"), None, None, None),
        P(("slab", "dom"), None, None),
    )
    return jax.shard_map(
        on_device,
        mesh=mesh,
        in_specs=placed,
        out_specs=(P(("slab", "band", "sub"), "dom", None, None), P(("slab", "band", "sub"), None)),
        check_vma=False,
    )
```

```python
import functools
import math

import jax
import jax.numpy as jnp
from jax import lax
from jax.experimental import pallas as pl
from jax.experimental.pallas import tpu as pltpu
from jax.sharding import PartitionSpec as P

DEGREE = 12

CENTER_LEVEL = 3.6
HALF_WIDTH = 3.4
SHIFT = 3.0

TOGETHER = 4
SUBLANES = 8
ME, BAND, SUB, GROUP = range(4)
MIB = 1024 * 1024

VMEM = pl.BlockSpec(memory_space=pltpu.VMEM)
SMEM = pl.BlockSpec(memory_space=pltpu.SMEM)
NT = (((1,), (1,)), ((), ()))
TN = (((0,), (0,)), ((), ()))


def params(mib):
    return pltpu.CompilerParams(vmem_limit_bytes=mib * MIB)


def split_bf16(x):
    high = x.astype(jnp.bfloat16)
    return high, (x - high.astype(jnp.float32)).astype(jnp.bfloat16)


def shifted(x, by):
    size = lax.axis_size("dom")
    return lax.ppermute(x, "dom", [(i, (i - by) % size) for i in range(size)])


def swapped(x, axes, size, by):
    return lax.ppermute(x, axes, [(i, i ^ by) for i in range(size)])


def filter_kernel(n_dom, planes, rows, starts, first, n_levels, place, *refs):
    levels, refs = refs[:n_levels], list(refs[n_levels:])
    given = None if first else refs.pop(0)
    ins, outs = refs[:n_dom], refs[n_dom : 2 * n_dom]
    refs = refs[2 * n_dom :]
    diagonal = refs.pop(0) if first else given
    even, odd = refs
    half_planes = n_dom * planes // 2
    cells = planes * rows
    lanes = even.shape[3]
    scale = 1.0 / HALF_WIDTH
    mirrored = (place[ME] & 1) != 0
    plane_at = [jnp.where(mirrored, planes - 1 - i, i) for i in range(planes)]

    for x in range(half_planes):
        for half in range(2):
            m, i = divmod(half * half_planes + x, planes)
            part = slice(half * TOGETHER, (half + 1) * TOGETHER)
            base = starts[m] + plane_at[i] * rows
            for y in range(rows):
                even[x, y, part] = ins[m][pl.ds(base + y, TOGETHER, stride=cells), :]
                if first:
                    if m >= 3:
                        level = levels[m - 3][pl.ds(plane_at[i] * rows + y, 1), :]
                    else:
                        level = ins[m][pl.ds(base + (TOGETHER * cells + y), 1), :]
                    diagonal[x, y, part] = jnp.broadcast_to(
                        (level + (SHIFT - CENTER_LEVEL)) * (2.0 * scale), (TOGETHER, lanes)
                    )

    block = SUBLANES
    lane = lax.broadcasted_iota(jnp.int32, (block, SUBLANES, lanes), 2)
    at_start, at_end = lane == 0, lane == lanes - 1

    def twice_operator(source, x, y):
        here = slice(y, y + block)
        centre = source[x, here]
        if x == 0:
            near = pltpu.roll(source[half_planes - 1, here], TOGETHER, 1) + source[x + 1, here]
        elif x == half_planes - 1:
            near = pltpu.roll(source[0, here], TOGETHER, 1) + source[x - 1, here]
        else:
            near = source[x - 1, here] + source[x + 1, here]
        before = (y - 1) % rows
        after = (y + block) % rows
        near += jnp.concatenate([source[x, before : before + 1], centre[:-1]], axis=0)
        near += jnp.concatenate([centre[1:], source[x, after : after + 1]], axis=0)
        low = pltpu.roll(centre, 1, 2)
        high = pltpu.roll(centre, lanes - 1, 2)
        near += jnp.where(at_start, high, jnp.where(at_end, low, low + high))
        return diagonal[x, here] * centre - scale * near

    places = [(x, y) for x in range(half_planes) for y in range(0, rows, block)]

    def next_field(source, target):
        for x, y in places:
            target[x, y : y + block] = twice_operator(source, x, y) - target[x, y : y + block]

    for x, y in places:
        odd[x, y : y + block] = 0.5 * twice_operator(even, x, y)
    next_field(odd, even)

    def two_steps(_, carry):
        next_field(even, odd)
        next_field(odd, even)
        return carry

    lax.fori_loop(0, DEGREE // 2 - 1, two_steps, 0)
    for m in range(n_dom):
        for i in range(planes):
            half, x = divmod(m * planes + i, half_planes)
            part = slice(half * TOGETHER, (half + 1) * TOGETHER)
            for y in range(rows):
                here = slice(y * TOGETHER, (y + 1) * TOGETHER)
                outs[m][plane_at[i], here, :] = even[x, y, part]


def filter_orbitals(place, diagonal, levels, blocks, starts, planes, rows):
    n_dom = len(blocks)
    first = diagonal is None
    lanes = blocks[0].shape[1]
    field = (n_dom * planes // 2, rows, SUBLANES, lanes)
    out = jax.ShapeDtypeStruct((planes, rows * TOGETHER, lanes), jnp.float32)
    extra = [jax.ShapeDtypeStruct(field, jnp.float32)] if first else []
    given = [] if first else [diagonal]
    size = n_dom * planes * rows * TOGETHER * lanes
    return pl.pallas_call(
        functools.partial(filter_kernel, n_dom, planes, rows, starts, first, len(levels)),
        out_shape=[out] * n_dom + extra,
        in_specs=[SMEM] + [VMEM] * (len(levels) + n_dom + len(given)),
        out_specs=[VMEM] * (n_dom + len(extra)),
        scratch_shapes=[pltpu.VMEM(field, jnp.float32)] * 2,
        compiler_params=params(8),
        cost_estimate=pl.CostEstimate(
            flops=12 * DEGREE * size, bytes_accessed=8 * size, transcendentals=0
        ),
        name="chebyshev",
    )(place, *levels, *given, *blocks)


def cell_first_kernel(n_band, place, *refs):
    pieces, parts = refs[:-n_band], refs[-n_band:]
    share = parts[0].shape[0]
    me = place[ME]
    together = SUBLANES // TOGETHER
    tiles = len(pieces) // together
    for p, part in enumerate(parts):
        base = pl.multiple_of((place[BAND] ^ p) * (share * TOGETHER), SUBLANES)
        for first in range(0, share, together):
            loaded = [piece[pl.ds(base + first * TOGETHER, SUBLANES), :] for piece in pieces]
            for k in range(together):
                here = slice(k * TOGETHER, (k + 1) * TOGETHER)
                for q in range(tiles):
                    tile = jnp.concatenate(
                        [loaded[q * together + i][here] for i in range(together)], axis=0
                    )
                    tile = jnp.where((me & 1) != 0, pltpu.roll(tile, TOGETHER, 0), tile)
                    if tiles == 1:
                        part[first + k] = tile
                    else:
                        row = pl.multiple_of((q ^ (me // together)) * SUBLANES, SUBLANES)
                        part[first + k, pl.ds(row, SUBLANES), :] = tile


def cell_first(place, n_band, pieces):
    rows, lanes = pieces[0].shape
    orbitals = len(pieces) * TOGETHER
    part = jax.ShapeDtypeStruct((rows // (TOGETHER * n_band), orbitals, lanes), jnp.float32)
    return pl.pallas_call(
        functools.partial(cell_first_kernel, n_band),
        out_shape=[part] * n_band,
        in_specs=[SMEM] + [VMEM] * len(pieces),
        out_specs=[VMEM] * n_band,
        compiler_params=params(8),
        name="cell_first",
    )(place, *pieces)


def orbital_first_kernel(n_dom, which, place, *refs):
    pieces, (out, laid_out, sems) = refs[: len(which)], refs[-3:]
    cells = out.shape[1]
    copies = []
    for k, (chunk, m) in enumerate(which):
        for t in range(TOGETHER):
            laid_out[k * TOGETHER + t] = pieces[k][pl.ds(t, cells, stride=TOGETHER), :]
        start = (chunk * n_dom + (place[ME] ^ m)) * TOGETHER
        copies.append(
            pltpu.make_async_copy(
                laid_out.at[pl.ds(k * TOGETHER, TOGETHER)],
                out.at[pl.ds(start, TOGETHER)],
                sems.at[k],
            )
        )
        copies[-1].start()
    for copy in copies:
        copy.wait()


def orbital_first(place, n_dom, orbitals, pieces, which, onto=None):
    rows, lanes = pieces[0].shape
    cells = rows // TOGETHER
    hbm = pl.BlockSpec(memory_space=pltpu.HBM)
    given = [] if onto is None else [onto]
    return pl.pallas_call(
        functools.partial(orbital_first_kernel, n_dom, which),
        out_shape=jax.ShapeDtypeStruct((orbitals, cells, lanes), jnp.float32),
        in_specs=[SMEM] + [VMEM] * len(pieces) + [hbm] * len(given),
        out_specs=hbm,
        input_output_aliases={len(pieces) + 1: 0} if given else {},
        scratch_shapes=[
            pltpu.VMEM((len(pieces) * TOGETHER, cells, lanes), jnp.float32),
            pltpu.SemaphoreType.DMA((len(pieces),)),
        ],
        compiler_params=params(8),
        name="orbital_first",
    )(place, *pieces, *given)


def projector_kernel(n_band, n_sub, place, offsets_ref, coefs_ref, high_out, low_out):
    atoms, shells, channels, spread = coefs_ref.shape
    own = atoms // (n_band * n_sub)
    lanes = spread
    cells = high_out.shape[1] // lanes
    pairs = own // 2
    row_index = lax.broadcasted_iota(jnp.int32, (cells, channels, spread), 0)
    row_index += place[BAND] * cells
    lane_index = lax.broadcasted_iota(jnp.int32, (lanes, spread), 0)

    def two_atoms(step, carry):
        shell = lax.rem(2 * (step // (n_band * pairs)), shells)
        seen = (step // pairs) % n_band
        seen = jnp.where(shell == 1, n_band - 1 - seen, seen)
        band = place[BAND] ^ seen
        first_atom = (place[SUB] * n_band + band) * own + 2 * (step % pairs)
        dense = []
        for i in range(2):
            offsets = offsets_ref[shell, pl.ds(first_atom + i, 1), :]
            coefs = coefs_ref[first_atom + i, shell]
            at_row = row_index == (offsets // lanes)[None]
            at_row &= (offsets >= 0)[None]
            left = [
                jnp.where(at_row, part.astype(jnp.float32)[None], 0.0)
                .reshape(cells * channels, spread)
                .astype(jnp.bfloat16)
                for part in split_bf16(coefs)
            ]
            at_lane = jnp.where(lane_index == (offsets & (lanes - 1)), 1.0, 0.0)
            at_lane = at_lane.astype(jnp.bfloat16)
            values = lax.dot_general(
                jnp.concatenate(left, axis=1),
                jnp.concatenate([at_lane, at_lane], axis=1),
                NT,
                preferred_element_type=jnp.float32,
            )
            dense.append(values.reshape(cells, channels, lanes))
        high, low = split_bf16(jnp.concatenate(dense, axis=1))
        rows = pl.ds(pl.multiple_of(step * 2 * channels, 2 * channels), 2 * channels)
        for cell in range(cells):
            high_out[rows, cell * lanes : (cell + 1) * lanes] = high[cell]
            low_out[rows, cell * lanes : (cell + 1) * lanes] = low[cell]
        return carry

    lax.fori_loop(0, shells * n_band * pairs, two_atoms, 0)


def build_projectors(n_band, n_sub, place, offsets, coefs, cells, lanes):
    atoms, shells, channels, spread = coefs.shape
    rows = atoms // n_sub * shells * channels
    shape = jax.ShapeDtypeStruct((rows, cells * lanes), jnp.bfloat16)
    return pl.pallas_call(
        functools.partial(projector_kernel, n_band, n_sub),
        out_shape=[shape, shape],
        in_specs=[SMEM, VMEM, VMEM],
        out_specs=[VMEM, VMEM],
        compiler_params=params(8),
        cost_estimate=pl.CostEstimate(
            flops=4 * rows * cells * lanes * spread,
            bytes_accessed=8 * rows * cells * lanes,
            transcendentals=0,
        ),
        name="projectors",
    )(place, offsets.swapaxes(0, 1), coefs)


def product_kernel(spots, n_sub, first_row, n_blocks, with_grid, place, w_high, w_low, *refs):
    refs, proj_out = refs[:-1], refs[-1]
    n_outs = n_blocks + (1 if with_grid else 0)
    arrays, outs = refs[:-n_outs], list(refs[-n_outs:])
    rows, orbitals = proj_out.shape
    cells, _, lanes = arrays[0].shape
    block = 12
    swap = (place[ME] & 2) != 0

    def parts(start):
        highs, lows = [], []
        for spot in spots:
            tiles = [
                arrays[at][pl.ds(start, block), first : first + width] for at, first, width in spot
            ]
            if len(tiles) == 2:
                near, far = tiles
                tiles = [jnp.where(swap, far, near), jnp.where(swap, near, far)]
            high, low = split_bf16(jnp.concatenate(tiles, axis=1))
            highs.append(jnp.concatenate([high[k] for k in range(block)], axis=1))
            lows.append(jnp.concatenate([low[k] for k in range(block)], axis=1))
        return jnp.concatenate(highs, axis=0), jnp.concatenate(lows, axis=0)

    def product(left_high, left_low, high, low):
        right = jnp.concatenate([high, low], axis=0)
        wide = lax.dot_general(left_high, right, NT, preferred_element_type=jnp.float32)
        narrow = lax.dot_general(left_low, high, NT, preferred_element_type=jnp.float32)
        return wide[:, :orbitals] + wide[:, orbitals:] + narrow

    if with_grid:
        grid_out = outs.pop(0)
        grid_out[...] = jnp.zeros_like(grid_out)

        def grid_block(step, carry):
            high, low = parts(place[SUB] * (cells // n_sub) + step * block)
            grid_out[...] += product(high, low, high, low)
            return carry

        lax.fori_loop(0, cells // (n_sub * block), grid_block, 0)

    def proj_block(step, carry):
        high, low = parts(step * block)
        depth = block * lanes
        here = pl.ds(pl.multiple_of(step * depth, depth), depth)
        some = slice(first_row, first_row + rows)
        proj_out[...] += product(w_high[some, here], w_low[some, here], high, low)
        return carry

    proj_out[...] = jnp.zeros_like(proj_out)
    lax.fori_loop(0, cells // block, proj_block, 0)
    for k, out in enumerate(outs):
        out[...] = proj_out[k * (rows // n_blocks) : (k + 1) * (rows // n_blocks), :]


def products(n_sub, first_row, rows, n_blocks, with_grid, place, projectors, arrays, spots):
    orbitals = sum(width for spot in spots for _, _, width in spot)
    grid = [jax.ShapeDtypeStruct((orbitals, orbitals), jnp.float32)] if with_grid else []
    block = jax.ShapeDtypeStruct((rows // n_blocks, orbitals), jnp.float32)
    flops = 12 * rows * orbitals * projectors[0].shape[1]
    return pl.pallas_call(
        functools.partial(product_kernel, spots, n_sub, first_row, n_blocks, with_grid),
        out_shape=grid + [block] * n_blocks,
        in_specs=[SMEM] + [VMEM] * (2 + len(arrays)),
        out_specs=[VMEM] * (len(grid) + n_blocks),
        scratch_shapes=[pltpu.VMEM((rows, orbitals), jnp.float32)],
        compiler_params=params(8),
        cost_estimate=pl.CostEstimate(
            flops=flops, bytes_accessed=4 * rows * projectors[0].shape[1], transcendentals=0
        ),
        name="products",
    )(place, *projectors, *arrays)


def reordered(x, width, by):
    span = width * by
    column = lax.broadcasted_iota(jnp.int32, x.shape, 1)
    up, down = pltpu.roll(x, span, 1), pltpu.roll(x, x.shape[1] - span, 1)
    return jnp.where((column & span) == 0, down, up)


def gram_kernel(scales, groups, seen, place, corr_ref, grid_ref, proj_ref, *refs):
    sums, outs = refs[: len(seen)], refs[len(seen) :]
    orbitals = grid_ref.shape[0]
    width = orbitals // groups
    bits = [1 << k for k in range(groups.bit_length() - 1)]
    projections = proj_ref[...]
    for part, by in zip(sums, seen):
        columns = part[...]
        for bit in bits:
            if by & bit:
                columns = reordered(columns, width, bit)
        projections += columns
    corr, rows = split_bf16(corr_ref[...]), split_bf16(projections)
    weighted = jnp.dot(
        jnp.concatenate([corr[0], corr[0], corr[1]], axis=1),
        jnp.concatenate([rows[0], rows[1], rows[0]], axis=0),
        preferred_element_type=jnp.float32,
    )
    parts = split_bf16(weighted)
    atom_part = lax.dot_general(
        jnp.concatenate([rows[0], rows[0], rows[1]], axis=0),
        jnp.concatenate([parts[0], parts[1], parts[0]], axis=0),
        TN,
        preferred_element_type=jnp.float32,
    )
    share = grid_ref[...] * scales[0] + atom_part * scales[1]
    for bit in bits:
        share = jnp.where((place[GROUP] & bit) != 0, reordered(share, width, bit), share)
    for k, out in enumerate(outs):
        out[...] = share[k * width : (k + 1) * width]


def gram_share(scales, groups, seen, place, corr, grid_part, proj, sums):
    rows = jax.ShapeDtypeStruct((grid_part.shape[0] // groups, grid_part.shape[1]), jnp.float32)
    return pl.pallas_call(
        functools.partial(gram_kernel, scales, groups, seen),
        out_shape=[rows] * groups,
        in_specs=[SMEM] + [VMEM] * (3 + len(sums)),
        out_specs=[VMEM] * groups,
        compiler_params=params(8),
        name="gram_share",
    )(place, corr, grid_part, proj, *sums)


def added(terms):
    while len(terms) > 1:
        terms = [a + b for a, b in zip(terms[::2], terms[1::2])]
    return terms[0]


def whole_columns(panel, potential, place, me, build):
    n_dom = lax.axis_size("dom")
    orbitals, planes, rows, lanes = panel.shape
    cells = planes * rows
    flat = panel.reshape(orbitals * cells, lanes)
    levels = potential.reshape(cells, lanes)
    size = TOGETHER * cells
    n_chunks = orbitals // (n_dom * TOGETHER)

    def block(c, m):
        return lax.dynamic_slice_in_dim(flat, (c * n_dom + (me ^ m)) * size, size, 0)

    def sent(x, m):
        return swapped(x, "dom", n_dom, m)

    own = []
    for m in range(n_dom):
        blocks = [block(c, m) for c in range(n_chunks)]
        if m < 3:
            blocks[0] = jnp.concatenate([blocks[0], levels], axis=0)
        own.append(blocks)
    near = jnp.concatenate(own[1], axis=0)
    if n_dom > 2:
        near, own[2][0] = lax.optimization_barrier((near, own[2][0]))
    near = sent(near, 1)
    arrived = [[own[0][0], near] + [sent(own[m][0], m) for m in range(2, n_dom)]]
    handed_on = [sent(arrived[0][2][size:], 1)] if n_dom > 3 else []
    for c in range(1, n_chunks):
        far = [own[m][c] for m in range(2, n_dom)]
        near, far = lax.optimization_barrier((near, far))
        arrived.append([own[0][c], near] + [sent(x, m) for m, x in enumerate(far, start=2)])
    diagonal = None
    done = []
    for c, blocks in enumerate(arrived):
        starts = [0] * n_dom
        starts[1] = c * size + (cells if c else 0)
        filtered = filter_orbitals(
            place, diagonal, [] if c else handed_on, blocks, starts, planes, rows
        )
        if diagonal is None:
            diagonal = filtered[n_dom]
        done.append(list(filtered[:n_dom]))
        if c == 0:
            done[0][0], place = lax.optimization_barrier((done[0][0], place))
            place, projectors = lax.optimization_barrier((place, build(place)))
    return [
        [(sent(x, m) if m else x).reshape(size, lanes) for m, x in enumerate(blocks)]
        for blocks in done
    ], projectors


def plane_by_plane(panel, potential):
    n_dom = lax.axis_size("dom")
    diagonal = (potential + (SHIFT - CENTER_LEVEL)) * (2.0 / HALF_WIDTH)

    def twice_operator(field):
        low, high = shifted(field[:, -1:], -1), shifted(field[:, :1], 1)
        extended = jnp.concatenate([low, field, high], axis=1)
        near = extended[:, 2:] + extended[:, :-2]
        near += jnp.roll(field, 1, axis=2) + jnp.roll(field, -1, axis=2)
        padded = jnp.pad(field, ((0, 0), (0, 0), (0, 0), (1, 1)))
        near += padded[..., 2:] + padded[..., :-2]
        return diagonal * field - near / HALF_WIDTH

    def one_step(_, carry):
        before, current = carry
        return current, twice_operator(current) - before

    start = (panel, 0.5 * twice_operator(panel))
    return lax.fori_loop(0, DEGREE - 1, one_step, start)[1]


def on_device(panel, potential, point_offsets, point_coefs, correlation):
    orbitals, planes, rows, lanes = panel.shape
    n_dom, n_band, n_sub = (lax.axis_size(axis) for axis in ("dom", "band", "sub"))
    groups = n_band * n_sub
    me, band, sub = (lax.axis_index(axis) for axis in ("dom", "band", "sub"))
    place = jnp.stack([me, band, sub, band * n_sub + sub]).astype(jnp.int32)

    cells = planes * rows
    share = cells // n_band
    channels = correlation.shape[1]
    own_atoms = point_offsets.shape[0] // groups
    own_corr = lax.dynamic_slice_in_dim(
        correlation, (sub * n_band + band) * own_atoms, own_atoms, 0
    )
    same_atom = jnp.eye(own_atoms, dtype=jnp.float32)
    corr_matrix = (same_atom[:, None, :, None] * own_corr[:, :, None, :]).reshape(
        own_atoms * channels, own_atoms * channels
    )

    place, corr_matrix = lax.optimization_barrier((place, corr_matrix))

    def build(place):
        return build_projectors(n_band, n_sub, place, point_offsets, point_coefs, share, lanes)

    if n_dom in (2, 4) and orbitals % (n_dom * TOGETHER) == 0 and planes * n_dom % 2 == 0:
        chunks, projectors = whole_columns(panel, potential, place, me, build)
        sooner = place
        which = [(c, m) for c in range(len(chunks)) for m in range(n_dom)]
        pieces = [chunks[c][m] for c, m in which]
        n_late = 2 if n_dom == 4 else 0
        first = len(pieces) - n_late
        filtered = orbital_first(place, n_dom, orbitals, pieces[:first], which[:first])
        early, place = lax.optimization_barrier((filtered, place))
        if n_late:
            filtered = orbital_first(
                place, n_dom, orbitals, pieces[first:], which[first:], early
            )
        parts = [cell_first(sooner, n_band, pieces) for pieces in chunks[:-1]]
        tiles = [[c] for c in range(len(chunks))]
        last = [chunks[-1]]
        if n_dom == 4:
            last = [chunks[-1][:2], chunks[-1][2:]]
            tiles[-1].append(len(chunks))
        if len(parts) and len(last) == 2:
            parts[-1], last[0] = lax.optimization_barrier((parts[-1], last[0]))
        parts.append(cell_first(place, n_band, last[0]))
        if len(last) == 2:
            near = parts[-1]
            crossed = [swapped(x, "band", n_band, m) if m else x for m, x in enumerate(near)]
            crossed, last[1] = lax.optimization_barrier((crossed, last[1]))
            parts.append(cell_first(place, n_band, last[1]))
            parts[-2] = crossed
    else:
        projectors = build(place)
        filtered = plane_by_plane(panel, potential)
        by_cell = filtered.reshape(orbitals, cells, lanes).swapaxes(0, 1)
        parts = [
            [
                lax.dynamic_slice_in_dim(by_cell, (band ^ m) * share, share, 0)
                for m in range(n_band)
            ]
        ]
        tiles = [[0]]
    filtered = filtered.reshape(panel.shape)
    own = [part[0] for part in parts]
    pieces = []
    for at, part in enumerate(parts):
        crossed = len(tiles[-1]) == 2 and at == len(parts) - 2
        for m in range(1, n_band):
            pieces.append(part[m] if crossed else swapped(part[m], "band", n_band, m))
    arrays = own + pieces
    pieces = [jnp.concatenate(own, axis=1)] + pieces
    arrays += [swapped(x, "sub", n_sub, k) for k in range(1, n_sub) for x in pieces]
    starts = [sum(x.shape[1] for x in own[:at]) for at in range(len(own))]
    spots = []
    for m in range(n_band):
        for k in range(n_sub):
            for tile in tiles:
                spot = []
                for at in tile:
                    index, first = at, 0
                    if m:
                        index = len(own) + at * (n_band - 1) + m - 1 + k * len(pieces)
                    elif k:
                        index = len(own) * n_band + (k - 1) * len(pieces)
                        first = starts[at]
                    spot.append((index, first, own[at].shape[1]))
                spots.append(spot)

    rows = own_atoms * channels
    n_sent = 3 * n_band - 1
    outgoing = products(
        n_sub, 0, n_sent * rows, n_sent, False, place, projectors, arrays, spots
    )
    outgoing, place = lax.optimization_barrier((outgoing, place))
    grid_part, own_proj = products(
        n_sub, n_sent * rows, rows, 1, True, place, projectors, arrays, spots
    )
    sums, seen = [], []
    to = [(by, m) for by in (1, -1) for m in range(n_band)]
    to += [(0, m) for m in range(n_band - 1, 0, -1)]
    for x, (by, m) in zip(outgoing, to):
        pairs = [
            (d * n_band + b, (d - by) % n_dom * n_band + (b ^ m))
            for d in range(n_dom)
            for b in range(n_band)
        ]
        seen.append(m * n_sub)
        sums.append(lax.ppermute(x, ("dom", "band"), pairs))
    scale_point = 1.0 / (cells * lanes * n_dom)
    scale_atom = 1.0 / math.sqrt(own_atoms * groups * n_dom)
    shares = gram_share(
        (scale_point, scale_atom), groups, seen, place, corr_matrix, grid_part, own_proj, sums
    )
    gram_rows = added(
        [swapped(x, ("band", "sub"), groups, m) if m else x for m, x in enumerate(shares)]
    )
    if n_dom <= 4:
        gram_rows = added(
            [swapped(gram_rows, "dom", n_dom, m) if m else gram_rows for m in range(n_dom)]
        )
    else:
        by = 1
        while by < n_dom:
            gram_rows += swapped(gram_rows, "dom", n_dom, by)
            by *= 2
    return filtered, gram_rows


def solution(mesh):
    placed = (
        P(("slab", "band", "sub"), "dom", None, None),
        P(("slab", "dom"), None, None),
        P(("slab", "dom"), None, None),
        P(("slab", "dom"), None, None, None),
        P(("slab", "dom"), None, None),
    )
    return jax.shard_map(
        on_device,
        mesh=mesh,
        in_specs=placed,
        out_specs=(P(("slab", "band", "sub"), "dom", None, None), P(("slab", "band", "sub"), None)),
        check_vma=False,
    )
```

```python
import functools
import math

import jax
import jax.numpy as jnp
from jax import lax
from jax.experimental import pallas as pl
from jax.experimental.pallas import tpu as pltpu
from jax.sharding import PartitionSpec as P

DEGREE = 12

CENTER_LEVEL = 3.6
HALF_WIDTH = 3.4
SHIFT = 3.0

TOGETHER = 4
SUBLANES = 8
ME, BAND, SUB, GROUP = range(4)
MIB = 1024 * 1024

VMEM = pl.BlockSpec(memory_space=pltpu.VMEM)
SMEM = pl.BlockSpec(memory_space=pltpu.SMEM)
NT = (((1,), (1,)), ((), ()))
TN = (((0,), (0,)), ((), ()))


def params(mib):
    return pltpu.CompilerParams(vmem_limit_bytes=mib * MIB)


def split_bf16(x):
    high = x.astype(jnp.bfloat16)
    return high, (x - high.astype(jnp.float32)).astype(jnp.bfloat16)


def shifted(x, by):
    size = lax.axis_size("dom")
    return lax.ppermute(x, "dom", [(i, (i - by) % size) for i in range(size)])


def swapped(x, axes, size, by):
    return lax.ppermute(x, axes, [(i, i ^ by) for i in range(size)])


def filter_kernel(n_dom, planes, rows, starts, first, n_levels, place, *refs):
    levels, refs = refs[:n_levels], list(refs[n_levels:])
    given = None if first else refs.pop(0)
    ins, outs = refs[:n_dom], refs[n_dom : 2 * n_dom]
    refs = refs[2 * n_dom :]
    diagonal = refs.pop(0) if first else given
    even, odd = refs
    half_planes = n_dom * planes // 2
    cells = planes * rows
    lanes = even.shape[3]
    scale = 1.0 / HALF_WIDTH
    mirrored = (place[ME] & 1) != 0
    plane_at = [jnp.where(mirrored, planes - 1 - i, i) for i in range(planes)]

    for x in range(half_planes):
        for half in range(2):
            m, i = divmod(half * half_planes + x, planes)
            part = slice(half * TOGETHER, (half + 1) * TOGETHER)
            base = starts[m] + plane_at[i] * rows
            for y in range(rows):
                even[x, y, part] = ins[m][pl.ds(base + y, TOGETHER, stride=cells), :]
                if first:
                    if m >= 3:
                        level = levels[m - 3][pl.ds(plane_at[i] * rows + y, 1), :]
                    else:
                        level = ins[m][pl.ds(base + (TOGETHER * cells + y), 1), :]
                    diagonal[x, y, part] = jnp.broadcast_to(
                        (level + (SHIFT - CENTER_LEVEL)) * (2.0 * scale), (TOGETHER, lanes)
                    )

    block = SUBLANES
    lane = lax.broadcasted_iota(jnp.int32, (block, SUBLANES, lanes), 2)
    at_start, at_end = lane == 0, lane == lanes - 1

    def twice_operator(source, x, y):
        here = slice(y, y + block)
        centre = source[x, here]
        if x == 0:
            near = pltpu.roll(source[half_planes - 1, here], TOGETHER, 1) + source[x + 1, here]
        elif x == half_planes - 1:
            near = pltpu.roll(source[0, here], TOGETHER, 1) + source[x - 1, here]
        else:
            near = source[x - 1, here] + source[x + 1, here]
        before = (y - 1) % rows
        after = (y + block) % rows
        near += jnp.concatenate([source[x, before : before + 1], centre[:-1]], axis=0)
        near += jnp.concatenate([centre[1:], source[x, after : after + 1]], axis=0)
        low = pltpu.roll(centre, 1, 2)
        high = pltpu.roll(centre, lanes - 1, 2)
        near += jnp.where(at_start, high, jnp.where(at_end, low, low + high))
        return diagonal[x, here] * centre - scale * near

    places = [(x, y) for x in range(half_planes) for y in range(0, rows, block)]

    def next_field(source, target):
        for x, y in places:
            target[x, y : y + block] = twice_operator(source, x, y) - target[x, y : y + block]

    for x, y in places:
        odd[x, y : y + block] = 0.5 * twice_operator(even, x, y)
    next_field(odd, even)

    def two_steps(_, carry):
        next_field(even, odd)
        next_field(odd, even)
        return carry

    lax.fori_loop(0, DEGREE // 2 - 1, two_steps, 0)
    for m in range(n_dom):
        for i in range(planes):
            half, x = divmod(m * planes + i, half_planes)
            part = slice(half * TOGETHER, (half + 1) * TOGETHER)
            for y in range(rows):
                here = slice(y * TOGETHER, (y + 1) * TOGETHER)
                outs[m][plane_at[i], here, :] = even[x, y, part]


def filter_orbitals(place, diagonal, levels, blocks, starts, planes, rows):
    n_dom = len(blocks)
    first = diagonal is None
    lanes = blocks[0].shape[1]
    field = (n_dom * planes // 2, rows, SUBLANES, lanes)
    out = jax.ShapeDtypeStruct((planes, rows * TOGETHER, lanes), jnp.float32)
    extra = [jax.ShapeDtypeStruct(field, jnp.float32)] if first else []
    given = [] if first else [diagonal]
    size = n_dom * planes * rows * TOGETHER * lanes
    return pl.pallas_call(
        functools.partial(filter_kernel, n_dom, planes, rows, starts, first, len(levels)),
        out_shape=[out] * n_dom + extra,
        in_specs=[SMEM] + [VMEM] * (len(levels) + n_dom + len(given)),
        out_specs=[VMEM] * (n_dom + len(extra)),
        scratch_shapes=[pltpu.VMEM(field, jnp.float32)] * 2,
        compiler_params=params(8),
        cost_estimate=pl.CostEstimate(
            flops=12 * DEGREE * size, bytes_accessed=8 * size, transcendentals=0
        ),
        name="chebyshev",
    )(place, *levels, *given, *blocks)


def cell_first_kernel(n_band, place, *refs):
    pieces, parts = refs[:-n_band], refs[-n_band:]
    share = parts[0].shape[0]
    me = place[ME]
    together = SUBLANES // TOGETHER
    tiles = len(pieces) // together
    for p, part in enumerate(parts):
        base = pl.multiple_of((place[BAND] ^ p) * (share * TOGETHER), SUBLANES)
        for first in range(0, share, together):
            loaded = [piece[pl.ds(base + first * TOGETHER, SUBLANES), :] for piece in pieces]
            for k in range(together):
                here = slice(k * TOGETHER, (k + 1) * TOGETHER)
                for q in range(tiles):
                    tile = jnp.concatenate(
                        [loaded[q * together + i][here] for i in range(together)], axis=0
                    )
                    tile = jnp.where((me & 1) != 0, pltpu.roll(tile, TOGETHER, 0), tile)
                    if tiles == 1:
                        part[first + k] = tile
                    else:
                        row = pl.multiple_of((q ^ (me // together)) * SUBLANES, SUBLANES)
                        part[first + k, pl.ds(row, SUBLANES), :] = tile


def cell_first(place, n_band, pieces):
    rows, lanes = pieces[0].shape
    orbitals = len(pieces) * TOGETHER
    part = jax.ShapeDtypeStruct((rows // (TOGETHER * n_band), orbitals, lanes), jnp.float32)
    return pl.pallas_call(
        functools.partial(cell_first_kernel, n_band),
        out_shape=[part] * n_band,
        in_specs=[SMEM] + [VMEM] * len(pieces),
        out_specs=[VMEM] * n_band,
        compiler_params=params(8),
        name="cell_first",
    )(place, *pieces)


def orbital_first_kernel(n_dom, which, place, *refs):
    pieces, (out, laid_out, sems) = refs[: len(which)], refs[-3:]
    cells = out.shape[1]
    copies = []
    for k, (chunk, m) in enumerate(which):
        for t in range(TOGETHER):
            laid_out[k * TOGETHER + t] = pieces[k][pl.ds(t, cells, stride=TOGETHER), :]
        start = (chunk * n_dom + (place[ME] ^ m)) * TOGETHER
        copies.append(
            pltpu.make_async_copy(
                laid_out.at[pl.ds(k * TOGETHER, TOGETHER)],
                out.at[pl.ds(start, TOGETHER)],
                sems.at[k],
            )
        )
        copies[-1].start()
    for copy in copies:
        copy.wait()


def orbital_first(place, n_dom, orbitals, pieces, which, onto=None):
    rows, lanes = pieces[0].shape
    cells = rows // TOGETHER
    hbm = pl.BlockSpec(memory_space=pltpu.HBM)
    given = [] if onto is None else [onto]
    return pl.pallas_call(
        functools.partial(orbital_first_kernel, n_dom, which),
        out_shape=jax.ShapeDtypeStruct((orbitals, cells, lanes), jnp.float32),
        in_specs=[SMEM] + [VMEM] * len(pieces) + [hbm] * len(given),
        out_specs=hbm,
        input_output_aliases={len(pieces) + 1: 0} if given else {},
        scratch_shapes=[
            pltpu.VMEM((len(pieces) * TOGETHER, cells, lanes), jnp.float32),
            pltpu.SemaphoreType.DMA((len(pieces),)),
        ],
        compiler_params=params(8),
        name="orbital_first",
    )(place, *pieces, *given)


def projector_kernel(n_band, n_sub, place, offsets_ref, coefs_ref, high_out, low_out):
    atoms, shells, channels, spread = coefs_ref.shape
    own = atoms // (n_band * n_sub)
    lanes = spread
    cells = high_out.shape[1] // lanes
    pairs = own // 2
    row_index = lax.broadcasted_iota(jnp.int32, (cells, channels, spread), 0)
    row_index += place[BAND] * cells
    lane_index = lax.broadcasted_iota(jnp.int32, (lanes, spread), 0)

    def two_atoms(step, carry):
        shell = lax.rem(2 * (step // (n_band * pairs)), shells)
        seen = (step // pairs) % n_band
        seen = jnp.where(shell == 1, n_band - 1 - seen, seen)
        band = place[BAND] ^ seen
        first_atom = (place[SUB] * n_band + band) * own + 2 * (step % pairs)
        dense = []
        for i in range(2):
            offsets = offsets_ref[shell, pl.ds(first_atom + i, 1), :]
            coefs = coefs_ref[first_atom + i, shell]
            at_row = row_index == (offsets // lanes)[None]
            at_row &= (offsets >= 0)[None]
            left = [
                jnp.where(at_row, part.astype(jnp.float32)[None], 0.0)
                .reshape(cells * channels, spread)
                .astype(jnp.bfloat16)
                for part in split_bf16(coefs)
            ]
            at_lane = jnp.where(lane_index == (offsets & (lanes - 1)), 1.0, 0.0)
            at_lane = at_lane.astype(jnp.bfloat16)
            values = lax.dot_general(
                jnp.concatenate(left, axis=1),
                jnp.concatenate([at_lane, at_lane], axis=1),
                NT,
                preferred_element_type=jnp.float32,
            )
            dense.append(values.reshape(cells, channels, lanes))
        high, low = split_bf16(jnp.concatenate(dense, axis=1))
        rows = pl.ds(pl.multiple_of(step * 2 * channels, 2 * channels), 2 * channels)
        for cell in range(cells):
            high_out[rows, cell * lanes : (cell + 1) * lanes] = high[cell]
            low_out[rows, cell * lanes : (cell + 1) * lanes] = low[cell]
        return carry

    lax.fori_loop(0, shells * n_band * pairs, two_atoms, 0)


def build_projectors(n_band, n_sub, place, offsets, coefs, cells, lanes):
    atoms, shells, channels, spread = coefs.shape
    rows = atoms // n_sub * shells * channels
    shape = jax.ShapeDtypeStruct((rows, cells * lanes), jnp.bfloat16)
    return pl.pallas_call(
        functools.partial(projector_kernel, n_band, n_sub),
        out_shape=[shape, shape],
        in_specs=[SMEM, VMEM, VMEM],
        out_specs=[VMEM, VMEM],
        compiler_params=params(8),
        cost_estimate=pl.CostEstimate(
            flops=4 * rows * cells * lanes * spread,
            bytes_accessed=8 * rows * cells * lanes,
            transcendentals=0,
        ),
        name="projectors",
    )(place, offsets.swapaxes(0, 1), coefs)


def product_kernel(spots, n_sub, first_row, n_blocks, with_grid, place, w_high, w_low, *refs):
    refs, proj_out = refs[:-1], refs[-1]
    n_outs = n_blocks + (1 if with_grid else 0)
    arrays, outs = refs[:-n_outs], list(refs[-n_outs:])
    rows, orbitals = proj_out.shape
    cells, _, lanes = arrays[0].shape
    block = 12
    swap = (place[ME] & 2) != 0

    def parts(start):
        highs, lows = [], []
        for spot in spots:
            tiles = [
                arrays[at][pl.ds(start, block), first : first + width] for at, first, width in spot
            ]
            if len(tiles) == 2:
                near, far = tiles
                tiles = [jnp.where(swap, far, near), jnp.where(swap, near, far)]
            high, low = split_bf16(jnp.concatenate(tiles, axis=1))
            highs.append(jnp.concatenate([high[k] for k in range(block)], axis=1))
            lows.append(jnp.concatenate([low[k] for k in range(block)], axis=1))
        return jnp.concatenate(highs, axis=0), jnp.concatenate(lows, axis=0)

    def product(left_high, left_low, high, low):
        right = jnp.concatenate([high, low], axis=0)
        wide = lax.dot_general(left_high, right, NT, preferred_element_type=jnp.float32)
        narrow = lax.dot_general(left_low, high, NT, preferred_element_type=jnp.float32)
        return wide[:, :orbitals] + wide[:, orbitals:] + narrow

    if with_grid:
        grid_out = outs.pop(0)
        grid_out[...] = jnp.zeros_like(grid_out)

        def grid_block(step, carry):
            high, low = parts(place[SUB] * (cells // n_sub) + step * block)
            grid_out[...] += product(high, low, high, low)
            return carry

        lax.fori_loop(0, cells // (n_sub * block), grid_block, 0)

    def proj_block(step, carry):
        high, low = parts(step * block)
        depth = block * lanes
        here = pl.ds(pl.multiple_of(step * depth, depth), depth)
        some = slice(first_row, first_row + rows)
        proj_out[...] += product(w_high[some, here], w_low[some, here], high, low)
        return carry

    proj_out[...] = jnp.zeros_like(proj_out)
    lax.fori_loop(0, cells // block, proj_block, 0)
    for k, out in enumerate(outs):
        out[...] = proj_out[k * (rows // n_blocks) : (k + 1) * (rows // n_blocks), :]


def products(n_sub, first_row, rows, n_blocks, with_grid, place, projectors, arrays, spots):
    orbitals = sum(width for spot in spots for _, _, width in spot)
    grid = [jax.ShapeDtypeStruct((orbitals, orbitals), jnp.float32)] if with_grid else []
    block = jax.ShapeDtypeStruct((rows // n_blocks, orbitals), jnp.float32)
    flops = 12 * rows * orbitals * projectors[0].shape[1]
    return pl.pallas_call(
        functools.partial(product_kernel, spots, n_sub, first_row, n_blocks, with_grid),
        out_shape=grid + [block] * n_blocks,
        in_specs=[SMEM] + [VMEM] * (2 + len(arrays)),
        out_specs=[VMEM] * (len(grid) + n_blocks),
        scratch_shapes=[pltpu.VMEM((rows, orbitals), jnp.float32)],
        compiler_params=params(8),
        cost_estimate=pl.CostEstimate(
            flops=flops, bytes_accessed=4 * rows * projectors[0].shape[1], transcendentals=0
        ),
        name="products",
    )(place, *projectors, *arrays)


def reordered(x, width, by):
    span = width * by
    column = lax.broadcasted_iota(jnp.int32, x.shape, 1)
    up, down = pltpu.roll(x, span, 1), pltpu.roll(x, x.shape[1] - span, 1)
    return jnp.where((column & span) == 0, down, up)


def gram_kernel(scales, groups, seen, place, corr_ref, grid_ref, proj_ref, *refs):
    sums, outs = refs[: len(seen)], refs[len(seen) :]
    orbitals = grid_ref.shape[0]
    width = orbitals // groups
    bits = [1 << k for k in range(groups.bit_length() - 1)]
    projections = proj_ref[...]
    for part, by in zip(sums, seen):
        columns = part[...]
        for bit in bits:
            if by & bit:
                columns = reordered(columns, width, bit)
        projections += columns
    highest = lax.Precision.HIGHEST
    weighted = jnp.dot(
        corr_ref[...], projections, precision=highest, preferred_element_type=jnp.float32
    )
    atom_part = lax.dot_general(
        projections, weighted, TN, precision=highest, preferred_element_type=jnp.float32
    )
    share = grid_ref[...] * scales[0] + atom_part * scales[1]
    for bit in bits:
        share = jnp.where((place[GROUP] & bit) != 0, reordered(share, width, bit), share)
    for k, out in enumerate(outs):
        out[...] = share[k * width : (k + 1) * width]


def gram_share(scales, groups, seen, place, corr, grid_part, proj, sums):
    rows = jax.ShapeDtypeStruct((grid_part.shape[0] // groups, grid_part.shape[1]), jnp.float32)
    return pl.pallas_call(
        functools.partial(gram_kernel, scales, groups, seen),
        out_shape=[rows] * groups,
        in_specs=[SMEM] + [VMEM] * (3 + len(sums)),
        out_specs=[VMEM] * groups,
        compiler_params=params(8),
        name="gram_share",
    )(place, corr, grid_part, proj, *sums)


def added(terms):
    while len(terms) > 1:
        terms = [a + b for a, b in zip(terms[::2], terms[1::2])]
    return terms[0]


def whole_columns(panel, potential, place, me, build):
    n_dom = lax.axis_size("dom")
    orbitals, planes, rows, lanes = panel.shape
    cells = planes * rows
    flat = panel.reshape(orbitals * cells, lanes)
    levels = potential.reshape(cells, lanes)
    size = TOGETHER * cells
    n_chunks = orbitals // (n_dom * TOGETHER)

    def block(c, m):
        return lax.dynamic_slice_in_dim(flat, (c * n_dom + (me ^ m)) * size, size, 0)

    def sent(x, m):
        return swapped(x, "dom", n_dom, m)

    own = []
    for m in range(n_dom):
        blocks = [block(c, m) for c in range(n_chunks)]
        if m < 3:
            blocks[0] = jnp.concatenate([blocks[0], levels], axis=0)
        own.append(blocks)
    near = sent(jnp.concatenate(own[1], axis=0), 1)
    arrived = [[own[0][0], near] + [sent(own[m][0], m) for m in range(2, n_dom)]]
    handed_on = [sent(arrived[0][2][size:], 1)] if n_dom > 3 else []
    for c in range(1, n_chunks):
        far = [own[m][c] for m in range(2, n_dom)]
        near, far = lax.optimization_barrier((near, far))
        arrived.append([own[0][c], near] + [sent(x, m) for m, x in enumerate(far, start=2)])
    diagonal = None
    done = []
    for c, blocks in enumerate(arrived):
        starts = [0] * n_dom
        starts[1] = c * size + (cells if c else 0)
        filtered = filter_orbitals(
            place, diagonal, [] if c else handed_on, blocks, starts, planes, rows
        )
        if diagonal is None:
            diagonal = filtered[n_dom]
        done.append(list(filtered[:n_dom]))
        if c == 0:
            done[0][0], place = lax.optimization_barrier((done[0][0], place))
            place, projectors = lax.optimization_barrier((place, build(place)))
    return [
        [(sent(x, m) if m else x).reshape(size, lanes) for m, x in enumerate(blocks)]
        for blocks in done
    ], projectors


def plane_by_plane(panel, potential):
    n_dom = lax.axis_size("dom")
    diagonal = (potential + (SHIFT - CENTER_LEVEL)) * (2.0 / HALF_WIDTH)

    def twice_operator(field):
        low, high = shifted(field[:, -1:], -1), shifted(field[:, :1], 1)
        extended = jnp.concatenate([low, field, high], axis=1)
        near = extended[:, 2:] + extended[:, :-2]
        near += jnp.roll(field, 1, axis=2) + jnp.roll(field, -1, axis=2)
        padded = jnp.pad(field, ((0, 0), (0, 0), (0, 0), (1, 1)))
        near += padded[..., 2:] + padded[..., :-2]
        return diagonal * field - near / HALF_WIDTH

    def one_step(_, carry):
        before, current = carry
        return current, twice_operator(current) - before

    start = (panel, 0.5 * twice_operator(panel))
    return lax.fori_loop(0, DEGREE - 1, one_step, start)[1]


def on_device(panel, potential, point_offsets, point_coefs, correlation):
    orbitals, planes, rows, lanes = panel.shape
    n_dom, n_band, n_sub = (lax.axis_size(axis) for axis in ("dom", "band", "sub"))
    groups = n_band * n_sub
    me, band, sub = (lax.axis_index(axis) for axis in ("dom", "band", "sub"))
    place = jnp.stack([me, band, sub, band * n_sub + sub]).astype(jnp.int32)

    cells = planes * rows
    share = cells // n_band
    channels = correlation.shape[1]
    own_atoms = point_offsets.shape[0] // groups
    own_corr = lax.dynamic_slice_in_dim(
        correlation, (sub * n_band + band) * own_atoms, own_atoms, 0
    )
    same_atom = jnp.eye(own_atoms, dtype=jnp.float32)
    corr_matrix = (same_atom[:, None, :, None] * own_corr[:, :, None, :]).reshape(
        own_atoms * channels, own_atoms * channels
    )

    place, corr_matrix = lax.optimization_barrier((place, corr_matrix))

    def build(place):
        return build_projectors(n_band, n_sub, place, point_offsets, point_coefs, share, lanes)

    if n_dom in (2, 4) and orbitals % (n_dom * TOGETHER) == 0 and planes * n_dom % 2 == 0:
        chunks, projectors = whole_columns(panel, potential, place, me, build)
        sooner = place
        which = [(c, m) for c in range(len(chunks)) for m in range(n_dom)]
        pieces = [chunks[c][m] for c, m in which]
        n_late = 2 if n_dom == 4 else 0
        first = len(pieces) - n_late
        filtered = orbital_first(place, n_dom, orbitals, pieces[:first], which[:first])
        early, place = lax.optimization_barrier((filtered, place))
        if n_late:
            filtered = orbital_first(
                place, n_dom, orbitals, pieces[first:], which[first:], early
            )
        parts = [cell_first(sooner, n_band, pieces) for pieces in chunks[:-1]]
        tiles = [[c] for c in range(len(chunks))]
        last = [chunks[-1]]
        if n_dom == 4:
            last = [chunks[-1][:2], chunks[-1][2:]]
            tiles[-1].append(len(chunks))
        if len(parts) and len(last) == 2:
            parts[-1], last[0] = lax.optimization_barrier((parts[-1], last[0]))
        parts.append(cell_first(place, n_band, last[0]))
        if len(last) == 2:
            near = parts[-1]
            crossed = [swapped(x, "band", n_band, m) if m else x for m, x in enumerate(near)]
            crossed, last[1] = lax.optimization_barrier((crossed, last[1]))
            parts.append(cell_first(place, n_band, last[1]))
            parts[-2] = crossed
    else:
        projectors = build(place)
        filtered = plane_by_plane(panel, potential)
        by_cell = filtered.reshape(orbitals, cells, lanes).swapaxes(0, 1)
        parts = [
            [
                lax.dynamic_slice_in_dim(by_cell, (band ^ m) * share, share, 0)
                for m in range(n_band)
            ]
        ]
        tiles = [[0]]
    filtered = filtered.reshape(panel.shape)
    own = [part[0] for part in parts]
    pieces = []
    for at, part in enumerate(parts):
        crossed = len(tiles[-1]) == 2 and at == len(parts) - 2
        for m in range(1, n_band):
            pieces.append(part[m] if crossed else swapped(part[m], "band", n_band, m))
    pieces[-1], filtered = lax.optimization_barrier((pieces[-1], filtered))
    arrays = own + pieces
    pieces = [jnp.concatenate(own, axis=1)] + pieces
    arrays += [swapped(x, "sub", n_sub, k) for k in range(1, n_sub) for x in pieces]
    starts = [sum(x.shape[1] for x in own[:at]) for at in range(len(own))]
    spots = []
    for m in range(n_band):
        for k in range(n_sub):
            for tile in tiles:
                spot = []
                for at in tile:
                    index, first = at, 0
                    if m:
                        index = len(own) + at * (n_band - 1) + m - 1 + k * len(pieces)
                    elif k:
                        index = len(own) * n_band + (k - 1) * len(pieces)
                        first = starts[at]
                    spot.append((index, first, own[at].shape[1]))
                spots.append(spot)

    rows = own_atoms * channels
    n_sent = 3 * n_band - 1
    outgoing = products(
        n_sub, 0, n_sent * rows, n_sent, False, place, projectors, arrays, spots
    )
    outgoing, place = lax.optimization_barrier((outgoing, place))
    grid_part, own_proj = products(
        n_sub, n_sent * rows, rows, 1, True, place, projectors, arrays, spots
    )
    sums, seen = [], []
    to = [(by, m) for by in (1, -1) for m in range(n_band)]
    to += [(0, m) for m in range(n_band - 1, 0, -1)]
    for x, (by, m) in zip(outgoing, to):
        pairs = [
            (d * n_band + b, (d - by) % n_dom * n_band + (b ^ m))
            for d in range(n_dom)
            for b in range(n_band)
        ]
        seen.append(m * n_sub)
        sums.append(lax.ppermute(x, ("dom", "band"), pairs))
    scale_point = 1.0 / (cells * lanes * n_dom)
    scale_atom = 1.0 / math.sqrt(own_atoms * groups * n_dom)
    shares = gram_share(
        (scale_point, scale_atom), groups, seen, place, corr_matrix, grid_part, own_proj, sums
    )
    gram_rows = added(
        [swapped(x, ("band", "sub"), groups, m) if m else x for m, x in enumerate(shares)]
    )
    if n_dom <= 4:
        gram_rows = added(
            [swapped(gram_rows, "dom", n_dom, m) if m else gram_rows for m in range(n_dom)]
        )
    else:
        by = 1
        while by < n_dom:
            gram_rows += swapped(gram_rows, "dom", n_dom, by)
            by *= 2
    return filtered, gram_rows


def solution(mesh):
    placed = (
        P(("slab", "band", "sub"), "dom", None, None),
        P(("slab", "dom"), None, None),
        P(("slab", "dom"), None, None),
        P(("slab", "dom"), None, None, None),
        P(("slab", "dom"), None, None),
    )
    return jax.shard_map(
        on_device,
        mesh=mesh,
        in_specs=placed,
        out_specs=(P(("slab", "band", "sub"), "dom", None, None), P(("slab", "band", "sub"), None)),
        check_vma=False,
    )
```
